512 devices in a mesh: fsdp: 8 (over x, core), ctx: 64 (over z, y).
Axes of the slice: x: 4, y: 4, z: 16, core: 2. Of those that a mesh axis runs over, the one named last changes fastest.
Arguments:
- tokens: bfloat16 [8, 8192, 4096], P('fsdp', 'ctx'), may hold values from -64 to 64
- doc_start: int32 [8, 8192], P('fsdp', 'ctx'), may hold values from 0 to 8191, as said below
- out_grad: bfloat16 [8, 8192, 1024], P('fsdp', 'ctx'), may hold values from -6 to 6
- w_qkv: bfloat16 [4096, 1280], P(('fsdp', 'ctx')), may hold values from -1 to 1
Outputs:
- grad_tokens: bfloat16 [8, 8192, 4096], P('fsdp', 'ctx')
The draws below stay inside these ranges and needn't reach their ends.
Inputs may be any that keep to these rules, and one draw needn't show every extreme that they name: Documents are runs of consecutive tokens of 1 to 385 tokens; doc_start gives each token the position in its sequence of its document's first token, and every sequence holds a document of exactly 385 tokens.
All inputs are finite; a program needn't handle non-finite values.
Results may differ from the reference program's by a relative error of at most 0.04.
Values may be sent and summed in bfloat16 or wider, within the bound.
No kernel may reach another device: no remote copies, remote signals or barrier semaphores. Data moves between devices by JAX's collectives and lax.ppermute only.
A program may use at most 64 MiB of HBM per device.

```python
import math
import jax
import jax.numpy as jnp
from jax import lax

D = 4096
HQ = 8
HD = 128
REACH = 4
TOK_DEV = 128
BATCH = 8
SEQ = 8192
QKV = 1280
DOC_MAX = 385
N_CTX = 64


def draw_tokens(key, part):
    key_base = jax.random.fold_in(jax.random.fold_in(key, 11), 0)
    values = 2.0 * jax.random.normal(key_base, (BATCH, SEQ, D), jnp.float32)
    return jnp.clip(values, -64.0, 64.0).astype(jnp.bfloat16)


def draw_w_qkv(key, part):
    key_first = jax.random.fold_in(jax.random.fold_in(key, 23), 0)
    spread = D ** (-0.5)
    matrix = jax.random.normal(key_first, (D, QKV), jnp.float32) * spread
    return matrix.astype(jnp.bfloat16)


def draw_doc_start(key, part):
    row_keys = jax.random.split(jax.random.fold_in(key, 37), BATCH)

    def draw_row(row_key):
        key_len, key_pos = jax.random.split(row_key)
        doc_lengths = jax.random.randint(key_len, (SEQ,), 1, DOC_MAX + 1, dtype=jnp.int32)
        longest = jax.random.randint(key_pos, (), 0, 2, dtype=jnp.int32)
        doc_lengths = jnp.where(jnp.arange(SEQ, dtype=jnp.int32) == longest, DOC_MAX, doc_lengths).astype(jnp.int32)
        doc_ends = jnp.cumsum(doc_lengths).astype(jnp.int32)
        doc_begin = doc_ends - doc_lengths
        owner = jnp.searchsorted(doc_ends, jnp.arange(SEQ, dtype=jnp.int32), side='right')
        return doc_begin[owner].astype(jnp.int32)
    return jax.vmap(draw_row)(row_keys)


def block_levels(key, shape, pieces, low, high):
    def one(axis_at, parts):
        draws = jax.random.uniform(jax.random.fold_in(jax.random.fold_in(key, 6), axis_at), (parts,), jnp.float32, low / len(pieces), high / len(pieces))
        return jnp.repeat(jnp.exp(draws), shape[axis_at] // parts).reshape((-1,) + (1,) * (len(shape) - axis_at - 1))

    loudness = one(*pieces[0])
    for cut in pieces[1:]:
        loudness = loudness * one(*cut)
    return loudness


def normal_values(key, dims, deviation, reach, shards=(), kind=jnp.bfloat16):
    values = deviation * jax.random.normal(key, dims, jnp.float32)
    if shards:
        values = values * block_levels(key, dims, shards, -0.22, 0.18)
    return jnp.clip(values, -reach, reach).astype(kind)


def setup_inputs(seed: int = 0) -> dict:
    key_list = jax.random.split(jax.random.key(seed), 5)
    tokens = draw_tokens(jax.random.fold_in(key_list[4], 71), 0)
    doc_start = draw_doc_start(jax.random.fold_in(key_list[4], 71), 0)
    out_grad = normal_values(key_list[2], (BATCH, SEQ, HQ * HD), 1.0, 6.0, ((0, 8), (1, 64)))
    w_qkv = draw_w_qkv(jax.random.fold_in(key_list[4], 71), 0)
    return dict(tokens=tokens, doc_start=doc_start, out_grad=out_grad, w_qkv=w_qkv)


ROPE_BASE = 500000.0
MASKED = -1e+30

def angles_for(positions, head_size):
    half_size = head_size // 2
    inverse = jnp.power(jnp.float32(ROPE_BASE), -jnp.arange(half_size, dtype=jnp.float32) / half_size)
    phase_angle = positions.astype(jnp.float32)[:, None] * inverse[None, :]
    return (jnp.cos(phase_angle), jnp.sin(phase_angle))

def rotate(vectors, cos_part, sin_part):
    half_size = vectors.shape[-1] // 2
    first_half = vectors[..., :half_size]
    second_half = vectors[..., half_size:]
    return jnp.concatenate([first_half * cos_part - second_half * sin_part, second_half * cos_part + first_half * sin_part], axis=-1)

def unrotate(vectors, cos_part, sin_part):
    half_size = vectors.shape[-1] // 2
    first_half = vectors[..., :half_size]
    second_half = vectors[..., half_size:]
    return jnp.concatenate([first_half * cos_part + second_half * sin_part, second_half * cos_part - first_half * sin_part], axis=-1)

def reference(tokens, doc_start, out_grad, w_qkv):
    score_scale = 1.0 / math.sqrt(HD)
    key_span = REACH * TOK_DEV
    lead_rows = (REACH - 1) * TOK_DEV

    def one_sequence(inputs):
        features, starts, grad_out = inputs
        projected = jnp.dot(features, w_qkv, preferred_element_type=jnp.float32)
        positions = jnp.arange(SEQ, dtype=jnp.int32) - starts
        cos_part, sin_part = angles_for(positions, HD)
        queries = rotate(projected[:, :HQ * HD].reshape(SEQ, HQ, HD), cos_part[:, None, :], sin_part[:, None, :]).astype(jnp.bfloat16)
        keys_all = rotate(projected[:, HQ * HD:HQ * HD + HD], cos_part, sin_part).astype(jnp.bfloat16)
        values_all = projected[:, HQ * HD + HD:].astype(jnp.bfloat16)
        queries = lax.optimization_barrier(queries)
        pair_rows = lax.optimization_barrier(jnp.concatenate([keys_all, values_all], axis=1))
        padded = jnp.concatenate([jnp.zeros((lead_rows, 2 * HD), jnp.bfloat16), pair_rows], axis=0)
        grad_rows = grad_out.reshape(SEQ, HQ, HD)

        def block_step(current, block_id):
            start_row = block_id * TOK_DEV
            query_block = lax.dynamic_slice_in_dim(queries, start_row, TOK_DEV, 0).astype(jnp.float32)
            grad_block = lax.dynamic_slice_in_dim(grad_rows, start_row, TOK_DEV, 0).astype(jnp.float32)
            begin_block = lax.dynamic_slice_in_dim(starts, start_row, TOK_DEV, 0)
            window = lax.dynamic_slice_in_dim(padded, start_row, key_span, 0)
            key_win = window[:, :HD].astype(jnp.float32)
            value_win = window[:, HD:].astype(jnp.float32)
            query_index = start_row + jnp.arange(TOK_DEV, dtype=jnp.int32)
            key_index = start_row - lead_rows + jnp.arange(key_span, dtype=jnp.int32)
            allowed = (key_index[None, :] <= query_index[:, None]) & (key_index[None, :] >= begin_block[:, None])
            scores = jnp.einsum('qhd,kd->hqk', query_block, key_win) * score_scale
            scores = jnp.where(allowed[None], scores, MASKED)
            row_top = lax.optimization_barrier(jnp.max(scores, axis=-1, keepdims=True))
            row_total = lax.optimization_barrier(jnp.sum(jnp.where(allowed[None], jnp.exp(scores - row_top), 0.0), axis=-1, keepdims=True))
            log_total = row_top + jnp.log(row_total)
            probs = jnp.where(allowed[None], jnp.exp(scores - log_total), 0.0)
            attn_out = lax.optimization_barrier(jnp.einsum('hqk,kd->qhd', probs, value_win).astype(jnp.bfloat16))
            row_delta = lax.optimization_barrier(jnp.sum(grad_block * attn_out.astype(jnp.float32), axis=-1))
            probs_low = lax.optimization_barrier(probs.astype(jnp.bfloat16))
            grad_value = jnp.einsum('hqk,qhd->kd', probs_low.astype(jnp.float32), grad_block)
            grad_probs = jnp.einsum('qhd,kd->hqk', grad_block, value_win)
            grad_scores = lax.optimization_barrier((probs * (grad_probs - row_delta.T[:, :, None])).astype(jnp.bfloat16))
            grad_scores = grad_scores.astype(jnp.float32)
            grad_query = jnp.einsum('hqk,kd->qhd', grad_scores, key_win) * score_scale
            grad_key = jnp.einsum('hqk,qhd->kd', grad_scores, query_block) * score_scale
            window_grad = jnp.concatenate([grad_key, grad_value], axis=1)
            earlier = lax.dynamic_slice_in_dim(current, start_row, key_span, 0)
            current = lax.dynamic_update_slice_in_dim(current, earlier + window_grad, start_row, 0)
            return (current, grad_query)
        start_grad = jnp.zeros((SEQ + lead_rows, 2 * HD), jnp.float32)
        block_ids = jnp.arange(N_CTX, dtype=jnp.int32)
        pair_grad, grad_queries = lax.scan(block_step, start_grad, block_ids)
        pair_grad = pair_grad[lead_rows:]
        grad_queries = grad_queries.reshape(SEQ, HQ, HD)
        grad_q_pre = unrotate(grad_queries, cos_part[:, None, :], sin_part[:, None, :]).reshape(SEQ, HQ * HD)
        grad_k_pre = unrotate(pair_grad[:, :HD], cos_part, sin_part)
        all_grads = jnp.concatenate([grad_q_pre.astype(jnp.bfloat16), grad_k_pre.astype(jnp.bfloat16), pair_grad[:, HD:].astype(jnp.bfloat16)], axis=1)
        return jnp.dot(all_grads, w_qkv.T, preferred_element_type=jnp.float32).astype(jnp.bfloat16)
    return lax.map(one_sequence, (tokens, doc_start, out_grad))
```

```python
import math

import jax
import jax.numpy as jnp
from jax import lax
from jax.sharding import PartitionSpec as P

HQ = 8
HD = 128
REACH = 4
ROPE_BASE = 500000.0
MASKED = -1e30
NX, NC, NZ, NY = 4, 2, 16, 4
ALL = ("fsdp", "ctx")


def place(x, c, z, y):
    return (x * NC + c) * (NZ * NY) + z * NY + y


def route(move):
    return [
        (place(x, c, z, y), place(*move(x, c, z, y)))
        for x in range(NX)
        for c in range(NC)
        for z in range(NZ)
        for y in range(NY)
    ]


def hop(block, distance, x_core):
    def move(x, c, z, y):
        if c == x_core:
            return (x + distance) % NX, c, z, y
        return x, c, z, (y + distance) % NY

    return lax.ppermute(block, ALL, route(move))


def swap_cores(block):
    return lax.ppermute(block, ALL, route(lambda x, c, z, y: (x, 1 - c, z, y)))


def shifted(block, axis, distance):
    devices = range(lax.axis_size(axis))
    return lax.ppermute(block, axis, [(i - distance, i) for i in devices if i - distance in devices])


def angles_for(positions, head_size):
    half_size = head_size // 2
    inverse = jnp.power(
        jnp.float32(ROPE_BASE), -jnp.arange(half_size, dtype=jnp.float32) / half_size
    )
    phase_angle = positions.astype(jnp.float32)[:, None] * inverse[None, :]
    return (jnp.cos(phase_angle), jnp.sin(phase_angle))


def rotate(vectors, cos_part, sin_part):
    half_size = vectors.shape[-1] // 2
    a = vectors[..., :half_size]
    b = vectors[..., half_size:]
    return jnp.concatenate([a * cos_part - b * sin_part, b * cos_part + a * sin_part], axis=-1)


def local(tokens, doc_start, out_grad, w_qkv):
    row_count = tokens.shape[1]
    score_scale = 1.0 / math.sqrt(HD)
    features = tokens[0]
    begin_rows = doc_start[0]
    grad_rows = out_grad[0].reshape(row_count, HQ, HD)
    fsdp, ctx = lax.axis_index("fsdp"), lax.axis_index("ctx")
    x_me, core = fsdp // NC, fsdp % NC
    y_me = ctx % NY

    column = lax.all_gather(
        w_qkv, "ctx", axis=0, tiled=True,
        axis_index_groups=[[z * NY + y for z in range(NZ)] for y in range(NY)],
    )
    second, first, third = (hop(column, d, 0) for d in (2, 1, 3))
    plane = jnp.concatenate([column, first, second, third], axis=0)

    def spread(part):
        two, one, three = (hop(part, d, 1) for d in (2, 1, 3))
        mine = [part, one, two, three]
        return mine + [swap_cores(piece) for piece in mine]

    pair_w = spread(plane[:, HQ * HD :])
    query_w = spread(plane[:, : HQ * HD])

    block = NZ * NY * 8
    slot = lax.broadcasted_iota(jnp.int32, (block, block), 1)
    source = lax.broadcasted_iota(jnp.int32, (block, block), 0)
    wanted = slot // 8 % NZ * (NY * 8) + (y_me - slot // (NZ * 8) + NY) % NY * 8 + slot % 8
    order = (source == wanted).astype(jnp.bfloat16)

    def taken(shift, c):
        at = ((x_me - shift + NX) % NX * NC + c) * block
        return jnp.dot(
            lax.dynamic_slice_in_dim(features, at, block, 1), order,
            preferred_element_type=jnp.float32,
        ).astype(jnp.bfloat16)

    by_x = [taken(s, 0) for s in range(NX)]
    span = NZ * 8
    order0 = [
        jnp.concatenate([by_x[d][:, e * span : (e + 1) * span] for d in range(NX)], axis=1)
        for e in range(NY)
    ]
    order1 = [taken(e, 1) for e in range(NX)]
    own = [jnp.where(core == 0, a, b) for a, b in zip(order0, order1)]
    other = [jnp.where(core == 0, b, a) for a, b in zip(order0, order1)]
    features_in = own + other

    def project(weights):
        total = 0.0
        for part, w in zip(features_in, weights):
            total = total + jnp.dot(part, w, preferred_element_type=jnp.float32)
        return total

    first_row = ctx * row_count
    query_index = first_row + jnp.arange(row_count, dtype=jnp.int32)
    cos_part, sin_part = angles_for(query_index - begin_rows, HD)
    pair_pre = project(pair_w)
    pair_rows = jnp.concatenate(
        [rotate(pair_pre[:, :HD], cos_part, sin_part), pair_pre[:, HD:]], axis=1
    ).astype(jnp.bfloat16)
    near = jnp.concatenate([shifted(pair_rows, "ctx", 1), pair_rows], axis=0)
    window = jnp.concatenate([shifted(near, "ctx", 2), near], axis=0)

    queries = rotate(
        project(query_w).reshape(row_count, HQ, HD), cos_part[:, None, :], sin_part[:, None, :]
    ).astype(jnp.bfloat16)
    keys, values = window[:, :HD], window[:, HD:]
    key_index = first_row - (REACH - 1) * row_count + jnp.arange(REACH * row_count, dtype=jnp.int32)
    allowed = (key_index[None, :] <= query_index[:, None]) & (
        key_index[None, :] >= begin_rows[:, None]
    )
    scores = (
        jnp.einsum("qhd,kd->hqk", queries, keys, preferred_element_type=jnp.float32) * score_scale
    )
    scores = jnp.where(allowed[None], scores, MASKED)
    top = jnp.max(scores, axis=-1, keepdims=True)
    unnormed = jnp.where(allowed[None], jnp.exp(scores - top), 0.0)
    probs = unnormed / jnp.sum(unnormed, axis=-1, keepdims=True)
    probs_low = probs.astype(jnp.bfloat16)
    grad_probs = jnp.einsum("qhd,kd->hqk", grad_rows, values, preferred_element_type=jnp.float32)
    attn_out = jnp.einsum(
        "hqk,kd->hqd", probs_low, values, preferred_element_type=jnp.float32
    ).astype(jnp.bfloat16)
    row_delta = jnp.sum(
        jnp.transpose(grad_rows, (1, 0, 2)).astype(jnp.float32) * attn_out.astype(jnp.float32),
        axis=-1, keepdims=True,
    )
    grad_value = jnp.einsum("hqk,qhd->kd", probs_low, grad_rows, preferred_element_type=jnp.float32)
    grad_scores = (probs * (grad_probs - row_delta)).astype(jnp.bfloat16)
    grad_query = (
        jnp.einsum("hqk,kd->qhd", grad_scores, keys, preferred_element_type=jnp.float32)
        * score_scale
    )
    grad_key = (
        jnp.einsum("hqk,qhd->kd", grad_scores, queries, preferred_element_type=jnp.float32)
        * score_scale
    )
    pair_grad = jnp.concatenate([grad_key, grad_value], axis=1)
    far, near = pair_grad[: 2 * row_count], pair_grad[2 * row_count :]
    near = near + shifted(far, "ctx", -2)
    pair_total = near[row_count:] + shifted(near[:row_count], "ctx", -1)

    query_out = rotate(grad_query, cos_part[:, None, :], -sin_part[:, None, :]).reshape(
        row_count, HQ * HD
    ).astype(jnp.bfloat16)
    pair_out = jnp.concatenate(
        [rotate(pair_total[:, :HD], cos_part, -sin_part), pair_total[:, HD:]], axis=1
    ).astype(jnp.bfloat16)

    turn = (((1,), (1,)), ((), ()))
    arrived = [
        (
            lax.dot_general(query_out, wq, turn, preferred_element_type=jnp.float32)
            + lax.dot_general(pair_out, wp, turn, preferred_element_type=jnp.float32)
        ).astype(jnp.bfloat16)
        for wq, wp in zip(query_w, pair_w)
    ]
    own, other = arrived[:NX], arrived[NX:]
    order0 = [jnp.where(core == 0, a, b) for a, b in zip(own, other)]
    order1 = [jnp.where(core == 0, b, a) for a, b in zip(own, other)]
    by_x = [
        jnp.concatenate([order0[e][:, d * span : (d + 1) * span] for e in range(NY)], axis=1)
        for d in range(NX)
    ]
    result = jnp.zeros(features.shape, jnp.bfloat16)
    for s in range(NX):
        for c, part in ((0, by_x[s]), (1, order1[s])):
            at = ((x_me - s + NX) % NX * NC + c) * block
            back = lax.dot_general(part, order, turn, preferred_element_type=jnp.float32)
            result = lax.dynamic_update_slice_in_dim(result, back.astype(jnp.bfloat16), at, 1)
    return result[None]


def solution(mesh):
    placed = (
        P("fsdp", "ctx", None),
        P("fsdp", "ctx"),
        P("fsdp", "ctx", None),
        P(("fsdp", "ctx"), None),
    )
    return jax.shard_map(
        local, mesh=mesh, in_specs=placed, out_specs=P("fsdp", "ctx", None), check_vma=False
    )
```

```python
import math

import jax
import jax.numpy as jnp
from jax import lax
from jax.experimental import pallas as pl
from jax.experimental.pallas import tpu as pltpu
from jax.sharding import PartitionSpec as P

HQ = 8
HD = 128
REACH = 4
ROPE_BASE = 500000.0
MASKED = -1e30
NX, NC, NZ, NY = 4, 2, 16, 4
ALL = ("fsdp", "ctx")


def place(x, c, z, y):
    return (x * NC + c) * (NZ * NY) + z * NY + y


def route(move):
    return [
        (place(x, c, z, y), place(*move(x, c, z, y)))
        for x in range(NX)
        for c in range(NC)
        for z in range(NZ)
        for y in range(NY)
    ]


def hop(block, distance, x_core):
    def move(x, c, z, y):
        if c == x_core:
            return (x + distance) % NX, c, z, y
        return x, c, z, (y + distance) % NY

    return lax.ppermute(block, ALL, route(move))


def swap_cores(block):
    return lax.ppermute(block, ALL, route(lambda x, c, z, y: (x, 1 - c, z, y)))


BLOCK = NZ * NY * 8
SPAN = NZ * 8
TURN = (((1,), (1,)), ((), ()))
VMEM_LIMIT = 48 * 1024 * 1024


def order_matrix(y_me):
    slot = lax.broadcasted_iota(jnp.int32, (BLOCK, BLOCK), 1)
    source = lax.broadcasted_iota(jnp.int32, (BLOCK, BLOCK), 0)
    step, inner = slot // SPAN, slot % SPAN
    wanted = inner // 8 * (NY * 8) + (y_me - step + NY) % NY * 8 + inner % 8
    return (source == wanted).astype(jnp.bfloat16)


def block_at(x_me, s, c):
    return pl.multiple_of(((x_me - s + NX) % NX * NC + c) * BLOCK, BLOCK)


def arrange_body(at, features, theirs, out_ref):
    x_me, y_me, core = at[0], at[1], at[2]
    order = order_matrix(y_me)
    for s in range(NX):
        own = features[:, pl.ds(block_at(x_me, s, core), BLOCK)]
        other = theirs[:, pl.ds(pl.multiple_of((x_me - s + NX) % NX * BLOCK, BLOCK), BLOCK)]
        both = jnp.concatenate([own, other], axis=0)
        rows = both.shape[0]
        got = jnp.dot(both, order, preferred_element_type=jnp.float32).astype(jnp.bfloat16)

        @pl.when(core == 1)
        def _():
            out_ref[pl.ds(s * rows, rows), :] = got

        @pl.when(core == 0)
        def _():
            for e in range(NY):
                out_ref[pl.ds(e * rows, rows), pl.ds(s * SPAN, SPAN)] = got[
                    :, e * SPAN : (e + 1) * SPAN
                ]


def arrange(at, features, theirs):
    return pl.pallas_call(
        arrange_body,
        in_specs=[pl.BlockSpec(memory_space=pltpu.SMEM)]
        + [pl.BlockSpec(memory_space=pltpu.VMEM)] * 2,
        out_shape=jax.ShapeDtypeStruct((NX * 2 * features.shape[0], BLOCK), jnp.bfloat16),
        compiler_params=pltpu.CompilerParams(vmem_limit_bytes=VMEM_LIMIT),
        cost_estimate=pl.CostEstimate(
            flops=4 * 2 * 256 * BLOCK * BLOCK, bytes_accessed=4 << 20, transcendentals=0
        ),
    )(at, features, theirs)


def stack_body(own, first, second, third, query_ref, pair_ref):
    rows = own.shape[0]
    for i, piece in enumerate((own, first, second, third)):
        at = pl.ds(i * rows, rows)
        query_ref[at, :] = piece[:, : HQ * HD]
        pair_ref[at, :] = piece[:, HQ * HD :]


def stack_planes(*pieces):
    rows = sum(piece.shape[0] for piece in pieces)
    return pl.pallas_call(
        stack_body,
        out_shape=[
            pltpu.VMEM((rows, HQ * HD), jnp.bfloat16),
            pltpu.VMEM((rows, 2 * HD), jnp.bfloat16),
        ],
    )(*[pltpu.with_memory_space_constraint(p, pltpu.VMEM) for p in pieces])


def query_part_body(at, grads, *refs):
    pieces, out_ref, held = refs[:8], refs[8], refs[9]
    x_me, y_me, core = at[0], at[1], at[2]
    order = order_matrix(y_me)
    for i, piece in enumerate(pieces):
        held[i] = lax.dot_general(
            grads[...], piece[...], TURN, preferred_element_type=jnp.float32
        )
    rows = grads.shape[0]
    by_x, by_y = core * NX, (1 - core) * NX
    for s in range(NX):
        even = jnp.concatenate(
            [held[by_x + e, :, s * SPAN : (s + 1) * SPAN] for e in range(NY)], axis=1
        )
        for c, part in ((0, even), (1, held[by_y + s])):
            high = part.astype(jnp.bfloat16)
            low = (part - high.astype(jnp.float32)).astype(jnp.bfloat16)
            back = lax.dot_general(
                jnp.concatenate([high, low], axis=0), order, TURN,
                preferred_element_type=jnp.float32,
            )
            out_ref[:, pl.ds(block_at(x_me, s, c), BLOCK)] = back[:rows] + back[rows:]


def query_part_of(at, grads, pieces):
    rows = grads.shape[0]
    return pl.pallas_call(
        query_part_body,
        in_specs=[pl.BlockSpec(memory_space=pltpu.SMEM)]
        + [pl.BlockSpec(memory_space=pltpu.VMEM)] * 9,
        out_shape=jax.ShapeDtypeStruct((rows, 8 * BLOCK), jnp.float32),
        scratch_shapes=[pltpu.VMEM((8, rows, BLOCK), jnp.float32)],
        compiler_params=pltpu.CompilerParams(vmem_limit_bytes=VMEM_LIMIT),
        cost_estimate=pl.CostEstimate(
            flops=8 * 2 * rows * BLOCK * (HQ * HD + 2 * BLOCK),
            bytes_accessed=12 << 20,
            transcendentals=0,
        ),
    )(at, grads, *pieces)


def shifted(block, axis, distance):
    devices = range(lax.axis_size(axis))
    return lax.ppermute(block, axis, [(i - distance, i) for i in devices if i - distance in devices])


def angles_for(positions, head_size):
    half_size = head_size // 2
    inverse = jnp.power(
        jnp.float32(ROPE_BASE), -jnp.arange(half_size, dtype=jnp.float32) / half_size
    )
    phase_angle = positions.astype(jnp.float32)[:, None] * inverse[None, :]
    return (jnp.cos(phase_angle), jnp.sin(phase_angle))


def rotate(vectors, cos_part, sin_part):
    half_size = vectors.shape[-1] // 2
    a = vectors[..., :half_size]
    b = vectors[..., half_size:]
    return jnp.concatenate([a * cos_part - b * sin_part, b * cos_part + a * sin_part], axis=-1)


def local(tokens, doc_start, out_grad, w_qkv):
    row_count = tokens.shape[1]
    score_scale = 1.0 / math.sqrt(HD)
    features = tokens[0]
    begin_rows = doc_start[0]
    grad_rows = out_grad[0].reshape(row_count, HQ, HD)
    fsdp, ctx = lax.axis_index("fsdp"), lax.axis_index("ctx")
    x_me, core = fsdp // NC, fsdp % NC
    y_me = ctx % NY

    column = lax.all_gather(
        w_qkv, "ctx", axis=0, tiled=True,
        axis_index_groups=[[z * NY + y for z in range(NZ)] for y in range(NY)],
    )
    second, first, third = (hop(column, d, 0) for d in (2, 1, 3))

    at = jnp.stack([x_me, y_me, core]).astype(jnp.int32)
    blocks = [features[:, i * BLOCK : (i + 1) * BLOCK] for i in range(NX * NC)]
    halves = [jnp.concatenate(blocks[c::NC], axis=1) for c in range(NC)]
    theirs = swap_cores(jnp.where(core == 0, halves[1], halves[0]))
    arranged = arrange(at, features, theirs)

    def project(pieces):
        total = 0.0
        rows = 2 * row_count
        for e, piece in enumerate(pieces):
            total = total + jnp.dot(
                arranged[e * rows : (e + 1) * rows], piece, preferred_element_type=jnp.float32
            )
        return total[:row_count] + swap_cores(total[row_count:])

    plane_q, plane_p = stack_planes(column, first, second, third)
    two, one, three = (hop(plane_p, d, 1) for d in (2, 1, 3))
    two_q, one_q, three_q = (hop(plane_q, d, 1) for d in (2, 1, 3))
    pair_pre = project([plane_p, one, two, three])

    first_row = ctx * row_count
    query_index = first_row + jnp.arange(row_count, dtype=jnp.int32)
    cos_part, sin_part = angles_for(query_index - begin_rows, HD)
    pair_rows = jnp.concatenate(
        [rotate(pair_pre[:, :HD], cos_part, sin_part), pair_pre[:, HD:]], axis=1
    ).astype(jnp.bfloat16)
    near = jnp.concatenate([shifted(pair_rows, "ctx", 1), pair_rows], axis=0)
    near, one_q, two_q, three_q = lax.optimization_barrier((near, one_q, two_q, three_q))
    query_pre = project([plane_q, one_q, two_q, three_q])
    far, query_pre = lax.optimization_barrier((shifted(near, "ctx", 2), query_pre))
    window = jnp.concatenate([far, near], axis=0)
    pair_own = jnp.concatenate([plane_p, one, two, three], axis=0)
    pair_other = swap_cores(pair_own)
    plane_q_other = swap_cores(plane_q)

    queries = rotate(
        query_pre.reshape(row_count, HQ, HD), cos_part[:, None, :], sin_part[:, None, :]
    ).astype(jnp.bfloat16)
    keys, values = window[:, :HD], window[:, HD:]
    key_index = first_row - (REACH - 1) * row_count + jnp.arange(REACH * row_count, dtype=jnp.int32)
    allowed = (key_index[None, :] <= query_index[:, None]) & (
        key_index[None, :] >= begin_rows[:, None]
    )
    scores = (
        jnp.einsum("qhd,kd->hqk", queries, keys, preferred_element_type=jnp.float32) * score_scale
    )
    scores = jnp.where(allowed[None], scores, MASKED)
    top = jnp.max(scores, axis=-1, keepdims=True)
    unnormed = jnp.where(allowed[None], jnp.exp(scores - top), 0.0)
    probs = unnormed / jnp.sum(unnormed, axis=-1, keepdims=True)
    probs_low = probs.astype(jnp.bfloat16)
    grad_probs = jnp.einsum("qhd,kd->hqk", grad_rows, values, preferred_element_type=jnp.float32)
    attn_out = jnp.einsum(
        "hqk,kd->hqd", probs_low, values, preferred_element_type=jnp.float32
    ).astype(jnp.bfloat16)
    row_delta = jnp.sum(
        jnp.transpose(grad_rows, (1, 0, 2)).astype(jnp.float32) * attn_out.astype(jnp.float32),
        axis=-1, keepdims=True,
    )
    grad_value = jnp.einsum("hqk,qhd->kd", probs_low, grad_rows, preferred_element_type=jnp.float32)
    grad_scores = (probs * (grad_probs - row_delta)).astype(jnp.bfloat16)
    grad_query = (
        jnp.einsum("hqk,kd->qhd", grad_scores, keys, preferred_element_type=jnp.float32)
        * score_scale
    )
    grad_key = (
        jnp.einsum("hqk,qhd->kd", grad_scores, queries, preferred_element_type=jnp.float32)
        * score_scale
    )
    pair_grad = jnp.concatenate([grad_key, grad_value], axis=1)
    query_out = rotate(grad_query, cos_part[:, None, :], -sin_part[:, None, :]).reshape(
        row_count, HQ * HD
    ).astype(jnp.bfloat16)
    far, near = pair_grad[: 2 * row_count], pair_grad[2 * row_count :]
    one_q, two_q, three_q, query_out = lax.optimization_barrier((one_q, two_q, three_q, query_out))
    swapped = [swap_cores(piece) for piece in (one_q, two_q, three_q)]
    near = near + shifted(far, "ctx", -2)
    query_part = query_part_of(
        at, query_out, [plane_q, one_q, two_q, three_q, plane_q_other] + swapped
    )

    pair_w = [
        w[i * BLOCK : (i + 1) * BLOCK] for w in (pair_own, pair_other) for i in range(NX)
    ]
    order = order_matrix(y_me)
    order0 = [jnp.where(core == 0, a, b) for a, b in zip(pair_w[:NX], pair_w[NX:])]
    order1 = [jnp.where(core == 0, b, a) for a, b in zip(pair_w[:NX], pair_w[NX:])]
    pair_all = jnp.zeros((features.shape[1], 2 * HD), jnp.bfloat16)
    for s in range(NX):
        even = jnp.concatenate([order0[e][s * SPAN : (s + 1) * SPAN] for e in range(NY)], axis=0)
        for c, part in ((0, even), (1, order1[s])):
            back = jnp.dot(order, part, preferred_element_type=jnp.float32).astype(jnp.bfloat16)
            place_at = ((x_me - s + NX) % NX * NC + c) * BLOCK
            pair_all = lax.dynamic_update_slice_in_dim(pair_all, back, place_at, 0)

    came, query_part, pair_all = lax.optimization_barrier(
        (shifted(near[:row_count], "ctx", -1), query_part, pair_all)
    )
    pair_total = near[row_count:] + came
    pair_out = jnp.concatenate(
        [rotate(pair_total[:, :HD], cos_part, -sin_part), pair_total[:, HD:]], axis=1
    ).astype(jnp.bfloat16)
    result = query_part + lax.dot_general(
        pair_out, pair_all, TURN, preferred_element_type=jnp.float32
    )
    return result.astype(jnp.bfloat16)[None]


def solution(mesh):
    placed = (
        P("fsdp", "ctx", None),
        P("fsdp", "ctx"),
        P("fsdp", "ctx", None),
        P(("fsdp", "ctx"), None),
    )
    return jax.shard_map(
        local, mesh=mesh, in_specs=placed, out_specs=P("fsdp", "ctx", None), check_vma=False
    )
```

```python
import math

import jax
import jax.numpy as jnp
from jax import lax
from jax.experimental import pallas as pl
from jax.experimental.pallas import tpu as pltpu
from jax.sharding import PartitionSpec as P

HQ = 8
HD = 128
REACH = 4
ROPE_BASE = 500000.0
MASKED = -1e30
NX, NC, NZ, NY = 4, 2, 16, 4
ALL = ("fsdp", "ctx")


def place(x, c, z, y):
    return (x * NC + c) * (NZ * NY) + z * NY + y


def route(move):
    return [
        (place(x, c, z, y), place(*move(x, c, z, y)))
        for x in range(NX)
        for c in range(NC)
        for z in range(NZ)
        for y in range(NY)
    ]


def hop(block, distance, x_core):
    def move(x, c, z, y):
        if c == x_core:
            return (x + distance) % NX, c, z, y
        return x, c, z, (y + distance) % NY

    return lax.ppermute(block, ALL, route(move))


def swap_cores(block):
    return lax.ppermute(block, ALL, route(lambda x, c, z, y: (x, 1 - c, z, y)))


BLOCK = NZ * NY * 8
SPAN = NZ * 8
TURN = (((1,), (1,)), ((), ()))
VMEM_LIMIT = 48 * 1024 * 1024


def order_matrix(y_me):
    slot = lax.broadcasted_iota(jnp.int32, (BLOCK, BLOCK), 1)
    source = lax.broadcasted_iota(jnp.int32, (BLOCK, BLOCK), 0)
    step, inner = slot // SPAN, slot % SPAN
    wanted = inner // 8 * (NY * 8) + (y_me - step + NY) % NY * 8 + inner % 8
    return (source == wanted).astype(jnp.bfloat16)


def block_at(x_me, s, c):
    return pl.multiple_of(((x_me - s + NX) % NX * NC + c) * BLOCK, BLOCK)


def arrange_body(at, features, theirs, out_ref):
    x_me, y_me, core = at[0], at[1], at[2]
    order = order_matrix(y_me)
    for s in range(NX):
        own = features[:, pl.ds(block_at(x_me, s, core), BLOCK)]
        other = theirs[:, pl.ds(pl.multiple_of((x_me - s + NX) % NX * BLOCK, BLOCK), BLOCK)]
        both = jnp.concatenate([own, other], axis=0)
        rows = both.shape[0]
        got = jnp.dot(both, order, preferred_element_type=jnp.float32).astype(jnp.bfloat16)

        @pl.when(core == 1)
        def _():
            out_ref[pl.ds(s * rows, rows), :] = got

        @pl.when(core == 0)
        def _():
            for e in range(NY):
                out_ref[pl.ds(e * rows, rows), pl.ds(s * SPAN, SPAN)] = got[
                    :, e * SPAN : (e + 1) * SPAN
                ]


def arrange(at, features, theirs):
    return pl.pallas_call(
        arrange_body,
        in_specs=[pl.BlockSpec(memory_space=pltpu.SMEM)]
        + [pl.BlockSpec(memory_space=pltpu.VMEM)] * 2,
        out_shape=jax.ShapeDtypeStruct((NX * 2 * features.shape[0], BLOCK), jnp.bfloat16),
        compiler_params=pltpu.CompilerParams(vmem_limit_bytes=VMEM_LIMIT),
        cost_estimate=pl.CostEstimate(
            flops=4 * 2 * 256 * BLOCK * BLOCK, bytes_accessed=4 << 20, transcendentals=0
        ),
    )(at, features, theirs)


def stack_body(at, features, own, first, second, third, plane_ref, theirs_ref):
    rows = own.shape[0]
    for i, piece in enumerate((own, first, second, third)):
        plane_ref[pl.ds(i * rows, rows), :] = piece[...]
    for x in range(NX):
        from_block = pl.ds(pl.multiple_of((x * NC + 1 - at[2]) * BLOCK, BLOCK), BLOCK)
        theirs_ref[:, x * BLOCK : (x + 1) * BLOCK] = features[:, from_block]


def stack_plane(at, features, pieces):
    rows = sum(piece.shape[0] for piece in pieces)
    return pl.pallas_call(
        stack_body,
        in_specs=[pl.BlockSpec(memory_space=pltpu.SMEM)]
        + [pl.BlockSpec(memory_space=pltpu.VMEM)] * 5,
        out_shape=[
            pltpu.VMEM((rows, pieces[0].shape[1]), jnp.bfloat16),
            pltpu.VMEM((features.shape[0], NX * BLOCK), jnp.bfloat16),
        ],
        compiler_params=pltpu.CompilerParams(vmem_limit_bytes=VMEM_LIMIT),
    )(at, in_vmem(features), *[in_vmem(p) for p in pieces])


def in_vmem(array):
    return pltpu.with_memory_space_constraint(array, pltpu.VMEM)


def project_body(arranged, *refs):
    pieces, mine_ref, theirs_ref, rows_ref = refs[:4], refs[4], refs[5], refs[6]
    held, in_sems, out_sems = refs[7:]
    count = arranged.shape[0] // NX
    loads = [
        pltpu.make_async_copy(piece, held.at[e], in_sems.at[e]) for e, piece in enumerate(pieces)
    ]
    for load in loads:
        load.start()
    stores = []
    for e in range(NX):
        loads[e].wait()
        store = pltpu.make_async_copy(
            held.at[e], rows_ref.at[pl.ds(e * BLOCK, BLOCK)], out_sems.at[e]
        )
        store.start()
        stores.append(store)
        part = jnp.dot(
            arranged[e * count : (e + 1) * count, :], held[e], preferred_element_type=jnp.float32
        )
        for ref, half in ((mine_ref, part[: count // 2]), (theirs_ref, part[count // 2 :])):
            ref[...] = half if e == 0 else ref[...] + half
    for store in stores:
        store.wait()


def project(arranged, pieces):
    count, columns = arranged.shape[0] // NX // 2, pieces[0].shape[1]
    whole = pl.BlockSpec(memory_space=pltpu.VMEM)
    left = pl.BlockSpec(memory_space=pl.ANY)
    return pl.pallas_call(
        project_body,
        in_specs=[whole] + [left] * 4,
        out_specs=[whole, whole, left],
        out_shape=[
            jax.ShapeDtypeStruct((count, columns), jnp.float32),
            jax.ShapeDtypeStruct((count, columns), jnp.float32),
            jax.ShapeDtypeStruct((NX * BLOCK, columns), jnp.bfloat16),
        ],
        scratch_shapes=[
            pltpu.VMEM((NX, BLOCK, columns), jnp.bfloat16),
            pltpu.SemaphoreType.DMA((NX,)),
            pltpu.SemaphoreType.DMA((NX,)),
        ],
        compiler_params=pltpu.CompilerParams(vmem_limit_bytes=VMEM_LIMIT),
        cost_estimate=pl.CostEstimate(
            flops=NX * 4 * count * BLOCK * columns, bytes_accessed=12 << 20, transcendentals=0
        ),
    )(arranged, *pieces)


def query_part_body(at, grads, own, other, out_ref, pair_ref, weights, held, sems):
    x_me, y_me, core = at[0], at[1], at[2]
    loads = []
    for i in range(2 * NX):
        source = (own, other)[i // NX].at[pl.ds(i % NX * BLOCK, BLOCK)]
        loads.append(pltpu.make_async_copy(source, weights.at[i], sems.at[i]))
        loads[-1].start()
    order = order_matrix(y_me)
    queries = HQ * HD
    for i in range(2 * NX):
        loads[i].wait()
        held[i] = lax.dot_general(
            grads[...], weights[i, :, :queries], TURN, preferred_element_type=jnp.float32
        )
    rows = grads.shape[0]
    by_x, by_y = core * NX, (1 - core) * NX
    for s in range(NX):
        even = jnp.concatenate(
            [held[by_x + e, :, s * SPAN : (s + 1) * SPAN] for e in range(NY)], axis=1
        )
        for c, part in ((0, even), (1, held[by_y + s])):
            high = part.astype(jnp.bfloat16)
            low = (part - high.astype(jnp.float32)).astype(jnp.bfloat16)
            back = lax.dot_general(
                jnp.concatenate([high, low], axis=0), order, TURN,
                preferred_element_type=jnp.float32,
            )
            out_ref[:, pl.ds(block_at(x_me, s, c), BLOCK)] = back[:rows] + back[rows:]
    for s in range(NX):
        even = jnp.concatenate(
            [weights[by_x + e, s * SPAN : (s + 1) * SPAN, queries:] for e in range(NY)], axis=0
        )
        for c, part in ((0, even), (1, weights[by_y + s, :, queries:])):
            pair_ref[pl.ds(block_at(x_me, s, c), BLOCK), :] = jnp.dot(
                order, part, preferred_element_type=jnp.float32
            ).astype(jnp.bfloat16)


def query_part_of(at, grads, own, other):
    rows, columns = grads.shape[0], own.shape[1]
    whole = pl.BlockSpec(memory_space=pltpu.VMEM)
    left = pl.BlockSpec(memory_space=pl.ANY)
    return pl.pallas_call(
        query_part_body,
        in_specs=[pl.BlockSpec(memory_space=pltpu.SMEM), whole, left, left],
        out_shape=[
            pltpu.VMEM((rows, 8 * BLOCK), jnp.float32),
            pltpu.VMEM((8 * BLOCK, columns - HQ * HD), jnp.bfloat16),
        ],
        scratch_shapes=[
            pltpu.VMEM((8, BLOCK, columns), jnp.bfloat16),
            pltpu.VMEM((8, rows, BLOCK), jnp.float32),
            pltpu.SemaphoreType.DMA((8,)),
        ],
        compiler_params=pltpu.CompilerParams(vmem_limit_bytes=VMEM_LIMIT),
        cost_estimate=pl.CostEstimate(
            flops=8 * 2 * rows * BLOCK * (HQ * HD + 4 * BLOCK),
            bytes_accessed=12 << 20,
            transcendentals=0,
        ),
    )(at, grads, own, other)


def shifted(block, axis, distance):
    devices = range(lax.axis_size(axis))
    return lax.ppermute(block, axis, [(i - distance, i) for i in devices if i - distance in devices])


def angles_for(positions, head_size):
    half_size = head_size // 2
    inverse = jnp.power(
        jnp.float32(ROPE_BASE), -jnp.arange(half_size, dtype=jnp.float32) / half_size
    )
    phase_angle = positions.astype(jnp.float32)[:, None] * inverse[None, :]
    return (jnp.cos(phase_angle), jnp.sin(phase_angle))


def rotate(vectors, cos_part, sin_part):
    half_size = vectors.shape[-1] // 2
    a = vectors[..., :half_size]
    b = vectors[..., half_size:]
    return jnp.concatenate([a * cos_part - b * sin_part, b * cos_part + a * sin_part], axis=-1)


def local(tokens, doc_start, out_grad, w_qkv):
    row_count = tokens.shape[1]
    score_scale = 1.0 / math.sqrt(HD)
    features = tokens[0]
    begin_rows = doc_start[0]
    grad_rows = out_grad[0].reshape(row_count, HQ, HD)
    fsdp, ctx = lax.axis_index("fsdp"), lax.axis_index("ctx")
    x_me, core = fsdp // NC, fsdp % NC
    y_me = ctx % NY

    column = lax.all_gather(
        w_qkv, "ctx", axis=0, tiled=True,
        axis_index_groups=[[z * NY + y for z in range(NZ)] for y in range(NY)],
    )
    second, first, third = (hop(column, d, 0) for d in (2, 1, 3))

    at = jnp.stack([x_me, y_me, core]).astype(jnp.int32)
    plane, theirs = stack_plane(at, features, [column, first, second, third])
    two, one, three = (hop(plane, d, 1) for d in (2, 1, 3))
    arranged = arrange(at, features, swap_cores(theirs))
    mine, theirs, own_w = project(arranged, [plane, one, two, three])
    projected, own_w = lax.optimization_barrier((mine + swap_cores(theirs), own_w))
    other_w = swap_cores(own_w)
    pair_pre, query_pre = projected[:, HQ * HD :], projected[:, : HQ * HD]

    first_row = ctx * row_count
    query_index = first_row + jnp.arange(row_count, dtype=jnp.int32)
    cos_part, sin_part = angles_for(query_index - begin_rows, HD)
    pair_rows = jnp.concatenate(
        [rotate(pair_pre[:, :HD], cos_part, sin_part), pair_pre[:, HD:]], axis=1
    ).astype(jnp.bfloat16)
    near = jnp.concatenate([shifted(pair_rows, "ctx", 1), pair_rows], axis=0)
    window = jnp.concatenate([shifted(near, "ctx", 2), near], axis=0)
    queries = rotate(
        query_pre.reshape(row_count, HQ, HD), cos_part[:, None, :], sin_part[:, None, :]
    ).astype(jnp.bfloat16)
    keys, values = window[:, :HD], window[:, HD:]
    key_index = first_row - (REACH - 1) * row_count + jnp.arange(REACH * row_count, dtype=jnp.int32)
    allowed = (key_index[None, :] <= query_index[:, None]) & (
        key_index[None, :] >= begin_rows[:, None]
    )
    scores = (
        jnp.einsum("qhd,kd->hqk", queries, keys, preferred_element_type=jnp.float32) * score_scale
    )
    scores = jnp.where(allowed[None], scores, MASKED)
    top = jnp.max(scores, axis=-1, keepdims=True)
    unnormed = jnp.where(allowed[None], jnp.exp(scores - top), 0.0)
    probs = unnormed / jnp.sum(unnormed, axis=-1, keepdims=True)
    probs_low = probs.astype(jnp.bfloat16)
    grad_probs = jnp.einsum("qhd,kd->hqk", grad_rows, values, preferred_element_type=jnp.float32)
    attn_out = jnp.einsum(
        "hqk,kd->hqd", probs_low, values, preferred_element_type=jnp.float32
    ).astype(jnp.bfloat16)
    row_delta = jnp.sum(
        jnp.transpose(grad_rows, (1, 0, 2)).astype(jnp.float32) * attn_out.astype(jnp.float32),
        axis=-1, keepdims=True,
    )
    grad_value = jnp.einsum("hqk,qhd->kd", probs_low, grad_rows, preferred_element_type=jnp.float32)
    grad_scores = (probs * (grad_probs - row_delta)).astype(jnp.bfloat16)
    grad_query = (
        jnp.einsum("hqk,kd->qhd", grad_scores, keys, preferred_element_type=jnp.float32)
        * score_scale
    )
    grad_key = (
        jnp.einsum("hqk,qhd->kd", grad_scores, queries, preferred_element_type=jnp.float32)
        * score_scale
    )
    pair_grad = jnp.concatenate([grad_key, grad_value], axis=1)
    query_out = rotate(grad_query, cos_part[:, None, :], -sin_part[:, None, :]).reshape(
        row_count, HQ * HD
    ).astype(jnp.bfloat16)
    far, near = pair_grad[: 2 * row_count], pair_grad[2 * row_count :]
    query_part, pair_all = query_part_of(at, query_out, own_w, other_w)
    came, query_part, pair_all = lax.optimization_barrier(
        (shifted(far, "ctx", -2), query_part, pair_all)
    )
    near = near + came
    pair_total = near[row_count:] + shifted(near[:row_count], "ctx", -1)
    pair_out = jnp.concatenate(
        [rotate(pair_total[:, :HD], cos_part, -sin_part), pair_total[:, HD:]], axis=1
    ).astype(jnp.bfloat16)
    result = query_part + lax.dot_general(
        pair_out, pair_all, TURN, preferred_element_type=jnp.float32
    )
    return result.astype(jnp.bfloat16)[None]


def solution(mesh):
    placed = (
        P("fsdp", "ctx", None),
        P("fsdp", "ctx"),
        P("fsdp", "ctx", None),
        P(("fsdp", "ctx"), None),
    )
    return jax.shard_map(
        local, mesh=mesh, in_specs=placed, out_specs=P("fsdp", "ctx", None), check_vma=False
    )
```

```python
import functools
import math

import jax
import jax.numpy as jnp
from jax import lax
from jax.experimental import pallas as pl
from jax.experimental.pallas import tpu as pltpu
from jax.sharding import PartitionSpec as P

HQ = 8
HD = 128
REACH = 4
ROPE_BASE = 500000.0
MASKED = -1e30
NX, NC, NZ, NY = 4, 2, 16, 4
ALL = ("fsdp", "ctx")


def place(x, c, z, y):
    return (x * NC + c) * (NZ * NY) + z * NY + y


def route(move):
    return [
        (place(x, c, z, y), place(*move(x, c, z, y)))
        for x in range(NX)
        for c in range(NC)
        for z in range(NZ)
        for y in range(NY)
    ]


def hop(block, distance, x_core):
    def move(x, c, z, y):
        if c == x_core:
            return (x + distance) % NX, c, z, y
        return x, c, z, (y + distance) % NY

    return lax.ppermute(block, ALL, route(move))


def swap_cores(block):
    return lax.ppermute(block, ALL, route(lambda x, c, z, y: (x, 1 - c, z, y)))


BLOCK = NZ * NY * 8
SPAN = NZ * 8
TURN = (((1,), (1,)), ((), ()))
VMEM_LIMIT = 48 * 1024 * 1024


def order_matrix(y_me):
    slot = lax.broadcasted_iota(jnp.int32, (BLOCK, BLOCK), 1)
    source = lax.broadcasted_iota(jnp.int32, (BLOCK, BLOCK), 0)
    step, inner = slot // SPAN, slot % SPAN
    place_z = inner // 8
    z = place_z // 8 + place_z // 4 % 2 * 2 + place_z // 2 % 2 * 4 + place_z % 2 * 8
    wanted = z * (NY * 8) + (y_me - step + NY) % NY * 8 + inner % 8
    return (source == wanted).astype(jnp.bfloat16)


def block_at(x_me, s, c):
    return pl.multiple_of(((x_me - s + NX) % NX * NC + c) * BLOCK, BLOCK)


def arrange_body(at, features, theirs, out_ref):
    x_me, y_me, core = at[0], at[1], at[2]
    order = order_matrix(y_me)
    for s in range(NX):
        own = features[:, pl.ds(block_at(x_me, s, core), BLOCK)]
        other = theirs[:, pl.ds(pl.multiple_of((x_me - s + NX) % NX * BLOCK, BLOCK), BLOCK)]
        both = jnp.concatenate([own, other], axis=0)
        rows = both.shape[0]
        got = jnp.dot(both, order, preferred_element_type=jnp.float32).astype(jnp.bfloat16)

        @pl.when(core == 1)
        def _():
            out_ref[pl.ds(s * rows, rows), :] = got

        @pl.when(core == 0)
        def _():
            for e in range(NY):
                out_ref[pl.ds(e * rows, rows), pl.ds(s * SPAN, SPAN)] = got[
                    :, e * SPAN : (e + 1) * SPAN
                ]


def arrange(at, features, theirs):
    return pl.pallas_call(
        arrange_body,
        in_specs=[pl.BlockSpec(memory_space=pltpu.SMEM)]
        + [pl.BlockSpec(memory_space=pltpu.VMEM)] * 2,
        out_shape=jax.ShapeDtypeStruct((NX * 2 * features.shape[0], BLOCK), jnp.bfloat16),
        compiler_params=pltpu.CompilerParams(vmem_limit_bytes=VMEM_LIMIT),
        cost_estimate=pl.CostEstimate(
            flops=4 * 2 * 256 * BLOCK * BLOCK, bytes_accessed=4 << 20, transcendentals=0
        ),
    )(at, features, theirs)


def pick_body(at, features, theirs_ref):
    for x in range(NX):
        from_block = pl.ds(pl.multiple_of((x * NC + 1 - at[2]) * BLOCK, BLOCK), BLOCK)
        theirs_ref[:, x * BLOCK : (x + 1) * BLOCK] = features[:, from_block]


def pick(at, features):
    return pl.pallas_call(
        pick_body,
        in_specs=[pl.BlockSpec(memory_space=pltpu.SMEM), pl.BlockSpec(memory_space=pltpu.VMEM)],
        out_shape=jax.ShapeDtypeStruct((features.shape[0], NX * BLOCK), jnp.bfloat16),
        compiler_params=pltpu.CompilerParams(vmem_limit_bytes=VMEM_LIMIT),
    )(at, features)


def stack_body(own, first, second, third, plane_ref):
    rows = own.shape[0]
    for i, piece in enumerate((own, first, second, third)):
        plane_ref[pl.ds(i * rows, rows), :] = piece[...]


def stack_plane(pieces):
    rows = sum(piece.shape[0] for piece in pieces)
    return pl.pallas_call(
        stack_body,
        out_shape=pltpu.VMEM((rows, pieces[0].shape[1]), jnp.bfloat16),
        compiler_params=pltpu.CompilerParams(vmem_limit_bytes=VMEM_LIMIT),
    )(*[in_vmem(p) for p in pieces])


def in_vmem(array):
    return pltpu.with_memory_space_constraint(array, pltpu.VMEM)


def first_body(arranged, piece, mine_ref, theirs_ref):
    count = mine_ref.shape[0]
    part = jnp.dot(arranged[: 2 * count, :], piece[...], preferred_element_type=jnp.float32)
    mine_ref[...] = part[:count]
    theirs_ref[...] = part[count:]


def first_sums(arranged, plane):
    count, columns = arranged.shape[0] // NX // 2, plane.shape[1]
    return pl.pallas_call(
        first_body,
        out_shape=[pltpu.VMEM((count, columns), jnp.float32)] * 2,
        compiler_params=pltpu.CompilerParams(vmem_limit_bytes=VMEM_LIMIT),
        cost_estimate=pl.CostEstimate(
            flops=4 * count * BLOCK * columns, bytes_accessed=3 << 20, transcendentals=0
        ),
    )(arranged, in_vmem(plane))


def rest_body(steps, arranged, mine_in, theirs_in, plane, *refs):
    pieces, refs = refs[: len(steps)], refs[len(steps) :]
    mine_ref, theirs_ref, rows_ref, held, in_sems, out_sems = refs
    count = mine_ref.shape[0]
    loads = [
        pltpu.make_async_copy(piece, held.at[i], in_sems.at[i]) for i, piece in enumerate(pieces)
    ]
    for load in loads:
        load.start()
    stores = [pltpu.make_async_copy(plane, rows_ref.at[pl.ds(0, BLOCK)], out_sems.at[0])]
    stores[0].start()
    mine_ref[...] = mine_in[...]
    theirs_ref[...] = theirs_in[...]
    for i, step in enumerate(steps):
        loads[i].wait()
        store = pltpu.make_async_copy(
            held.at[i], rows_ref.at[pl.ds((i + 1) * BLOCK, BLOCK)], out_sems.at[i + 1]
        )
        store.start()
        stores.append(store)
        at = step * 2 * count
        part = jnp.dot(
            arranged[at : at + 2 * count, :], held[i], preferred_element_type=jnp.float32
        )
        mine_ref[...] += part[:count]
        theirs_ref[...] += part[count:]
    for store in stores:
        store.wait()


def rest_sums(arranged, sums, plane, pieces, steps):
    count, columns = sums[0].shape
    whole = pl.BlockSpec(memory_space=pltpu.VMEM)
    left = pl.BlockSpec(memory_space=pl.ANY)
    n = len(pieces)
    return pl.pallas_call(
        functools.partial(rest_body, steps),
        in_specs=[whole] * 3 + [left] * (n + 1),
        out_specs=[whole, whole, left],
        out_shape=[
            pltpu.VMEM((count, columns), jnp.float32),
            pltpu.VMEM((count, columns), jnp.float32),
            jax.ShapeDtypeStruct(((n + 1) * BLOCK, columns), jnp.bfloat16),
        ],
        scratch_shapes=[
            pltpu.VMEM((n, BLOCK, columns), jnp.bfloat16),
            pltpu.SemaphoreType.DMA((n,)),
            pltpu.SemaphoreType.DMA((n + 1,)),
        ],
        compiler_params=pltpu.CompilerParams(vmem_limit_bytes=VMEM_LIMIT),
        cost_estimate=pl.CostEstimate(
            flops=n * 4 * count * BLOCK * columns, bytes_accessed=n * 3 << 20, transcendentals=0
        ),
    )(arranged, *[in_vmem(x) for x in sums], plane, *pieces)


def by_source(pieces, steps, parity, cut, join):
    at = {step: piece for step, piece in zip(steps, pieces)}
    for s in range(NX):
        turned = join([cut(at[e], s) for e in range(NY)])
        yield s, jnp.where(parity == 0, turned, at[s])


def query_part_body(steps, flip, at, grads, all_rows, out_ref, weights, held, sems):
    x_me, y_me = at[0], at[1]
    parity = at[2] if flip == 0 else 1 - at[2]
    rows = grads.shape[0]
    loads = []
    for i in range(NX):
        source = all_rows.at[pl.ds(i * BLOCK, BLOCK), pl.ds(0, HQ * HD)]
        loads.append(pltpu.make_async_copy(source, weights.at[i], sems.at[i]))
        loads[-1].start()
    order = order_matrix(y_me)
    for i in range(NX):
        loads[i].wait()
        held[i] = lax.dot_general(
            grads[...], weights[i], TURN, preferred_element_type=jnp.float32
        )
    for s, part in by_source(
        [held[i] for i in range(NX)], steps, parity,
        lambda piece, d: piece[:, d * SPAN : (d + 1) * SPAN],
        lambda parts: jnp.concatenate(parts, axis=1),
    ):
        high = part.astype(jnp.bfloat16)
        low = (part - high.astype(jnp.float32)).astype(jnp.bfloat16)
        back = lax.dot_general(
            jnp.concatenate([high, low], axis=0), order, TURN, preferred_element_type=jnp.float32
        )
        to_block = pl.ds(pl.multiple_of((x_me - s + NX) % NX * BLOCK, BLOCK), BLOCK)
        out_ref[:, to_block] = back[:rows] + back[rows:]


def query_part_of(at, grads, all_rows, steps, flip):
    rows = grads.shape[0]
    whole = pl.BlockSpec(memory_space=pltpu.VMEM)
    left = pl.BlockSpec(memory_space=pl.ANY)
    return pl.pallas_call(
        functools.partial(query_part_body, steps, flip),
        in_specs=[pl.BlockSpec(memory_space=pltpu.SMEM), whole, left],
        out_shape=pltpu.VMEM((rows, NX * BLOCK), jnp.float32),
        scratch_shapes=[
            pltpu.VMEM((NX, BLOCK, HQ * HD), jnp.bfloat16),
            pltpu.VMEM((NX, rows, BLOCK), jnp.float32),
            pltpu.SemaphoreType.DMA((NX,)),
        ],
        compiler_params=pltpu.CompilerParams(vmem_limit_bytes=VMEM_LIMIT),
        cost_estimate=pl.CostEstimate(
            flops=NX * 2 * rows * BLOCK * (HQ * HD + 2 * BLOCK),
            bytes_accessed=6 << 20,
            transcendentals=0,
        ),
    )(at, grads, all_rows)


def pair_weights_body(steps, flip, at, all_rows, out_ref, weights, sem):
    x_me, y_me = at[0], at[1]
    parity = at[2] if flip == 0 else 1 - at[2]
    load = pltpu.make_async_copy(all_rows.at[:, pl.ds(HQ * HD, 2 * HD)], weights, sem)
    load.start()
    order = order_matrix(y_me)
    load.wait()
    for s, part in by_source(
        [weights[i * BLOCK : (i + 1) * BLOCK, :] for i in range(NX)], steps, parity,
        lambda piece, d: piece[d * SPAN : (d + 1) * SPAN],
        lambda parts: jnp.concatenate(parts, axis=0),
    ):
        to_block = pl.ds(pl.multiple_of((x_me - s + NX) % NX * BLOCK, BLOCK), BLOCK)
        out_ref[to_block, :] = jnp.dot(
            order, part, preferred_element_type=jnp.float32
        ).astype(jnp.bfloat16)


def pair_weights_of(at, all_rows, steps, flip):
    left = pl.BlockSpec(memory_space=pl.ANY)
    return pl.pallas_call(
        functools.partial(pair_weights_body, steps, flip),
        in_specs=[pl.BlockSpec(memory_space=pltpu.SMEM), left],
        out_shape=pltpu.VMEM((NX * BLOCK, 2 * HD), jnp.bfloat16),
        scratch_shapes=[
            pltpu.VMEM((NX * BLOCK, 2 * HD), jnp.bfloat16),
            pltpu.SemaphoreType.DMA,
        ],
        compiler_params=pltpu.CompilerParams(vmem_limit_bytes=VMEM_LIMIT),
        cost_estimate=pl.CostEstimate(
            flops=NX * 2 * BLOCK * BLOCK * 2 * HD, bytes_accessed=3 << 20, transcendentals=0
        ),
    )(at, all_rows)


def finish_body(at, pair_out, own_part, other_part, own_w, other_w, out_ref):
    for x in range(NX):
        cut = slice(x * BLOCK, (x + 1) * BLOCK)
        for flip, part, w in ((0, own_part, own_w), (1, other_part, other_w)):
            parity = at[2] if flip == 0 else 1 - at[2]
            total = part[:, cut] + lax.dot_general(
                pair_out[...], w[cut, :], TURN, preferred_element_type=jnp.float32
            )
            to_block = pl.ds(pl.multiple_of((x * NC + parity) * BLOCK, BLOCK), BLOCK)
            out_ref[:, to_block] = total.astype(jnp.bfloat16)


def finish(at, pair_out, parts, weights):
    whole = pl.BlockSpec(memory_space=pltpu.VMEM)
    return pl.pallas_call(
        finish_body,
        in_specs=[pl.BlockSpec(memory_space=pltpu.SMEM)] + [whole] * 5,
        out_shape=jax.ShapeDtypeStruct((pair_out.shape[0], NX * NC * BLOCK), jnp.bfloat16),
        compiler_params=pltpu.CompilerParams(vmem_limit_bytes=VMEM_LIMIT),
    )(at, pair_out, *[in_vmem(p) for p in parts], *[in_vmem(w) for w in weights])


def shifted(block, axis, distance):
    devices = range(lax.axis_size(axis))
    return lax.ppermute(block, axis, [(i - distance, i) for i in devices if i - distance in devices])


def angles_for(positions, head_size):
    half_size = head_size // 2
    inverse = jnp.power(
        jnp.float32(ROPE_BASE), -jnp.arange(half_size, dtype=jnp.float32) / half_size
    )
    phase_angle = positions.astype(jnp.float32)[:, None] * inverse[None, :]
    return (jnp.cos(phase_angle), jnp.sin(phase_angle))


def rotate(vectors, cos_part, sin_part):
    half_size = vectors.shape[-1] // 2
    a = vectors[..., :half_size]
    b = vectors[..., half_size:]
    return jnp.concatenate([a * cos_part - b * sin_part, b * cos_part + a * sin_part], axis=-1)


def local(tokens, doc_start, out_grad, w_qkv):
    row_count = tokens.shape[1]
    score_scale = 1.0 / math.sqrt(HD)
    features = tokens[0]
    begin_rows = doc_start[0]
    grad_rows = out_grad[0].reshape(row_count, HQ, HD)
    fsdp, ctx = lax.axis_index("fsdp"), lax.axis_index("ctx")
    x_me, core = fsdp // NC, fsdp % NC
    y_me = ctx % NY

    column = w_qkv
    for far in (8, 4, 2, 1):
        column = lax.all_gather(
            column, "ctx", axis=0, tiled=True,
            axis_index_groups=[
                [z * NY + y, (z + far) * NY + y] for z in range(NZ) if not z & far for y in range(NY)
            ],
        )
    second, first, third = (hop(column, d, 0) for d in (2, 1, 3))

    at = jnp.stack([x_me, y_me, core]).astype(jnp.int32)
    plane, theirs = lax.optimization_barrier(
        (stack_plane([column, first, second, third]), pick(at, features))
    )
    two, one, three = (hop(plane, d, 1) for d in (2, 1, 3))
    arranged = arrange(at, features, swap_cores(theirs))
    steps = (0, 3, 1, 2)
    sums = first_sums(arranged, plane)
    mine, theirs, own_w = rest_sums(arranged, sums, plane, [three, one, two], steps[1:])
    projected = mine + swap_cores(theirs)
    other_w = swap_cores(own_w)
    pair_pre, query_pre = projected[:, HQ * HD :], projected[:, : HQ * HD]

    first_row = ctx * row_count
    query_index = first_row + jnp.arange(row_count, dtype=jnp.int32)
    cos_part, sin_part = angles_for(query_index - begin_rows, HD)
    pair_rows = jnp.concatenate(
        [rotate(pair_pre[:, :HD], cos_part, sin_part), pair_pre[:, HD:]], axis=1
    ).astype(jnp.bfloat16)
    back2 = shifted(pair_rows, "ctx", 2)
    back2, at_later = lax.optimization_barrier((back2, at))
    back31, pair_w_own = lax.optimization_barrier(
        (
            shifted(jnp.concatenate([back2, pair_rows], axis=0), "ctx", 1),
            pair_weights_of(at_later, own_w, steps, 0),
        )
    )
    window = jnp.concatenate([back31[:row_count], back2, back31[row_count:], pair_rows], axis=0)

    queries = rotate(
        query_pre.reshape(row_count, HQ, HD), cos_part[:, None, :], sin_part[:, None, :]
    ).astype(jnp.bfloat16)
    keys, values = window[:, :HD], window[:, HD:]
    key_index = first_row - (REACH - 1) * row_count + jnp.arange(REACH * row_count, dtype=jnp.int32)
    allowed = (key_index[None, :] <= query_index[:, None]) & (
        key_index[None, :] >= begin_rows[:, None]
    )
    scores = (
        jnp.einsum("qhd,kd->hqk", queries, keys, preferred_element_type=jnp.float32) * score_scale
    )
    scores = jnp.where(allowed[None], scores, MASKED)
    top = jnp.max(scores, axis=-1, keepdims=True)
    unnormed = jnp.where(allowed[None], jnp.exp(scores - top), 0.0)
    probs = unnormed / jnp.sum(unnormed, axis=-1, keepdims=True)
    probs_low = probs.astype(jnp.bfloat16)
    grad_probs = jnp.einsum("qhd,kd->hqk", grad_rows, values, preferred_element_type=jnp.float32)
    attn_out = jnp.einsum(
        "hqk,kd->hqd", probs_low, values, preferred_element_type=jnp.float32
    ).astype(jnp.bfloat16)
    row_delta = jnp.sum(
        jnp.transpose(grad_rows, (1, 0, 2)).astype(jnp.float32) * attn_out.astype(jnp.float32),
        axis=-1, keepdims=True,
    )
    grad_value = jnp.einsum("hqk,qhd->kd", probs_low, grad_rows, preferred_element_type=jnp.float32)
    grad_scores = (probs * (grad_probs - row_delta)).astype(jnp.bfloat16)
    grad_query = (
        jnp.einsum("hqk,kd->qhd", grad_scores, keys, preferred_element_type=jnp.float32)
        * score_scale
    )
    grad_key = (
        jnp.einsum("hqk,qhd->kd", grad_scores, queries, preferred_element_type=jnp.float32)
        * score_scale
    )
    pair_grad = jnp.concatenate([grad_key, grad_value], axis=1)
    query_out = rotate(grad_query, cos_part[:, None, :], -sin_part[:, None, :]).reshape(
        row_count, HQ * HD
    ).astype(jnp.bfloat16)
    back3, back2, back1, own_grad = (
        pair_grad[i * row_count : (i + 1) * row_count] for i in range(REACH)
    )
    came, part_own = lax.optimization_barrier(
        (
            shifted(jnp.concatenate([back3, back1], axis=0).astype(jnp.bfloat16), "ctx", -1),
            query_part_of(at, query_out, own_w, steps, 0),
        )
    )
    came = came.astype(jnp.float32)
    last, part_other, pair_w_other = lax.optimization_barrier(
        (
            shifted((back2 + came[:row_count]).astype(jnp.bfloat16), "ctx", -2),
            query_part_of(at, query_out, other_w, steps, 1),
            pair_weights_of(at, other_w, steps, 1),
        )
    )
    pair_total = own_grad + came[row_count:] + last.astype(jnp.float32)
    pair_out = jnp.concatenate(
        [rotate(pair_total[:, :HD], cos_part, -sin_part), pair_total[:, HD:]], axis=1
    ).astype(jnp.bfloat16)
    return finish(at, pair_out, [part_own, part_other], [pair_w_own, pair_w_other])[None]


def solution(mesh):
    placed = (
        P("fsdp", "ctx", None),
        P("fsdp", "ctx"),
        P("fsdp", "ctx", None),
        P(("fsdp", "ctx"), None),
    )
    return jax.shard_map(
        local, mesh=mesh, in_specs=placed, out_specs=P("fsdp", "ctx", None), check_vma=False
    )
```

```python
import functools
import math

import jax
import jax.numpy as jnp
from jax import lax
from jax.experimental import pallas as pl
from jax.experimental.pallas import tpu as pltpu
from jax.sharding import PartitionSpec as P

HQ = 8
HD = 128
REACH = 4
ROPE_BASE = 500000.0
MASKED = -1e30
NX, NC, NZ, NY = 4, 2, 16, 4
ALL = ("fsdp", "ctx")


def place(x, c, z, y):
    return (x * NC + c) * (NZ * NY) + z * NY + y


def route(move):
    return [
        (place(x, c, z, y), place(*move(x, c, z, y)))
        for x in range(NX)
        for c in range(NC)
        for z in range(NZ)
        for y in range(NY)
    ]


def along_y(block, distance):
    return lax.ppermute(
        block, ALL, route(lambda x, c, z, y: (x, c, z, (y + distance) % NY))
    )


def along_x(block, distance):
    return lax.ppermute(
        block, ALL, route(lambda x, c, z, y: ((x + distance) % NX, c, z, y))
    )


def swap_cores(block):
    return lax.ppermute(block, ALL, route(lambda x, c, z, y: (x, 1 - c, z, y)))


BLOCK = NZ * NY * 8
SPAN = NZ * 8
TURN = (((1,), (1,)), ((), ()))
VMEM_LIMIT = 14 * 1024 * 1024


def order_matrix(y_me):
    slot = lax.broadcasted_iota(jnp.int32, (BLOCK, BLOCK), 1)
    source = lax.broadcasted_iota(jnp.int32, (BLOCK, BLOCK), 0)
    step, inner = slot // SPAN, slot % SPAN
    wanted = inner // 8 * (NY * 8) + (y_me - step + NY) % NY * 8 + inner % 8
    return (source == wanted).astype(jnp.bfloat16)


def x_block(x_me, step):
    return pl.multiple_of((x_me - step + NX) % NX * BLOCK, BLOCK)


def arrange_body(at, order, features, theirs, out_ref):
    for e in range(NX):
        x_at = (at[0] - e + NX) % NX
        own = features[:, pl.ds(pl.multiple_of((x_at * NC + at[2]) * BLOCK, BLOCK), BLOCK)]
        other = theirs[:, pl.ds(pl.multiple_of(x_at * BLOCK, BLOCK), BLOCK)]
        both = jnp.concatenate([own, other], axis=0)
        rows = both.shape[0]
        out_ref[e * rows : (e + 1) * rows, :] = jnp.dot(
            both, order[...], preferred_element_type=jnp.float32
        ).astype(jnp.bfloat16)


SCALARS = pl.BlockSpec(memory_space=pltpu.SMEM)
WHOLE = pl.BlockSpec(memory_space=pltpu.VMEM)
LEFT = pl.BlockSpec(memory_space=pl.ANY)


def call(body, in_specs, out_shape, flops, mib, **more):
    return pl.pallas_call(
        body,
        in_specs=in_specs,
        out_shape=out_shape,
        compiler_params=pltpu.CompilerParams(vmem_limit_bytes=VMEM_LIMIT),
        cost_estimate=pl.CostEstimate(flops=flops, bytes_accessed=mib << 20, transcendentals=0),
        **more,
    )


def arrange(at, order, features, theirs):
    rows = features.shape[0]
    return call(
        arrange_body,
        [SCALARS] + [WHOLE] * 3,
        pltpu.VMEM((NX * 2 * rows, BLOCK), jnp.bfloat16),
        NX * 4 * rows * BLOCK * BLOCK, 4,
    )(at, in_vmem(order), features, theirs)


def stack_body(at, features, own, first, second, third, a_ref, b_ref, theirs_ref, sems):
    copies = []
    for x in range(NX):
        from_block = pl.ds(pl.multiple_of((x * NC + 1 - at[2]) * BLOCK, BLOCK), BLOCK)
        copies.append(
            pltpu.make_async_copy(
                features.at[:, from_block], theirs_ref.at[:, pl.ds(x * BLOCK, BLOCK)], sems.at[x]
            )
        )
        copies[-1].start()
    rows = own.shape[0]
    for ref, pair in ((a_ref, (own, first)), (b_ref, (second, third))):
        for i, piece in enumerate(pair):
            ref[i * rows : (i + 1) * rows, :] = piece[...]
    for copy in copies:
        copy.wait()


def stack_plane(at, features, pieces):
    rows, columns = pieces[0].shape
    return call(
        stack_body,
        [SCALARS, LEFT] + [WHOLE] * 4,
        [
            pltpu.VMEM((2 * rows, columns), jnp.bfloat16),
            pltpu.VMEM((2 * rows, columns), jnp.bfloat16),
            jax.ShapeDtypeStruct((features.shape[0], NX * BLOCK), jnp.bfloat16),
        ],
        0, 4,
        out_specs=[WHOLE, WHOLE, LEFT],
        scratch_shapes=[pltpu.SemaphoreType.DMA((NX,))],
    )(at, features, *[in_vmem(p) for p in pieces])


def in_vmem(array):
    return pltpu.with_memory_space_constraint(array, pltpu.VMEM)


def put_rows(steps, pieces, rows_ref, sems):
    half, stores = BLOCK // 2, []
    for i, piece in enumerate(pieces):
        at = steps[i // 2] * BLOCK + i % 2 * half
        stores.append(pltpu.make_async_copy(piece, rows_ref.at[pl.ds(at, half)], sems.at[i]))
        stores[-1].start()
    return stores


def products(steps, count, arranged, pieces):
    half, total = BLOCK // 2, 0.0
    for i, step in enumerate(steps):
        left = arranged[step * 2 * count : (step + 1) * 2 * count, :]
        for j in range(2):
            total += jnp.dot(
                left[:, j * half : (j + 1) * half], pieces[2 * i + j][...],
                preferred_element_type=jnp.float32,
            )
    return total[:count], total[count:]


def early_body(steps, arranged, *refs):
    pieces, (mine_ref, theirs_ref, rows_ref, sems) = refs[: 2 * len(steps)], refs[2 * len(steps) :]
    stores = put_rows(steps, pieces, rows_ref, sems)
    mine_ref[...], theirs_ref[...] = products(steps, mine_ref.shape[0], arranged, pieces)
    for store in stores:
        store.wait()


def early_sums(arranged, pieces, steps):
    count, columns = arranged.shape[0] // NX // 2, pieces[0].shape[1]
    return call(
        functools.partial(early_body, steps),
        [WHOLE] * (1 + len(pieces)),
        [
            pltpu.VMEM((count, columns), jnp.float32),
            pltpu.VMEM((count, columns), jnp.float32),
            jax.ShapeDtypeStruct((NX * BLOCK, columns), jnp.bfloat16),
        ],
        len(steps) * 4 * count * BLOCK * columns, len(steps) * 2,
        out_specs=[WHOLE, WHOLE, LEFT],
        scratch_shapes=[pltpu.SemaphoreType.DMA((len(pieces),))],
    )(in_vmem(arranged), *[in_vmem(p) for p in pieces])


def late_body(steps, arranged, mine, theirs, first, second, mine_ref, theirs_ref):
    more, more_theirs = products(steps, mine.shape[0], arranged, (first, second))
    mine_ref[...] = mine[...] + more
    theirs_ref[...] = theirs[...] + more_theirs


def late_sums(arranged, sums, pieces, steps):
    count, columns = sums[0].shape
    return call(
        functools.partial(late_body, steps),
        [WHOLE] * 5,
        [pltpu.VMEM((count, columns), jnp.float32)] * 2,
        len(steps) * 4 * count * BLOCK * columns, 4,
    )(*[in_vmem(x) for x in (arranged, *sums, *pieces)])


def place_body(steps, first, second, after, rows_in, rows_ref, sems):
    for store in put_rows(steps, (first, second), rows_ref, sems):
        store.wait()


def place_rows(pieces, after, rows, steps):
    return call(
        functools.partial(place_body, steps),
        [WHOLE, WHOLE, LEFT, LEFT],
        jax.ShapeDtypeStruct(rows.shape, rows.dtype),
        0, 4,
        out_specs=LEFT,
        scratch_shapes=[pltpu.SemaphoreType.DMA((2,))],
        input_output_aliases={3: 0},
    )(*[in_vmem(p) for p in pieces], after, rows)


def query_part_body(at, order, grads, all_rows, out_ref, weights, sems):
    rows = grads.shape[0]
    loads = []
    for e in range(NX):
        source = all_rows.at[pl.ds(e * BLOCK, BLOCK), pl.ds(0, HQ * HD)]
        loads.append(pltpu.make_async_copy(source, weights.at[e], sems.at[e]))
        loads[-1].start()
    for e in range(NX):
        loads[e].wait()
        part = lax.dot_general(
            grads[...], weights[e], TURN, preferred_element_type=jnp.float32
        )
        high = part.astype(jnp.bfloat16)
        low = (part - high.astype(jnp.float32)).astype(jnp.bfloat16)
        back = lax.dot_general(
            jnp.concatenate([high, low], axis=0), order[...], TURN,
            preferred_element_type=jnp.float32,
        )
        out_ref[:, pl.ds(x_block(at[0], e), BLOCK)] = back[:rows] + back[rows:]


def query_part_of(at, order, grads, all_rows):
    rows = grads.shape[0]
    return call(
        query_part_body,
        [SCALARS, WHOLE, WHOLE, LEFT],
        pltpu.VMEM((rows, NX * BLOCK), jnp.float32),
        NX * 2 * rows * BLOCK * (HQ * HD + 2 * BLOCK), 6,
        scratch_shapes=[
            pltpu.VMEM((NX, BLOCK, HQ * HD), jnp.bfloat16),
            pltpu.SemaphoreType.DMA((NX,)),
        ],
    )(at, in_vmem(order), grads, all_rows)


def pair_weights_body(at, order, all_rows, out_ref, weights, sem):
    load = pltpu.make_async_copy(all_rows.at[:, pl.ds(HQ * HD, 2 * HD)], weights, sem)
    load.start()
    load.wait()
    for e in range(NX):
        out_ref[pl.ds(x_block(at[0], e), BLOCK), :] = jnp.dot(
            order[...], weights[e * BLOCK : (e + 1) * BLOCK, :],
            preferred_element_type=jnp.float32,
        ).astype(jnp.bfloat16)


def pair_weights_of(at, order, all_rows):
    return call(
        pair_weights_body,
        [SCALARS, WHOLE, LEFT],
        pltpu.VMEM((NX * BLOCK, 2 * HD), jnp.bfloat16),
        NX * 2 * BLOCK * BLOCK * 2 * HD, 3,
        scratch_shapes=[
            pltpu.VMEM((NX * BLOCK, 2 * HD), jnp.bfloat16),
            pltpu.SemaphoreType.DMA,
        ],
    )(at, in_vmem(order), all_rows)


def finish_body(at, pair_out, own_part, other_part, own_w, other_w, out_ref):
    for x in range(NX):
        cut = slice(x * BLOCK, (x + 1) * BLOCK)
        for flip, part, w in ((0, own_part, own_w), (1, other_part, other_w)):
            parity = at[2] if flip == 0 else 1 - at[2]
            total = part[:, cut] + lax.dot_general(
                pair_out[...], w[cut, :], TURN, preferred_element_type=jnp.float32
            )
            to_block = pl.ds(pl.multiple_of((x * NC + parity) * BLOCK, BLOCK), BLOCK)
            out_ref[:, to_block] = total.astype(jnp.bfloat16)


def finish(at, pair_out, parts, weights):
    whole = pl.BlockSpec(memory_space=pltpu.VMEM)
    return pl.pallas_call(
        finish_body,
        in_specs=[pl.BlockSpec(memory_space=pltpu.SMEM)] + [whole] * 5,
        out_shape=jax.ShapeDtypeStruct((pair_out.shape[0], NX * NC * BLOCK), jnp.bfloat16),
        compiler_params=pltpu.CompilerParams(vmem_limit_bytes=VMEM_LIMIT),
    )(at, pair_out, *[in_vmem(p) for p in parts], *[in_vmem(w) for w in weights])


def shifted(block, axis, distance):
    devices = range(lax.axis_size(axis))
    return lax.ppermute(block, axis, [(i - distance, i) for i in devices if i - distance in devices])


def angles_for(positions, head_size):
    half_size = head_size // 2
    inverse = jnp.power(
        jnp.float32(ROPE_BASE), -jnp.arange(half_size, dtype=jnp.float32) / half_size
    )
    phase_angle = positions.astype(jnp.float32)[:, None] * inverse[None, :]
    return (jnp.cos(phase_angle), jnp.sin(phase_angle))


def rotate(vectors, cos_part, sin_part):
    half_size = vectors.shape[-1] // 2
    a = vectors[..., :half_size]
    b = vectors[..., half_size:]
    return jnp.concatenate([a * cos_part - b * sin_part, b * cos_part + a * sin_part], axis=-1)


def local(tokens, doc_start, out_grad, w_qkv):
    row_count = tokens.shape[1]
    score_scale = 1.0 / math.sqrt(HD)
    features = tokens[0]
    begin_rows = doc_start[0]
    grad_rows = out_grad[0].reshape(row_count, HQ, HD)
    fsdp, ctx = lax.axis_index("fsdp"), lax.axis_index("ctx")
    x_me, core = fsdp // NC, fsdp % NC
    y_me = ctx % NY

    column = lax.all_gather(
        w_qkv, "ctx", axis=0, tiled=True,
        axis_index_groups=[[z * NY + y for z in range(NZ)] for y in range(NY)],
    )
    second, first, third = (along_y(column, d) for d in (2, 1, 3))

    at = jnp.stack([x_me, y_me, core]).astype(jnp.int32)
    order = order_matrix(y_me)
    a0, b0, theirs = stack_plane(at, features, [column, first, second, third])
    a1, b3 = along_x(a0, 1), along_x(b0, 3)
    b1, a3 = along_x(b0, 1), along_x(a0, 3)
    a2, b2 = along_x(a1, 1), along_x(b3, 3)
    arranged = arrange(at, order, features, swap_cores(theirs))
    *sums, own_w = early_sums(arranged, [a0, b0, a1, b1, a3, b3], (0, 1, 3))
    mine, theirs = late_sums(arranged, sums, [a2, b2], (2,))
    own_w = place_rows([a2, b2], theirs, own_w, (2,))
    projected = mine + swap_cores(theirs)
    other_w = swap_cores(own_w)
    pair_pre, query_pre = projected[:, HQ * HD :], projected[:, : HQ * HD]

    first_row = ctx * row_count
    query_index = first_row + jnp.arange(row_count, dtype=jnp.int32)
    cos_part, sin_part = angles_for(query_index - begin_rows, HD)
    pair_rows = jnp.concatenate(
        [rotate(pair_pre[:, :HD], cos_part, sin_part), pair_pre[:, HD:]], axis=1
    ).astype(jnp.bfloat16)
    projected_at, pair_rows = lax.optimization_barrier((at, pair_rows))
    back2, pair_w_own = lax.optimization_barrier(
        (shifted(pair_rows, "ctx", 2), pair_weights_of(projected_at, order, own_w))
    )
    back31 = shifted(jnp.concatenate([back2, pair_rows], axis=0), "ctx", 1)
    window = jnp.concatenate([back31[:row_count], back2, back31[row_count:], pair_rows], axis=0)

    queries = rotate(
        query_pre.reshape(row_count, HQ, HD), cos_part[:, None, :], sin_part[:, None, :]
    ).astype(jnp.bfloat16)
    keys, values = window[:, :HD], window[:, HD:]
    key_index = first_row - (REACH - 1) * row_count + jnp.arange(REACH * row_count, dtype=jnp.int32)
    allowed = (key_index[None, :] <= query_index[:, None]) & (
        key_index[None, :] >= begin_rows[:, None]
    )
    scores = (
        jnp.einsum("qhd,kd->hqk", queries, keys, preferred_element_type=jnp.float32) * score_scale
    )
    scores = jnp.where(allowed[None], scores, MASKED)
    top = jnp.max(scores, axis=-1, keepdims=True)
    unnormed = jnp.where(allowed[None], jnp.exp(scores - top), 0.0)
    probs = unnormed / jnp.sum(unnormed, axis=-1, keepdims=True)
    probs_low = probs.astype(jnp.bfloat16)
    grad_probs = jnp.einsum("qhd,kd->hqk", grad_rows, values, preferred_element_type=jnp.float32)
    attn_out = jnp.einsum(
        "hqk,kd->hqd", probs_low, values, preferred_element_type=jnp.float32
    ).astype(jnp.bfloat16)
    row_delta = jnp.sum(
        jnp.transpose(grad_rows, (1, 0, 2)).astype(jnp.float32) * attn_out.astype(jnp.float32),
        axis=-1, keepdims=True,
    )
    grad_value = jnp.einsum("hqk,qhd->kd", probs_low, grad_rows, preferred_element_type=jnp.float32)
    grad_scores = (probs * (grad_probs - row_delta)).astype(jnp.bfloat16)
    grad_query = (
        jnp.einsum("hqk,kd->qhd", grad_scores, keys, preferred_element_type=jnp.float32)
        * score_scale
    )
    grad_key = (
        jnp.einsum("hqk,qhd->kd", grad_scores, queries, preferred_element_type=jnp.float32)
        * score_scale
    )
    pair_grad = jnp.concatenate([grad_key, grad_value], axis=1)
    query_out = rotate(grad_query, cos_part[:, None, :], -sin_part[:, None, :]).reshape(
        row_count, HQ * HD
    ).astype(jnp.bfloat16)
    back3, back2, back1, own_grad = (
        pair_grad[i * row_count : (i + 1) * row_count] for i in range(REACH)
    )
    came, part_own = lax.optimization_barrier(
        (
            shifted(jnp.concatenate([back3, back1], axis=0).astype(jnp.bfloat16), "ctx", -1),
            query_part_of(at, order, query_out, own_w),
        )
    )
    came = came.astype(jnp.float32)
    last, part_other, pair_w_other = lax.optimization_barrier(
        (
            shifted((back2 + came[:row_count]).astype(jnp.bfloat16), "ctx", -2),
            query_part_of(at, order, query_out, other_w),
            pair_weights_of(at, order, other_w),
        )
    )
    pair_total = own_grad + came[row_count:] + last.astype(jnp.float32)
    pair_out = jnp.concatenate(
        [rotate(pair_total[:, :HD], cos_part, -sin_part), pair_total[:, HD:]], axis=1
    ).astype(jnp.bfloat16)
    return finish(at, pair_out, [part_own, part_other], [pair_w_own, pair_w_other])[None]


def solution(mesh):
    placed = (
        P("fsdp", "ctx", None),
        P("fsdp", "ctx"),
        P("fsdp", "ctx", None),
        P(("fsdp", "ctx"), None),
    )
    return jax.shard_map(
        local, mesh=mesh, in_specs=placed, out_specs=P("fsdp", "ctx", None), check_vma=False
    )
```

```python
import functools
import math

import jax
import jax.numpy as jnp
from jax import lax
from jax.experimental import pallas as pl
from jax.experimental.pallas import tpu as pltpu
from jax.sharding import PartitionSpec as P

HQ = 8
HD = 128
REACH = 4
ROPE_BASE = 500000.0
MASKED = -1e30
NX, NC, NZ, NY = 4, 2, 16, 4
ALL = ("fsdp", "ctx")


def place(x, c, z, y):
    return (x * NC + c) * (NZ * NY) + z * NY + y


def route(move):
    return [
        (place(x, c, z, y), place(*move(x, c, z, y)))
        for x in range(NX)
        for c in range(NC)
        for z in range(NZ)
        for y in range(NY)
    ]


def along_y(block, distance):
    return lax.ppermute(
        block, ALL, route(lambda x, c, z, y: (x, c, z, (y + distance) % NY))
    )


def along_x(block, distance):
    return lax.ppermute(
        block, ALL, route(lambda x, c, z, y: ((x + distance) % NX, c, z, y))
    )


def swap_cores(block):
    return lax.ppermute(block, ALL, route(lambda x, c, z, y: (x, 1 - c, z, y)))


BLOCK = NZ * NY * 8
SPAN = NZ * 8
VMEM_LIMIT = 14 * 1024 * 1024


def order_matrix(y_me):
    slot = lax.broadcasted_iota(jnp.int32, (BLOCK, BLOCK), 1)
    source = lax.broadcasted_iota(jnp.int32, (BLOCK, BLOCK), 0)
    step, inner = slot // SPAN, slot % SPAN
    wanted = inner // 8 * (NY * 8) + (y_me - step + NY) % NY * 8 + inner % 8
    return (source == wanted).astype(jnp.bfloat16)


def x_block(x_me, step):
    return pl.multiple_of((x_me - step + NX) % NX * BLOCK, BLOCK)


def arrange_body(at, order, features, theirs, out_ref):
    for e in range(NX):
        x_at = (at[0] - e + NX) % NX
        own = features[:, pl.ds(pl.multiple_of((x_at * NC + at[2]) * BLOCK, BLOCK), BLOCK)]
        other = theirs[:, pl.ds(pl.multiple_of(x_at * BLOCK, BLOCK), BLOCK)]
        both = jnp.concatenate([own, other], axis=0)
        rows = both.shape[0]
        out_ref[e * rows : (e + 1) * rows, :] = jnp.dot(
            both, order[...], preferred_element_type=jnp.float32
        ).astype(jnp.bfloat16)


SCALARS = pl.BlockSpec(memory_space=pltpu.SMEM)
WHOLE = pl.BlockSpec(memory_space=pltpu.VMEM)
LEFT = pl.BlockSpec(memory_space=pltpu.HBM)


def call(body, in_specs, out_shape, flops, mib, **more):
    return pl.pallas_call(
        body,
        in_specs=in_specs,
        out_shape=out_shape,
        compiler_params=pltpu.CompilerParams(vmem_limit_bytes=VMEM_LIMIT),
        cost_estimate=pl.CostEstimate(flops=flops, bytes_accessed=mib << 20, transcendentals=0),
        **more,
    )


def arrange(at, order, features, theirs):
    rows = features.shape[0]
    return call(
        arrange_body,
        [SCALARS] + [WHOLE] * 3,
        pltpu.VMEM((NX * 2 * rows, BLOCK), jnp.bfloat16),
        NX * 4 * rows * BLOCK * BLOCK, 4,
    )(at, order, features, theirs)


def pick_body(at, features, theirs_ref):
    for x in range(NX):
        from_block = pl.ds(pl.multiple_of((x * NC + 1 - at[2]) * BLOCK, BLOCK), BLOCK)
        theirs_ref[:, x * BLOCK : (x + 1) * BLOCK] = features[:, from_block]


def pick(at, features):
    return call(
        pick_body,
        [SCALARS, WHOLE],
        jax.ShapeDtypeStruct((features.shape[0], NX * BLOCK), jnp.bfloat16),
        0, 2,
    )(at, features)


def stack_body(own, first, second, third, plane_ref):
    rows = own.shape[0]
    for i, piece in enumerate((own, first, second, third)):
        plane_ref[i * rows : (i + 1) * rows, :] = piece[...]


def stack_plane(pieces):
    rows, columns = pieces[0].shape
    return call(
        stack_body, [WHOLE] * 4, pltpu.VMEM((4 * rows, columns), jnp.bfloat16), 0, 3
    )(*[in_vmem(p) for p in pieces])


def in_hbm(array):
    return pltpu.with_memory_space_constraint(array, pltpu.HBM)


def in_vmem(array):
    return pltpu.with_memory_space_constraint(array, pltpu.VMEM)


def early_body(steps, arranged, *refs):
    pieces, (mine_ref, theirs_ref, rows_ref, sems) = refs[: len(steps)], refs[len(steps) :]
    count, stores, total = mine_ref.shape[0], [], 0.0
    for i, (step, piece) in enumerate(zip(steps, pieces)):
        store = pltpu.make_async_copy(
            piece, rows_ref.at[pl.ds(step * BLOCK, BLOCK)], sems.at[i]
        )
        store.start()
        stores.append(store)
    for step, piece in zip(steps, pieces):
        total += jnp.dot(
            arranged[step * 2 * count : (step + 1) * 2 * count, :], piece[...],
            preferred_element_type=jnp.float32,
        )
    mine_ref[...] = total[:count]
    theirs_ref[...] = total[count:]
    for store in stores:
        store.wait()


def early_sums(arranged, pieces, steps):
    count, columns = arranged.shape[0] // NX // 2, pieces[0].shape[1]
    return call(
        functools.partial(early_body, steps),
        [WHOLE] * (1 + len(pieces)),
        [
            pltpu.VMEM((count, columns), jnp.float32),
            pltpu.VMEM((count, columns), jnp.float32),
            jax.ShapeDtypeStruct((NX * BLOCK, columns), jnp.bfloat16),
        ],
        len(steps) * 4 * count * BLOCK * columns, len(steps) * 2,
        out_specs=[WHOLE, WHOLE, LEFT],
        scratch_shapes=[pltpu.SemaphoreType.DMA((len(pieces),))],
    )(in_vmem(arranged), *[in_vmem(p) for p in pieces])


def late_body(step, arranged, mine, theirs, first, second, mine_ref, theirs_ref):
    count, half = mine.shape[0], BLOCK // 2
    left = arranged[step * 2 * count : (step + 1) * 2 * count, :]
    more = jnp.dot(left[:, :half], first[...], preferred_element_type=jnp.float32)
    more += jnp.dot(left[:, half:], second[...], preferred_element_type=jnp.float32)
    mine_ref[...] = mine[...] + more[:count]
    theirs_ref[...] = theirs[...] + more[count:]


def late_sums(arranged, sums, halves, step):
    count, columns = sums[0].shape
    return call(
        functools.partial(late_body, step),
        [WHOLE] * 5,
        [pltpu.VMEM((count, columns), jnp.float32)] * 2,
        4 * count * BLOCK * columns, 4,
    )(*[in_vmem(x) for x in (arranged, *sums, *halves)])


def place_body(step, first, second, after, rows_in, rows_ref, sems):
    half, stores = BLOCK // 2, []
    for i, piece in enumerate((first, second)):
        to_rows = rows_ref.at[pl.ds(step * BLOCK + i * half, half)]
        stores.append(pltpu.make_async_copy(piece, to_rows, sems.at[i]))
        stores[-1].start()
    for store in stores:
        store.wait()


def place_rows(halves, after, rows, step):
    return call(
        functools.partial(place_body, step),
        [WHOLE, WHOLE, pl.BlockSpec(memory_space=pl.ANY), LEFT],
        jax.ShapeDtypeStruct(rows.shape, rows.dtype),
        0, 4,
        out_specs=LEFT,
        scratch_shapes=[pltpu.SemaphoreType.DMA((2,))],
        input_output_aliases={3: 0},
    )(*[in_vmem(p) for p in halves], after, rows)


def query_part_body(at, order, grads, all_rows, out_ref, weights, sems):
    rows = grads.shape[0]
    loads = []
    for e in range(NX):
        source = all_rows.at[pl.ds(e * BLOCK, BLOCK), pl.ds(0, HQ * HD)]
        loads.append(pltpu.make_async_copy(source, weights.at[e], sems.at[e]))
        loads[-1].start()
    turned = grads[...].T
    for e in range(NX):
        loads[e].wait()
        part = jnp.dot(weights[e], turned, preferred_element_type=jnp.float32)
        high = part.astype(jnp.bfloat16)
        low = (part - high.astype(jnp.float32)).astype(jnp.bfloat16)
        back = jnp.dot(
            order[...], jnp.concatenate([high, low], axis=1), preferred_element_type=jnp.float32
        )
        out_ref[:, pl.ds(x_block(at[0], e), BLOCK)] = (back[:, :rows] + back[:, rows:]).T


def query_part_of(at, order, grads, all_rows):
    rows = grads.shape[0]
    return call(
        query_part_body,
        [SCALARS, WHOLE, WHOLE, LEFT],
        pltpu.VMEM((rows, NX * BLOCK), jnp.float32),
        NX * 2 * rows * BLOCK * (HQ * HD + 2 * BLOCK), 6,
        scratch_shapes=[
            pltpu.VMEM((NX, BLOCK, HQ * HD), jnp.bfloat16),
            pltpu.SemaphoreType.DMA((NX,)),
        ],
    )(at, in_hbm(order), grads, all_rows)


def pair_weights_body(at, order_t, all_rows, out_ref, weights, sems):
    loads = []
    for e in range(NX):
        source = all_rows.at[pl.ds(e * BLOCK, BLOCK), pl.ds(HQ * HD, 2 * HD)]
        loads.append(pltpu.make_async_copy(source, weights.at[e], sems.at[e]))
        loads[-1].start()
    for e in range(NX):
        loads[e].wait()
        out_ref[:, pl.ds(x_block(at[0], e), BLOCK)] = jnp.dot(
            weights[e].T, order_t[...], preferred_element_type=jnp.float32
        ).astype(jnp.bfloat16)


def pair_weights_of(at, order_t, all_rows):
    return call(
        pair_weights_body,
        [SCALARS, WHOLE, LEFT],
        pltpu.HBM((2 * HD, NX * BLOCK), jnp.bfloat16),
        NX * 2 * BLOCK * BLOCK * 2 * HD, 3,
        scratch_shapes=[
            pltpu.VMEM((NX, BLOCK, 2 * HD), jnp.bfloat16),
            pltpu.SemaphoreType.DMA((NX,)),
        ],
    )(at, in_hbm(order_t), all_rows)


def finish_body(at, pair_out, own_part, other_part, own_w, other_w, out_ref):
    for x in range(NX):
        cut = slice(x * BLOCK, (x + 1) * BLOCK)
        for flip, part, w in ((0, own_part, own_w), (1, other_part, other_w)):
            parity = at[2] if flip == 0 else 1 - at[2]
            total = part[:, cut] + jnp.dot(
                pair_out[...], w[:, cut], preferred_element_type=jnp.float32
            )
            to_block = pl.ds(pl.multiple_of((x * NC + parity) * BLOCK, BLOCK), BLOCK)
            out_ref[:, to_block] = total.astype(jnp.bfloat16)


def finish(at, pair_out, parts, weights):
    whole = pl.BlockSpec(memory_space=pltpu.VMEM)
    return pl.pallas_call(
        finish_body,
        in_specs=[pl.BlockSpec(memory_space=pltpu.SMEM)] + [whole] * 5,
        out_shape=jax.ShapeDtypeStruct((pair_out.shape[0], NX * NC * BLOCK), jnp.bfloat16),
        compiler_params=pltpu.CompilerParams(vmem_limit_bytes=VMEM_LIMIT),
    )(at, pair_out, *[in_vmem(p) for p in parts], *[in_hbm(w) for w in weights])


def shifted(block, axis, distance):
    devices = range(lax.axis_size(axis))
    return lax.ppermute(block, axis, [(i - distance, i) for i in devices if i - distance in devices])


def angles_for(positions, head_size):
    half_size = head_size // 2
    inverse = jnp.power(
        jnp.float32(ROPE_BASE), -jnp.arange(half_size, dtype=jnp.float32) / half_size
    )
    phase_angle = positions.astype(jnp.float32)[:, None] * inverse[None, :]
    return (jnp.cos(phase_angle), jnp.sin(phase_angle))


def rotate(vectors, cos_part, sin_part):
    half_size = vectors.shape[-1] // 2
    a = vectors[..., :half_size]
    b = vectors[..., half_size:]
    return jnp.concatenate([a * cos_part - b * sin_part, b * cos_part + a * sin_part], axis=-1)


def local(tokens, doc_start, out_grad, w_qkv):
    row_count = tokens.shape[1]
    score_scale = 1.0 / math.sqrt(HD)
    features = tokens[0]
    begin_rows = doc_start[0]
    grad_rows = out_grad[0].reshape(row_count, HQ, HD)
    fsdp, ctx = lax.axis_index("fsdp"), lax.axis_index("ctx")
    x_me, core = fsdp // NC, fsdp % NC
    y_me = ctx % NY

    column = lax.all_gather(
        w_qkv, "ctx", axis=0, tiled=True,
        axis_index_groups=[[z * NY + y for z in range(NZ)] for y in range(NY)],
    )
    second, first, third = (along_y(column, d) for d in (2, 1, 3))

    at = jnp.stack([x_me, y_me, core]).astype(jnp.int32)
    order = order_matrix(y_me)
    order_t = order.T
    plane, theirs = lax.optimization_barrier(
        (stack_plane([column, first, second, third]), pick(at, features))
    )
    right, left = along_x(plane, 1), along_x(plane, 3)
    half = BLOCK // 2
    far_a, far_b = along_x(right[:half], 1), along_x(left[half:], 3)
    arranged = arrange(at, order, features, swap_cores(theirs))
    *sums, own_w = early_sums(arranged, [plane, right, left], (0, 1, 3))
    mine, theirs = late_sums(arranged, sums, [far_a, far_b], 2)
    own_w = place_rows([far_a, far_b], theirs, own_w, 2)
    projected = mine + swap_cores(theirs)
    other_w = swap_cores(own_w)
    pair_pre, query_pre = projected[:, HQ * HD :], projected[:, : HQ * HD]

    first_row = ctx * row_count
    query_index = first_row + jnp.arange(row_count, dtype=jnp.int32)
    cos_part, sin_part = angles_for(query_index - begin_rows, HD)
    pair_rows = jnp.concatenate(
        [rotate(pair_pre[:, :HD], cos_part, sin_part), pair_pre[:, HD:]], axis=1
    ).astype(jnp.bfloat16)
    projected_at, pair_rows = lax.optimization_barrier((at, pair_rows))
    back2, pair_w_own = lax.optimization_barrier(
        (shifted(pair_rows, "ctx", 2), pair_weights_of(projected_at, order_t, own_w))
    )
    back31 = shifted(jnp.concatenate([back2, pair_rows], axis=0), "ctx", 1)
    window = jnp.concatenate([back31[:row_count], back2, back31[row_count:], pair_rows], axis=0)

    queries = rotate(
        query_pre.reshape(row_count, HQ, HD), cos_part[:, None, :], sin_part[:, None, :]
    ).astype(jnp.bfloat16)
    keys, values = window[:, :HD], window[:, HD:]
    key_index = first_row - (REACH - 1) * row_count + jnp.arange(REACH * row_count, dtype=jnp.int32)
    allowed = (key_index[None, :] <= query_index[:, None]) & (
        key_index[None, :] >= begin_rows[:, None]
    )
    scores = (
        jnp.einsum("qhd,kd->hqk", queries, keys, preferred_element_type=jnp.float32) * score_scale
    )
    scores = jnp.where(allowed[None], scores, MASKED)
    top = jnp.max(scores, axis=-1, keepdims=True)
    unnormed = jnp.where(allowed[None], jnp.exp(scores - top), 0.0)
    probs = unnormed / jnp.sum(unnormed, axis=-1, keepdims=True)
    probs_low = probs.astype(jnp.bfloat16)
    grad_probs = jnp.einsum("qhd,kd->hqk", grad_rows, values, preferred_element_type=jnp.float32)
    attn_out = jnp.einsum(
        "hqk,kd->hqd", probs_low, values, preferred_element_type=jnp.float32
    ).astype(jnp.bfloat16)
    row_delta = jnp.sum(
        jnp.transpose(grad_rows, (1, 0, 2)).astype(jnp.float32) * attn_out.astype(jnp.float32),
        axis=-1, keepdims=True,
    )
    grad_value = jnp.einsum("hqk,qhd->kd", probs_low, grad_rows, preferred_element_type=jnp.float32)
    grad_scores = (probs * (grad_probs - row_delta)).astype(jnp.bfloat16)
    grad_query = (
        jnp.einsum("hqk,kd->qhd", grad_scores, keys, preferred_element_type=jnp.float32)
        * score_scale
    )
    grad_key = (
        jnp.einsum("hqk,qhd->kd", grad_scores, queries, preferred_element_type=jnp.float32)
        * score_scale
    )
    pair_grad = jnp.concatenate([grad_key, grad_value], axis=1)
    query_out = rotate(grad_query, cos_part[:, None, :], -sin_part[:, None, :]).reshape(
        row_count, HQ * HD
    ).astype(jnp.bfloat16)
    back3, back2, back1, own_grad = (
        pair_grad[i * row_count : (i + 1) * row_count] for i in range(REACH)
    )
    came, part_own = lax.optimization_barrier(
        (
            shifted(jnp.concatenate([back3, back1], axis=0).astype(jnp.bfloat16), "ctx", -1),
            query_part_of(at, order, query_out, own_w),
        )
    )
    came = came.astype(jnp.float32)
    last, part_other, pair_w_other = lax.optimization_barrier(
        (
            shifted((back2 + came[:row_count]).astype(jnp.bfloat16), "ctx", -2),
            query_part_of(at, order, query_out, other_w),
            pair_weights_of(at, order_t, other_w),
        )
    )
    pair_total = own_grad + came[row_count:] + last.astype(jnp.float32)
    pair_out = jnp.concatenate(
        [rotate(pair_total[:, :HD], cos_part, -sin_part), pair_total[:, HD:]], axis=1
    ).astype(jnp.bfloat16)
    return finish(at, pair_out, [part_own, part_other], [pair_w_own, pair_w_other])[None]


def solution(mesh):
    placed = (
        P("fsdp", "ctx", None),
        P("fsdp", "ctx"),
        P("fsdp", "ctx", None),
        P(("fsdp", "ctx"), None),
    )
    return jax.shard_map(
        local, mesh=mesh, in_specs=placed, out_specs=P("fsdp", "ctx", None), check_vma=False
    )
```

```python
import functools
import math

import jax
import jax.numpy as jnp
from jax import lax
from jax.experimental import pallas as pl
from jax.experimental.pallas import tpu as pltpu
from jax.sharding import PartitionSpec as P

HQ = 8
HD = 128
REACH = 4
ROPE_BASE = 500000.0
MASKED = -1e30
NX, NC, NZ, NY = 4, 2, 16, 4
ALL = ("fsdp", "ctx")


def place(x, c, z, y):
    return (x * NC + c) * (NZ * NY) + z * NY + y


def route(move):
    return [
        (place(x, c, z, y), place(*move(x, c, z, y)))
        for x in range(NX)
        for c in range(NC)
        for z in range(NZ)
        for y in range(NY)
    ]


def hop(block, distance, x_core):
    def move(x, c, z, y):
        if c == x_core:
            return (x + distance) % NX, c, z, y
        return x, c, z, (y + distance) % NY

    return lax.ppermute(block, ALL, route(move))


def swap_cores(block):
    return lax.ppermute(block, ALL, route(lambda x, c, z, y: (x, 1 - c, z, y)))


BLOCK = NZ * NY * 8
SPAN = NZ * 8
VMEM_LIMIT = 14 * 1024 * 1024


def order_matrix(y_me):
    slot = lax.broadcasted_iota(jnp.int32, (BLOCK, BLOCK), 1)
    source = lax.broadcasted_iota(jnp.int32, (BLOCK, BLOCK), 0)
    step, inner = slot // SPAN, slot % SPAN
    wanted = inner // 8 * (NY * 8) + (y_me - step + NY) % NY * 8 + inner % 8
    return (source == wanted).astype(jnp.bfloat16)


def x_block(x_me, step):
    return pl.multiple_of((x_me - step + NX) % NX * BLOCK, BLOCK)


def arrange_body(at, order, features, theirs, out_ref):
    for s in range(NX):
        x_at = (at[0] - s + NX) % NX
        own = features[:, pl.ds(pl.multiple_of((x_at * NC + at[2]) * BLOCK, BLOCK), BLOCK)]
        other = theirs[:, pl.ds(pl.multiple_of(x_at * BLOCK, BLOCK), BLOCK)]
        both = jnp.concatenate([own, other], axis=0)
        rows = both.shape[0]
        got = jnp.dot(both, order[...], preferred_element_type=jnp.float32).astype(jnp.bfloat16)

        @pl.when(at[2] == 1)
        def _():
            out_ref[s * rows : (s + 1) * rows, :] = got

        @pl.when(at[2] == 0)
        def _():
            for e in range(NY):
                out_ref[e * rows : (e + 1) * rows, s * SPAN : (s + 1) * SPAN] = got[
                    :, e * SPAN : (e + 1) * SPAN
                ]


SCALARS = pl.BlockSpec(memory_space=pltpu.SMEM)
WHOLE = pl.BlockSpec(memory_space=pltpu.VMEM)
LEFT = pl.BlockSpec(memory_space=pltpu.HBM)


def call(body, in_specs, out_shape, flops, mib, **more):
    return pl.pallas_call(
        body,
        in_specs=in_specs,
        out_shape=out_shape,
        compiler_params=pltpu.CompilerParams(vmem_limit_bytes=VMEM_LIMIT),
        cost_estimate=pl.CostEstimate(flops=flops, bytes_accessed=mib << 20, transcendentals=0),
        **more,
    )


def arrange(at, order, features, theirs):
    rows = features.shape[0]
    return call(
        arrange_body,
        [SCALARS] + [WHOLE] * 3,
        pltpu.VMEM((NX * 2 * rows, BLOCK), jnp.bfloat16),
        NX * 4 * rows * BLOCK * BLOCK, 4,
    )(at, order, features, theirs)


def pick_body(at, features, theirs_ref):
    for x in range(NX):
        from_block = pl.ds(pl.multiple_of((x * NC + 1 - at[2]) * BLOCK, BLOCK), BLOCK)
        theirs_ref[:, x * BLOCK : (x + 1) * BLOCK] = features[:, from_block]


def pick(at, features):
    return call(
        pick_body,
        [SCALARS, WHOLE],
        jax.ShapeDtypeStruct((features.shape[0], NX * BLOCK), jnp.bfloat16),
        0, 2,
    )(at, features)


def stack_body(own, first, second, third, plane_ref):
    rows = own.shape[0]
    for i, piece in enumerate((own, first, second, third)):
        plane_ref[i * rows : (i + 1) * rows, :] = piece[...]


def stack_plane(pieces):
    rows, columns = pieces[0].shape
    return call(
        stack_body, [WHOLE] * 4, pltpu.VMEM((4 * rows, columns), jnp.bfloat16), 0, 3
    )(*[in_vmem(p) for p in pieces])


def in_hbm(array):
    return pltpu.with_memory_space_constraint(array, pltpu.HBM)


def in_vmem(array):
    return pltpu.with_memory_space_constraint(array, pltpu.VMEM)


def early_body(steps, arranged, *refs):
    pieces, (mine_ref, theirs_ref, rows_ref, sems) = refs[: len(steps)], refs[len(steps) :]
    count, stores, total = mine_ref.shape[0], [], 0.0
    for i, (step, piece) in enumerate(zip(steps, pieces)):
        store = pltpu.make_async_copy(
            piece, rows_ref.at[pl.ds(step * BLOCK, BLOCK)], sems.at[i]
        )
        store.start()
        stores.append(store)
    for step, piece in zip(steps, pieces):
        total += jnp.dot(
            arranged[step * 2 * count : (step + 1) * 2 * count, :], piece[...],
            preferred_element_type=jnp.float32,
        )
    mine_ref[...] = total[:count]
    theirs_ref[...] = total[count:]
    for store in stores:
        store.wait()


def early_sums(arranged, pieces, steps):
    count, columns = arranged.shape[0] // NX // 2, pieces[0].shape[1]
    return call(
        functools.partial(early_body, steps),
        [WHOLE] * (1 + len(pieces)),
        [
            pltpu.VMEM((count, columns), jnp.float32),
            pltpu.VMEM((count, columns), jnp.float32),
            jax.ShapeDtypeStruct((NX * BLOCK, columns), jnp.bfloat16),
        ],
        len(steps) * 4 * count * BLOCK * columns, len(steps) * 2,
        out_specs=[WHOLE, WHOLE, LEFT],
        scratch_shapes=[pltpu.SemaphoreType.DMA((len(pieces),))],
    )(in_vmem(arranged), *[in_vmem(p) for p in pieces])


def late_body(steps, arranged, mine, theirs, *refs):
    pieces, (mine_ref, theirs_ref) = refs[: len(steps)], refs[len(steps) :]
    count, more = mine.shape[0], 0.0
    for step, piece in zip(steps, pieces):
        more += jnp.dot(
            arranged[step * 2 * count : (step + 1) * 2 * count, :], piece[...],
            preferred_element_type=jnp.float32,
        )
    mine_ref[...] = mine[...] + more[:count]
    theirs_ref[...] = theirs[...] + more[count:]


def late_sums(arranged, sums, pieces, steps):
    count, columns = sums[0].shape
    return call(
        functools.partial(late_body, steps),
        [WHOLE] * (3 + len(pieces)),
        [pltpu.VMEM((count, columns), jnp.float32)] * 2,
        len(steps) * 4 * count * BLOCK * columns, 4,
    )(*[in_vmem(x) for x in (arranged, *sums, *pieces)])


def place_body(steps, first, second, after, rows_in, rows_ref, sems):
    stores = []
    for i, piece in enumerate((first, second)):
        to_rows = rows_ref.at[pl.ds(steps[i] * BLOCK, BLOCK)]
        stores.append(pltpu.make_async_copy(piece, to_rows, sems.at[i]))
        stores[-1].start()
    for store in stores:
        store.wait()


def place_rows(pieces, after, rows, steps):
    return call(
        functools.partial(place_body, steps),
        [WHOLE, WHOLE, pl.BlockSpec(memory_space=pl.ANY), LEFT],
        jax.ShapeDtypeStruct(rows.shape, rows.dtype),
        0, 4,
        out_specs=LEFT,
        scratch_shapes=[pltpu.SemaphoreType.DMA((2,))],
        input_output_aliases={3: 0},
    )(*[in_vmem(p) for p in pieces], after, rows)


TURN = (((1,), (1,)), ((), ()))


def by_source(pieces, parity, cut, join):
    for s in range(NX):
        turned = join([cut(piece, s) for piece in pieces])
        yield s, jnp.where(parity == 0, turned, pieces[s])


def query_part_body(flip, at, order, grads, all_rows, out_ref, weights, held, sems):
    parity = at[2] if flip == 0 else 1 - at[2]
    rows = grads.shape[0]
    loads = []
    for e in range(NX):
        source = all_rows.at[pl.ds(e * BLOCK, BLOCK), pl.ds(0, HQ * HD)]
        loads.append(pltpu.make_async_copy(source, weights.at[e], sems.at[e]))
        loads[-1].start()
    for e in range(NX):
        loads[e].wait()
        held[e] = lax.dot_general(
            grads[...], weights[e], TURN, preferred_element_type=jnp.float32
        )
    for s, part in by_source(
        [held[e] for e in range(NX)], parity,
        lambda piece, d: piece[:, d * SPAN : (d + 1) * SPAN],
        lambda parts: jnp.concatenate(parts, axis=1),
    ):
        high = part.astype(jnp.bfloat16)
        low = (part - high.astype(jnp.float32)).astype(jnp.bfloat16)
        back = lax.dot_general(
            jnp.concatenate([high, low], axis=0), order[...], TURN,
            preferred_element_type=jnp.float32,
        )
        out_ref[:, pl.ds(x_block(at[0], s), BLOCK)] = back[:rows] + back[rows:]


def query_part_of(at, order, grads, all_rows, flip):
    rows = grads.shape[0]
    return call(
        functools.partial(query_part_body, flip),
        [SCALARS, WHOLE, WHOLE, LEFT],
        pltpu.VMEM((rows, NX * BLOCK), jnp.float32),
        NX * 2 * rows * BLOCK * (HQ * HD + 2 * BLOCK), 6,
        scratch_shapes=[
            pltpu.VMEM((NX, BLOCK, HQ * HD), jnp.bfloat16),
            pltpu.VMEM((NX, rows, BLOCK), jnp.float32),
            pltpu.SemaphoreType.DMA((NX,)),
        ],
    )(at, in_hbm(order), grads, all_rows)


def pair_weights_body(flip, at, order, all_rows, out_ref, weights, sems):
    parity = at[2] if flip == 0 else 1 - at[2]
    loads = []
    for e in range(NX):
        source = all_rows.at[pl.ds(e * BLOCK, BLOCK), pl.ds(HQ * HD, 2 * HD)]
        loads.append(pltpu.make_async_copy(source, weights.at[e], sems.at[e]))
        loads[-1].start()
    for load in loads:
        load.wait()
    for s, part in by_source(
        [weights[e] for e in range(NX)], parity,
        lambda piece, d: piece[d * SPAN : (d + 1) * SPAN],
        lambda parts: jnp.concatenate(parts, axis=0),
    ):
        out_ref[pl.ds(x_block(at[0], s), BLOCK), :] = jnp.dot(
            order[...], part, preferred_element_type=jnp.float32
        ).astype(jnp.bfloat16)


def pair_weights_of(at, order, all_rows, flip):
    return call(
        functools.partial(pair_weights_body, flip),
        [SCALARS, WHOLE, LEFT],
        pltpu.HBM((NX * BLOCK, 2 * HD), jnp.bfloat16),
        NX * 2 * BLOCK * BLOCK * 2 * HD, 3,
        scratch_shapes=[
            pltpu.VMEM((NX, BLOCK, 2 * HD), jnp.bfloat16),
            pltpu.SemaphoreType.DMA((NX,)),
        ],
    )(at, in_hbm(order), all_rows)


def finish_body(at, pair_out, own_part, other_part, own_w, other_w, out_ref):
    for x in range(NX):
        cut = slice(x * BLOCK, (x + 1) * BLOCK)
        for flip, part, w in ((0, own_part, own_w), (1, other_part, other_w)):
            parity = at[2] if flip == 0 else 1 - at[2]
            total = part[:, cut] + lax.dot_general(
                pair_out[...], w[cut, :], TURN, preferred_element_type=jnp.float32
            )
            to_block = pl.ds(pl.multiple_of((x * NC + parity) * BLOCK, BLOCK), BLOCK)
            out_ref[:, to_block] = total.astype(jnp.bfloat16)


def finish(at, pair_out, parts, weights):
    whole = pl.BlockSpec(memory_space=pltpu.VMEM)
    return pl.pallas_call(
        finish_body,
        in_specs=[pl.BlockSpec(memory_space=pltpu.SMEM)] + [whole] * 5,
        out_shape=jax.ShapeDtypeStruct((pair_out.shape[0], NX * NC * BLOCK), jnp.bfloat16),
        compiler_params=pltpu.CompilerParams(vmem_limit_bytes=VMEM_LIMIT),
    )(at, pair_out, *[in_vmem(p) for p in parts], *[in_hbm(w) for w in weights])


def shifted(block, axis, distance):
    devices = range(lax.axis_size(axis))
    return lax.ppermute(block, axis, [(i - distance, i) for i in devices if i - distance in devices])


def angles_for(positions, head_size):
    half_size = head_size // 2
    inverse = jnp.power(
        jnp.float32(ROPE_BASE), -jnp.arange(half_size, dtype=jnp.float32) / half_size
    )
    phase_angle = positions.astype(jnp.float32)[:, None] * inverse[None, :]
    return (jnp.cos(phase_angle), jnp.sin(phase_angle))


def rotate(vectors, cos_part, sin_part):
    half_size = vectors.shape[-1] // 2
    a = vectors[..., :half_size]
    b = vectors[..., half_size:]
    return jnp.concatenate([a * cos_part - b * sin_part, b * cos_part + a * sin_part], axis=-1)


def local(tokens, doc_start, out_grad, w_qkv):
    row_count = tokens.shape[1]
    score_scale = 1.0 / math.sqrt(HD)
    features = tokens[0]
    begin_rows = doc_start[0]
    grad_rows = out_grad[0].reshape(row_count, HQ, HD)
    fsdp, ctx = lax.axis_index("fsdp"), lax.axis_index("ctx")
    x_me, core = fsdp // NC, fsdp % NC
    y_me = ctx % NY

    column = lax.all_gather(
        w_qkv, "ctx", axis=0, tiled=True,
        axis_index_groups=[[z * NY + y for z in range(NZ)] for y in range(NY)],
    )
    second, first, third = (hop(column, d, 0) for d in (2, 1, 3))

    at = jnp.stack([x_me, y_me, core]).astype(jnp.int32)
    order = order_matrix(y_me)
    plane, theirs = lax.optimization_barrier(
        (stack_plane([column, first, second, third]), pick(at, features))
    )
    two, one, three = (hop(plane, d, 1) for d in (2, 1, 3))
    arranged = arrange(at, order, features, swap_cores(theirs))
    *sums, own_w = early_sums(arranged, [plane, three], (0, 3))
    mine, theirs = late_sums(arranged, sums, [one, two], (1, 2))
    own_w = place_rows([one, two], theirs, own_w, (1, 2))
    projected = mine + swap_cores(theirs)
    other_w = swap_cores(own_w)
    pair_pre, query_pre = projected[:, HQ * HD :], projected[:, : HQ * HD]

    first_row = ctx * row_count
    query_index = first_row + jnp.arange(row_count, dtype=jnp.int32)
    cos_part, sin_part = angles_for(query_index - begin_rows, HD)
    pair_rows = jnp.concatenate(
        [rotate(pair_pre[:, :HD], cos_part, sin_part), pair_pre[:, HD:]], axis=1
    ).astype(jnp.bfloat16)
    projected_at, pair_rows = lax.optimization_barrier((at, pair_rows))
    back2, pair_w_own = lax.optimization_barrier(
        (shifted(pair_rows, "ctx", 2), pair_weights_of(projected_at, order, own_w, 0))
    )
    back31 = shifted(jnp.concatenate([back2, pair_rows], axis=0), "ctx", 1)
    window = jnp.concatenate([back31[:row_count], back2, back31[row_count:], pair_rows], axis=0)

    queries = rotate(
        query_pre.reshape(row_count, HQ, HD), cos_part[:, None, :], sin_part[:, None, :]
    ).astype(jnp.bfloat16)
    keys, values = window[:, :HD], window[:, HD:]
    key_index = first_row - (REACH - 1) * row_count + jnp.arange(REACH * row_count, dtype=jnp.int32)
    allowed = (key_index[None, :] <= query_index[:, None]) & (
        key_index[None, :] >= begin_rows[:, None]
    )
    scores = (
        jnp.einsum("qhd,kd->hqk", queries, keys, preferred_element_type=jnp.float32) * score_scale
    )
    scores = jnp.where(allowed[None], scores, MASKED)
    top = jnp.max(scores, axis=-1, keepdims=True)
    unnormed = jnp.where(allowed[None], jnp.exp(scores - top), 0.0)
    probs = unnormed / jnp.sum(unnormed, axis=-1, keepdims=True)
    probs_low = probs.astype(jnp.bfloat16)
    grad_probs = jnp.einsum("qhd,kd->hqk", grad_rows, values, preferred_element_type=jnp.float32)
    attn_out = jnp.einsum(
        "hqk,kd->hqd", probs_low, values, preferred_element_type=jnp.float32
    ).astype(jnp.bfloat16)
    row_delta = jnp.sum(
        jnp.transpose(grad_rows, (1, 0, 2)).astype(jnp.float32) * attn_out.astype(jnp.float32),
        axis=-1, keepdims=True,
    )
    grad_value = jnp.einsum("hqk,qhd->kd", probs_low, grad_rows, preferred_element_type=jnp.float32)
    grad_scores = (probs * (grad_probs - row_delta)).astype(jnp.bfloat16)
    grad_query = (
        jnp.einsum("hqk,kd->qhd", grad_scores, keys, preferred_element_type=jnp.float32)
        * score_scale
    )
    grad_key = (
        jnp.einsum("hqk,qhd->kd", grad_scores, queries, preferred_element_type=jnp.float32)
        * score_scale
    )
    pair_grad = jnp.concatenate([grad_key, grad_value], axis=1)
    query_out = rotate(grad_query, cos_part[:, None, :], -sin_part[:, None, :]).reshape(
        row_count, HQ * HD
    ).astype(jnp.bfloat16)
    back3, back2, back1, own_grad = (
        pair_grad[i * row_count : (i + 1) * row_count] for i in range(REACH)
    )
    came, part_own = lax.optimization_barrier(
        (
            shifted(jnp.concatenate([back3, back1], axis=0).astype(jnp.bfloat16), "ctx", -1),
            query_part_of(at, order, query_out, own_w, 0),
        )
    )
    came = came.astype(jnp.float32)
    last, part_other, pair_w_other = lax.optimization_barrier(
        (
            shifted((back2 + came[:row_count]).astype(jnp.bfloat16), "ctx", -2),
            query_part_of(at, order, query_out, other_w, 1),
            pair_weights_of(at, order, other_w, 1),
        )
    )
    pair_total = own_grad + came[row_count:] + last.astype(jnp.float32)
    pair_out = jnp.concatenate(
        [rotate(pair_total[:, :HD], cos_part, -sin_part), pair_total[:, HD:]], axis=1
    ).astype(jnp.bfloat16)
    return finish(at, pair_out, [part_own, part_other], [pair_w_own, pair_w_other])[None]


def solution(mesh):
    placed = (
        P("fsdp", "ctx", None),
        P("fsdp", "ctx"),
        P("fsdp", "ctx", None),
        P(("fsdp", "ctx"), None),
    )
    return jax.shard_map(
        local, mesh=mesh, in_specs=placed, out_specs=P("fsdp", "ctx", None), check_vma=False
    )
```

```python
import functools
import math

import jax
import jax.numpy as jnp
from jax import lax
from jax.experimental import pallas as pl
from jax.experimental.pallas import tpu as pltpu
from jax.sharding import PartitionSpec as P

HQ = 8
HD = 128
REACH = 4
ROPE_BASE = 500000.0
MASKED = -1e30
NX, NC, NZ, NY = 4, 2, 16, 4
ALL = ("fsdp", "ctx")


def place(x, c, z, y):
    return (x * NC + c) * (NZ * NY) + z * NY + y


def route(move):
    return [
        (place(x, c, z, y), place(*move(x, c, z, y)))
        for x in range(NX)
        for c in range(NC)
        for z in range(NZ)
        for y in range(NY)
    ]


def hop(block, distance, x_core):
    def move(x, c, z, y):
        if c == x_core:
            return (x + distance) % NX, c, z, y
        return x, c, z, (y + distance) % NY

    return lax.ppermute(block, ALL, route(move))


def swap_cores(block):
    return lax.ppermute(block, ALL, route(lambda x, c, z, y: (x, 1 - c, z, y)))


BLOCK = NZ * NY * 8
SPAN = NZ * 8
VMEM_LIMIT = 14 * 1024 * 1024


def order_matrix(y_me):
    slot = lax.broadcasted_iota(jnp.int32, (BLOCK, BLOCK), 1)
    source = lax.broadcasted_iota(jnp.int32, (BLOCK, BLOCK), 0)
    step, inner = slot // SPAN, slot % SPAN
    wanted = inner // 8 * (NY * 8) + (y_me - step + NY) % NY * 8 + inner % 8
    return (source == wanted).astype(jnp.bfloat16)


def x_block(x_me, step):
    return pl.multiple_of((x_me - step + NX) % NX * BLOCK, BLOCK)


def arrange_body(at, order, features, theirs, out_ref):
    for s in range(NX):
        x_at = (at[0] - s + NX) % NX
        own = features[:, pl.ds(pl.multiple_of((x_at * NC + at[2]) * BLOCK, BLOCK), BLOCK)]
        other = theirs[:, pl.ds(pl.multiple_of(x_at * BLOCK, BLOCK), BLOCK)]
        both = jnp.concatenate([own, other], axis=0)
        rows = both.shape[0]
        got = jnp.dot(both, order[...], preferred_element_type=jnp.float32).astype(jnp.bfloat16)

        @pl.when(at[2] == 1)
        def _():
            out_ref[s * rows : (s + 1) * rows, :] = got

        @pl.when(at[2] == 0)
        def _():
            for e in range(NY):
                out_ref[e * rows : (e + 1) * rows, s * SPAN : (s + 1) * SPAN] = got[
                    :, e * SPAN : (e + 1) * SPAN
                ]


SCALARS = pl.BlockSpec(memory_space=pltpu.SMEM)
WHOLE = pl.BlockSpec(memory_space=pltpu.VMEM)
LEFT = pl.BlockSpec(memory_space=pltpu.HBM)


def call(body, in_specs, out_shape, flops, mib, **more):
    return pl.pallas_call(
        body,
        in_specs=in_specs,
        out_shape=out_shape,
        compiler_params=pltpu.CompilerParams(vmem_limit_bytes=VMEM_LIMIT),
        cost_estimate=pl.CostEstimate(flops=flops, bytes_accessed=mib << 20, transcendentals=0),
        **more,
    )


def arrange(at, order, features, theirs):
    rows = features.shape[0]
    return call(
        arrange_body,
        [SCALARS] + [WHOLE] * 3,
        pltpu.VMEM((NX * 2 * rows, BLOCK), jnp.bfloat16),
        NX * 4 * rows * BLOCK * BLOCK, 4,
    )(at, order, features, theirs)


def pick_body(at, features, theirs_ref):
    for x in range(NX):
        from_block = pl.ds(pl.multiple_of((x * NC + 1 - at[2]) * BLOCK, BLOCK), BLOCK)
        theirs_ref[:, x * BLOCK : (x + 1) * BLOCK] = features[:, from_block]


def pick(at, features):
    return call(
        pick_body,
        [SCALARS, WHOLE],
        jax.ShapeDtypeStruct((features.shape[0], NX * BLOCK), jnp.bfloat16),
        0, 2,
    )(at, features)


def stack_body(own, first, second, third, plane_ref):
    rows = own.shape[0]
    for i, piece in enumerate((own, first, second, third)):
        plane_ref[i * rows : (i + 1) * rows, :] = piece[...]


def stack_plane(pieces):
    rows, columns = pieces[0].shape
    return call(
        stack_body, [WHOLE] * 4, pltpu.VMEM((4 * rows, columns), jnp.bfloat16), 0, 3
    )(*[in_vmem(p) for p in pieces])


def in_hbm(array):
    return pltpu.with_memory_space_constraint(array, pltpu.HBM)


def in_vmem(array):
    return pltpu.with_memory_space_constraint(array, pltpu.VMEM)


def early_body(steps, arranged, *refs):
    pieces, (mine_ref, theirs_ref, rows_ref, sems) = refs[: len(steps)], refs[len(steps) :]
    count, stores, total = mine_ref.shape[0], [], 0.0
    for i, (step, piece) in enumerate(zip(steps, pieces)):
        store = pltpu.make_async_copy(
            piece, rows_ref.at[pl.ds(step * BLOCK, BLOCK)], sems.at[i]
        )
        store.start()
        stores.append(store)
    for step, piece in zip(steps, pieces):
        total += jnp.dot(
            arranged[step * 2 * count : (step + 1) * 2 * count, :], piece[...],
            preferred_element_type=jnp.float32,
        )
    mine_ref[...] = total[:count]
    theirs_ref[...] = total[count:]
    for store in stores:
        store.wait()


def early_sums(arranged, pieces, steps):
    count, columns = arranged.shape[0] // NX // 2, pieces[0].shape[1]
    return call(
        functools.partial(early_body, steps),
        [WHOLE] * (1 + len(pieces)),
        [
            pltpu.VMEM((count, columns), jnp.float32),
            pltpu.VMEM((count, columns), jnp.float32),
            jax.ShapeDtypeStruct((NX * BLOCK, columns), jnp.bfloat16),
        ],
        len(steps) * 4 * count * BLOCK * columns, len(steps) * 2,
        out_specs=[WHOLE, WHOLE, LEFT],
        scratch_shapes=[pltpu.SemaphoreType.DMA((len(pieces),))],
    )(in_vmem(arranged), *[in_vmem(p) for p in pieces])


def late_body(steps, arranged, mine, theirs, *refs):
    pieces, (mine_ref, theirs_ref) = refs[: len(steps)], refs[len(steps) :]
    count, more = mine.shape[0], 0.0
    for step, piece in zip(steps, pieces):
        more += jnp.dot(
            arranged[step * 2 * count : (step + 1) * 2 * count, :], piece[...],
            preferred_element_type=jnp.float32,
        )
    mine_ref[...] = mine[...] + more[:count]
    theirs_ref[...] = theirs[...] + more[count:]


def late_sums(arranged, sums, pieces, steps):
    count, columns = sums[0].shape
    return call(
        functools.partial(late_body, steps),
        [WHOLE] * (3 + len(pieces)),
        [pltpu.VMEM((count, columns), jnp.float32)] * 2,
        len(steps) * 4 * count * BLOCK * columns, 4,
    )(*[in_vmem(x) for x in (arranged, *sums, *pieces)])


def place_body(steps, first, second, after, rows_in, rows_ref, sems):
    stores = []
    for i, piece in enumerate((first, second)):
        to_rows = rows_ref.at[pl.ds(steps[i] * BLOCK, BLOCK)]
        stores.append(pltpu.make_async_copy(piece, to_rows, sems.at[i]))
        stores[-1].start()
    for store in stores:
        store.wait()


def place_rows(pieces, after, rows, steps):
    return call(
        functools.partial(place_body, steps),
        [WHOLE, WHOLE, pl.BlockSpec(memory_space=pl.ANY), LEFT],
        jax.ShapeDtypeStruct(rows.shape, rows.dtype),
        0, 4,
        out_specs=LEFT,
        scratch_shapes=[pltpu.SemaphoreType.DMA((2,))],
        input_output_aliases={3: 0},
    )(*[in_vmem(p) for p in pieces], after, rows)


TURN = (((1,), (1,)), ((), ()))


def by_source(pieces, parity, cut, join):
    for s in range(NX):
        turned = join([cut(piece, s) for piece in pieces])
        yield s, jnp.where(parity == 0, turned, pieces[s])


def query_part_body(flip, at, grads, all_rows, out_ref, weights, held, sems):
    parity = at[2] if flip == 0 else 1 - at[2]
    rows = grads.shape[0]
    loads = []
    for e in range(NX):
        source = all_rows.at[pl.ds(e * BLOCK, BLOCK), pl.ds(0, HQ * HD)]
        loads.append(pltpu.make_async_copy(source, weights.at[e], sems.at[e]))
        loads[-1].start()
    order = order_matrix(at[1])
    for e in range(NX):
        loads[e].wait()
        held[e] = lax.dot_general(
            grads[...], weights[e], TURN, preferred_element_type=jnp.float32
        )
    for s, part in by_source(
        [held[e] for e in range(NX)], parity,
        lambda piece, d: piece[:, d * SPAN : (d + 1) * SPAN],
        lambda parts: jnp.concatenate(parts, axis=1),
    ):
        high = part.astype(jnp.bfloat16)
        low = (part - high.astype(jnp.float32)).astype(jnp.bfloat16)
        back = lax.dot_general(
            jnp.concatenate([high, low], axis=0), order, TURN,
            preferred_element_type=jnp.float32,
        )
        out_ref[:, pl.ds(x_block(at[0], s), BLOCK)] = back[:rows] + back[rows:]


def query_part_of(at, grads, all_rows, flip):
    rows = grads.shape[0]
    return call(
        functools.partial(query_part_body, flip),
        [SCALARS, WHOLE, LEFT],
        pltpu.VMEM((rows, NX * BLOCK), jnp.float32),
        NX * 2 * rows * BLOCK * (HQ * HD + 2 * BLOCK), 6,
        scratch_shapes=[
            pltpu.VMEM((NX, BLOCK, HQ * HD), jnp.bfloat16),
            pltpu.VMEM((NX, rows, BLOCK), jnp.float32),
            pltpu.SemaphoreType.DMA((NX,)),
        ],
    )(at, grads, all_rows)


def pair_weights_body(at, all_rows, out_ref, weights, sem):
    load = pltpu.make_async_copy(all_rows.at[:, pl.ds(HQ * HD, 2 * HD)], weights, sem)
    load.start()
    order = order_matrix(at[1])
    load.wait()
    for s, part in by_source(
        [weights[e * BLOCK : (e + 1) * BLOCK, :] for e in range(NX)], at[2],
        lambda piece, d: piece[d * SPAN : (d + 1) * SPAN],
        lambda parts: jnp.concatenate(parts, axis=0),
    ):
        out_ref[pl.ds(x_block(at[0], s), BLOCK), :] = jnp.dot(
            order, part, preferred_element_type=jnp.float32
        ).astype(jnp.bfloat16)


def pair_weights_of(at, all_rows):
    return call(
        pair_weights_body,
        [SCALARS, LEFT],
        pltpu.HBM((NX * BLOCK, 2 * HD), jnp.bfloat16),
        NX * 2 * BLOCK * BLOCK * 2 * HD, 3,
        scratch_shapes=[
            pltpu.VMEM((NX * BLOCK, 2 * HD), jnp.bfloat16),
            pltpu.SemaphoreType.DMA,
        ],
    )(at, all_rows)


def finish_body(at, pair_out, own_part, other_part, own_w, other_w, out_ref):
    for x in range(NX):
        cut = slice(x * BLOCK, (x + 1) * BLOCK)
        for flip, part, w in ((0, own_part, own_w), (1, other_part, other_w)):
            parity = at[2] if flip == 0 else 1 - at[2]
            total = part[:, cut] + lax.dot_general(
                pair_out[...], w[cut, :], TURN, preferred_element_type=jnp.float32
            )
            to_block = pl.ds(pl.multiple_of((x * NC + parity) * BLOCK, BLOCK), BLOCK)
            out_ref[:, to_block] = total.astype(jnp.bfloat16)


def finish(at, pair_out, parts, weights):
    whole = pl.BlockSpec(memory_space=pltpu.VMEM)
    return pl.pallas_call(
        finish_body,
        in_specs=[pl.BlockSpec(memory_space=pltpu.SMEM)] + [whole] * 5,
        out_shape=jax.ShapeDtypeStruct((pair_out.shape[0], NX * NC * BLOCK), jnp.bfloat16),
        compiler_params=pltpu.CompilerParams(vmem_limit_bytes=VMEM_LIMIT),
    )(at, pair_out, *[in_vmem(p) for p in parts], in_vmem(weights[0]), weights[1])


def shifted(block, axis, distance):
    devices = range(lax.axis_size(axis))
    return lax.ppermute(block, axis, [(i - distance, i) for i in devices if i - distance in devices])


def angles_for(positions, head_size):
    half_size = head_size // 2
    inverse = jnp.power(
        jnp.float32(ROPE_BASE), -jnp.arange(half_size, dtype=jnp.float32) / half_size
    )
    phase_angle = positions.astype(jnp.float32)[:, None] * inverse[None, :]
    return (jnp.cos(phase_angle), jnp.sin(phase_angle))


def rotate(vectors, cos_part, sin_part):
    half_size = vectors.shape[-1] // 2
    a = vectors[..., :half_size]
    b = vectors[..., half_size:]
    return jnp.concatenate([a * cos_part - b * sin_part, b * cos_part + a * sin_part], axis=-1)


def local(tokens, doc_start, out_grad, w_qkv):
    row_count = tokens.shape[1]
    score_scale = 1.0 / math.sqrt(HD)
    features = tokens[0]
    begin_rows = doc_start[0]
    grad_rows = out_grad[0].reshape(row_count, HQ, HD)
    fsdp, ctx = lax.axis_index("fsdp"), lax.axis_index("ctx")
    x_me, core = fsdp // NC, fsdp % NC
    y_me = ctx % NY

    column = lax.all_gather(
        w_qkv, "ctx", axis=0, tiled=True,
        axis_index_groups=[[z * NY + y for z in range(NZ)] for y in range(NY)],
    )
    second, first, third = (hop(column, d, 0) for d in (2, 1, 3))

    at = jnp.stack([x_me, y_me, core]).astype(jnp.int32)
    order = order_matrix(y_me)
    plane, theirs = lax.optimization_barrier(
        (stack_plane([column, first, second, third]), pick(at, features))
    )
    two, one, three = (hop(plane, d, 1) for d in (2, 1, 3))
    arranged = arrange(at, order, features, swap_cores(theirs))
    *sums, own_w = early_sums(arranged, [plane, three], (0, 3))
    mine, theirs = late_sums(arranged, sums, [one, two], (1, 2))
    own_w = place_rows([one, two], theirs, own_w, (1, 2))
    projected = mine + swap_cores(theirs)
    pair_pre, query_pre = projected[:, HQ * HD :], projected[:, : HQ * HD]

    first_row = ctx * row_count
    query_index = first_row + jnp.arange(row_count, dtype=jnp.int32)
    cos_part, sin_part = angles_for(query_index - begin_rows, HD)
    pair_rows = jnp.concatenate(
        [rotate(pair_pre[:, :HD], cos_part, sin_part), pair_pre[:, HD:]], axis=1
    ).astype(jnp.bfloat16)
    later_at, pair_rows = lax.optimization_barrier((at, pair_rows))
    back2, pair_w_own = lax.optimization_barrier(
        (shifted(pair_rows, "ctx", 2), pair_weights_of(later_at, own_w))
    )
    back31 = shifted(jnp.concatenate([back2, pair_rows], axis=0), "ctx", 1)
    other_w = swap_cores(own_w)
    window = jnp.concatenate([back31[:row_count], back2, back31[row_count:], pair_rows], axis=0)

    queries = rotate(
        query_pre.reshape(row_count, HQ, HD), cos_part[:, None, :], sin_part[:, None, :]
    ).astype(jnp.bfloat16)
    keys, values = window[:, :HD], window[:, HD:]
    key_index = first_row - (REACH - 1) * row_count + jnp.arange(REACH * row_count, dtype=jnp.int32)
    allowed = (key_index[None, :] <= query_index[:, None]) & (
        key_index[None, :] >= begin_rows[:, None]
    )
    scores = (
        jnp.einsum("qhd,kd->hqk", queries, keys, preferred_element_type=jnp.float32) * score_scale
    )
    scores = jnp.where(allowed[None], scores, MASKED)
    top = jnp.max(scores, axis=-1, keepdims=True)
    unnormed = jnp.where(allowed[None], jnp.exp(scores - top), 0.0)
    probs = unnormed / jnp.sum(unnormed, axis=-1, keepdims=True)
    probs_low = probs.astype(jnp.bfloat16)
    grad_probs = jnp.einsum("qhd,kd->hqk", grad_rows, values, preferred_element_type=jnp.float32)
    attn_out = jnp.einsum(
        "hqk,kd->hqd", probs_low, values, preferred_element_type=jnp.float32
    ).astype(jnp.bfloat16)
    row_delta = jnp.sum(
        jnp.transpose(grad_rows, (1, 0, 2)).astype(jnp.float32) * attn_out.astype(jnp.float32),
        axis=-1, keepdims=True,
    )
    grad_value = jnp.einsum("hqk,qhd->kd", probs_low, grad_rows, preferred_element_type=jnp.float32)
    grad_scores = (probs * (grad_probs - row_delta)).astype(jnp.bfloat16)
    grad_query = (
        jnp.einsum("hqk,kd->qhd", grad_scores, keys, preferred_element_type=jnp.float32)
        * score_scale
    )
    grad_key = (
        jnp.einsum("hqk,qhd->kd", grad_scores, queries, preferred_element_type=jnp.float32)
        * score_scale
    )
    pair_grad = jnp.concatenate([grad_key, grad_value], axis=1)
    query_out = rotate(grad_query, cos_part[:, None, :], -sin_part[:, None, :]).reshape(
        row_count, HQ * HD
    ).astype(jnp.bfloat16)
    back3, back2, back1, own_grad = (
        pair_grad[i * row_count : (i + 1) * row_count] for i in range(REACH)
    )
    came, part_own = lax.optimization_barrier(
        (
            shifted(jnp.concatenate([back3, back1], axis=0).astype(jnp.bfloat16), "ctx", -1),
            query_part_of(at, query_out, own_w, 0),
        )
    )
    came = came.astype(jnp.float32)
    last, part_other, pair_w_other = lax.optimization_barrier(
        (
            shifted((back2 + came[:row_count]).astype(jnp.bfloat16), "ctx", -2),
            query_part_of(at, query_out, other_w, 1),
            swap_cores(pair_w_own),
        )
    )
    pair_total = own_grad + came[row_count:] + last.astype(jnp.float32)
    pair_out = jnp.concatenate(
        [rotate(pair_total[:, :HD], cos_part, -sin_part), pair_total[:, HD:]], axis=1
    ).astype(jnp.bfloat16)
    return finish(at, pair_out, [part_own, part_other], [pair_w_own, pair_w_other])[None]


def solution(mesh):
    placed = (
        P("fsdp", "ctx", None),
        P("fsdp", "ctx"),
        P("fsdp", "ctx", None),
        P(("fsdp", "ctx"), None),
    )
    return jax.shard_map(
        local, mesh=mesh, in_specs=placed, out_specs=P("fsdp", "ctx", None), check_vma=False
    )
```

```python
import functools
import math

import jax
import jax.numpy as jnp
from jax import lax
from jax.experimental import pallas as pl
from jax.experimental.pallas import tpu as pltpu
from jax.sharding import PartitionSpec as P

HQ = 8
HD = 128
REACH = 4
ROPE_BASE = 500000.0
MASKED = -1e30
NX, NC, NZ, NY = 4, 2, 16, 4
ALL = ("fsdp", "ctx")


def place(x, c, z, y):
    return (x * NC + c) * (NZ * NY) + z * NY + y


def route(move):
    return [
        (place(x, c, z, y), place(*move(x, c, z, y)))
        for x in range(NX)
        for c in range(NC)
        for z in range(NZ)
        for y in range(NY)
    ]


def hop(block, distance, x_core):
    def move(x, c, z, y):
        if c == x_core:
            return (x + distance) % NX, c, z, y
        return x, c, z, (y + distance) % NY

    return lax.ppermute(block, ALL, route(move))


def swap_cores(block):
    return lax.ppermute(block, ALL, route(lambda x, c, z, y: (x, 1 - c, z, y)))


BLOCK = NZ * NY * 8
SPAN = NZ * 8
VMEM_LIMIT = 14 * 1024 * 1024


def order_matrix(y_me):
    slot = lax.broadcasted_iota(jnp.int32, (BLOCK, BLOCK), 1)
    source = lax.broadcasted_iota(jnp.int32, (BLOCK, BLOCK), 0)
    step, inner = slot // SPAN, slot % SPAN
    wanted = inner // 8 * (NY * 8) + (y_me - step + NY) % NY * 8 + inner % 8
    return (source == wanted).astype(jnp.bfloat16)


def x_block(x_me, step):
    return pl.multiple_of((x_me - step + NX) % NX * BLOCK, BLOCK)


def arrange_body(at, order, features, theirs, out_ref):
    for s in range(NX):
        x_at = (at[0] - s + NX) % NX
        own = features[:, pl.ds(pl.multiple_of((x_at * NC + at[2]) * BLOCK, BLOCK), BLOCK)]
        other = theirs[:, pl.ds(pl.multiple_of(x_at * BLOCK, BLOCK), BLOCK)]
        both = jnp.concatenate([own, other], axis=0)
        rows = both.shape[0]
        got = jnp.dot(both, order[...], preferred_element_type=jnp.float32).astype(jnp.bfloat16)

        @pl.when(at[2] == 1)
        def _():
            out_ref[s * rows : (s + 1) * rows, :] = got

        @pl.when(at[2] == 0)
        def _():
            for e in range(NY):
                out_ref[e * rows : (e + 1) * rows, s * SPAN : (s + 1) * SPAN] = got[
                    :, e * SPAN : (e + 1) * SPAN
                ]


SCALARS = pl.BlockSpec(memory_space=pltpu.SMEM)
WHOLE = pl.BlockSpec(memory_space=pltpu.VMEM)
LEFT = pl.BlockSpec(memory_space=pltpu.HBM)


def call(body, in_specs, out_shape, flops, mib, **more):
    return pl.pallas_call(
        body,
        in_specs=in_specs,
        out_shape=out_shape,
        compiler_params=pltpu.CompilerParams(vmem_limit_bytes=VMEM_LIMIT),
        cost_estimate=pl.CostEstimate(flops=flops, bytes_accessed=mib << 20, transcendentals=0),
        **more,
    )


def arrange(at, order, features, theirs):
    rows = features.shape[0]
    return call(
        arrange_body,
        [SCALARS] + [WHOLE] * 3,
        pltpu.VMEM((NX * 2 * rows, BLOCK), jnp.bfloat16),
        NX * 4 * rows * BLOCK * BLOCK, 4,
    )(at, order, features, theirs)


def pick_body(at, features, theirs_ref):
    for x in range(NX):
        from_block = pl.ds(pl.multiple_of((x * NC + 1 - at[2]) * BLOCK, BLOCK), BLOCK)
        theirs_ref[:, x * BLOCK : (x + 1) * BLOCK] = features[:, from_block]


def pick(at, features):
    return call(
        pick_body,
        [SCALARS, WHOLE],
        jax.ShapeDtypeStruct((features.shape[0], NX * BLOCK), jnp.bfloat16),
        0, 2,
    )(at, features)


def stack_body(own, first, second, third, plane_ref):
    rows = own.shape[0]
    for i, piece in enumerate((own, first, second, third)):
        plane_ref[i * rows : (i + 1) * rows, :] = piece[...]


def stack_plane(pieces):
    rows, columns = pieces[0].shape
    return call(
        stack_body, [WHOLE] * 4, pltpu.VMEM((4 * rows, columns), jnp.bfloat16), 0, 3
    )(*[in_vmem(p) for p in pieces])


def in_hbm(array):
    return pltpu.with_memory_space_constraint(array, pltpu.HBM)


def in_vmem(array):
    return pltpu.with_memory_space_constraint(array, pltpu.VMEM)


def early_body(steps, arranged, *refs):
    pieces, (mine_ref, theirs_ref, rows_ref, sems) = refs[: len(steps)], refs[len(steps) :]
    count, stores, total = mine_ref.shape[0], [], 0.0
    for i, (step, piece) in enumerate(zip(steps, pieces)):
        store = pltpu.make_async_copy(
            piece, rows_ref.at[pl.ds(step * BLOCK, BLOCK)], sems.at[i]
        )
        store.start()
        stores.append(store)
    for step, piece in zip(steps, pieces):
        total += jnp.dot(
            arranged[step * 2 * count : (step + 1) * 2 * count, :], piece[...],
            preferred_element_type=jnp.float32,
        )
    mine_ref[...] = total[:count]
    theirs_ref[...] = total[count:]
    for store in stores:
        store.wait()


def early_sums(arranged, pieces, steps):
    count, columns = arranged.shape[0] // NX // 2, pieces[0].shape[1]
    return call(
        functools.partial(early_body, steps),
        [WHOLE] * (1 + len(pieces)),
        [
            pltpu.VMEM((count, columns), jnp.float32),
            pltpu.VMEM((count, columns), jnp.float32),
            jax.ShapeDtypeStruct((NX * BLOCK, columns), jnp.bfloat16),
        ],
        len(steps) * 4 * count * BLOCK * columns, len(steps) * 2,
        out_specs=[WHOLE, WHOLE, LEFT],
        scratch_shapes=[pltpu.SemaphoreType.DMA((len(pieces),))],
    )(in_vmem(arranged), *[in_vmem(p) for p in pieces])


def late_body(steps, arranged, mine, theirs, *refs):
    pieces, (rows_in, mine_ref, theirs_ref, rows_ref, sems) = refs[: len(steps)], refs[len(steps) :]
    count, stores, more = mine.shape[0], [], 0.0
    for i, (step, piece) in enumerate(zip(steps, pieces)):
        to_rows = rows_ref.at[pl.ds(step * BLOCK, BLOCK)]
        stores.append(pltpu.make_async_copy(piece, to_rows, sems.at[i]))
        stores[-1].start()
    for step, piece in zip(steps, pieces):
        more += jnp.dot(
            arranged[step * 2 * count : (step + 1) * 2 * count, :], piece[...],
            preferred_element_type=jnp.float32,
        )
    mine_ref[...] = mine[...] + more[:count]
    theirs_ref[...] = theirs[...] + more[count:]
    for store in stores:
        store.wait()


def late_sums(arranged, sums, pieces, rows, steps):
    count, columns = sums[0].shape
    operands = [in_vmem(x) for x in (arranged, *sums, *pieces)]
    return call(
        functools.partial(late_body, steps),
        [WHOLE] * len(operands) + [LEFT],
        [
            pltpu.VMEM((count, columns), jnp.float32),
            pltpu.VMEM((count, columns), jnp.float32),
            jax.ShapeDtypeStruct(rows.shape, rows.dtype),
        ],
        len(steps) * 4 * count * BLOCK * columns, 4,
        out_specs=[WHOLE, WHOLE, LEFT],
        scratch_shapes=[pltpu.SemaphoreType.DMA((len(pieces),))],
        input_output_aliases={len(operands): 2},
    )(*operands, rows)


TURN = (((1,), (1,)), ((), ()))


def by_source(pieces, parity, cut, join):
    for s in range(NX):
        turned = join([cut(piece, s) for piece in pieces])
        yield s, jnp.where(parity == 0, turned, pieces[s])


def query_part_body(flip, at, grads, all_rows, out_ref, weights, held, sems):
    parity = at[2] if flip == 0 else 1 - at[2]
    rows = grads.shape[0]
    loads = []
    for e in range(NX):
        source = all_rows.at[pl.ds(e * BLOCK, BLOCK), pl.ds(0, HQ * HD)]
        loads.append(pltpu.make_async_copy(source, weights.at[e], sems.at[e]))
        loads[-1].start()
    order = order_matrix(at[1])
    for e in range(NX):
        loads[e].wait()
        held[e] = lax.dot_general(
            grads[...], weights[e], TURN, preferred_element_type=jnp.float32
        )
    for s, part in by_source(
        [held[e] for e in range(NX)], parity,
        lambda piece, d: piece[:, d * SPAN : (d + 1) * SPAN],
        lambda parts: jnp.concatenate(parts, axis=1),
    ):
        high = part.astype(jnp.bfloat16)
        low = (part - high.astype(jnp.float32)).astype(jnp.bfloat16)
        back = lax.dot_general(
            jnp.concatenate([high, low], axis=0), order, TURN,
            preferred_element_type=jnp.float32,
        )
        out_ref[:, pl.ds(x_block(at[0], s), BLOCK)] = back[:rows] + back[rows:]


def query_part_of(at, grads, all_rows, flip):
    rows = grads.shape[0]
    return call(
        functools.partial(query_part_body, flip),
        [SCALARS, WHOLE, LEFT],
        pltpu.VMEM((rows, NX * BLOCK), jnp.float32),
        NX * 2 * rows * BLOCK * (HQ * HD + 2 * BLOCK), 6,
        scratch_shapes=[
            pltpu.VMEM((NX, BLOCK, HQ * HD), jnp.bfloat16),
            pltpu.VMEM((NX, rows, BLOCK), jnp.float32),
            pltpu.SemaphoreType.DMA((NX,)),
        ],
    )(at, grads, all_rows)


def pair_weights_body(at, all_rows, out_ref, weights, sem):
    load = pltpu.make_async_copy(all_rows.at[:, pl.ds(HQ * HD, 2 * HD)], weights, sem)
    load.start()
    order = order_matrix(at[1])
    load.wait()
    for s, part in by_source(
        [weights[e * BLOCK : (e + 1) * BLOCK, :] for e in range(NX)], at[2],
        lambda piece, d: piece[d * SPAN : (d + 1) * SPAN],
        lambda parts: jnp.concatenate(parts, axis=0),
    ):
        out_ref[pl.ds(x_block(at[0], s), BLOCK), :] = jnp.dot(
            order, part, preferred_element_type=jnp.float32
        ).astype(jnp.bfloat16)


def pair_weights_of(at, all_rows):
    return call(
        pair_weights_body,
        [SCALARS, LEFT],
        pltpu.HBM((NX * BLOCK, 2 * HD), jnp.bfloat16),
        NX * 2 * BLOCK * BLOCK * 2 * HD, 3,
        scratch_shapes=[
            pltpu.VMEM((NX * BLOCK, 2 * HD), jnp.bfloat16),
            pltpu.SemaphoreType.DMA,
        ],
    )(at, all_rows)


def finish_body(at, pair_out, own_part, other_part, own_w, other_w, out_ref):
    for x in range(NX):
        cut = slice(x * BLOCK, (x + 1) * BLOCK)
        for flip, part, w in ((0, own_part, own_w), (1, other_part, other_w)):
            parity = at[2] if flip == 0 else 1 - at[2]
            total = part[:, cut] + lax.dot_general(
                pair_out[...], w[cut, :], TURN, preferred_element_type=jnp.float32
            )
            to_block = pl.ds(pl.multiple_of((x * NC + parity) * BLOCK, BLOCK), BLOCK)
            out_ref[:, to_block] = total.astype(jnp.bfloat16)


def finish(at, pair_out, parts, weights):
    whole = pl.BlockSpec(memory_space=pltpu.VMEM)
    return pl.pallas_call(
        finish_body,
        in_specs=[pl.BlockSpec(memory_space=pltpu.SMEM)] + [whole] * 5,
        out_shape=jax.ShapeDtypeStruct((pair_out.shape[0], NX * NC * BLOCK), jnp.bfloat16),
        compiler_params=pltpu.CompilerParams(vmem_limit_bytes=VMEM_LIMIT),
    )(at, pair_out, *[in_vmem(p) for p in parts], in_vmem(weights[0]), in_hbm(weights[1]))


def shifted(block, axis, distance):
    devices = range(lax.axis_size(axis))
    return lax.ppermute(block, axis, [(i - distance, i) for i in devices if i - distance in devices])


def angles_for(positions, head_size):
    half_size = head_size // 2
    inverse = jnp.power(
        jnp.float32(ROPE_BASE), -jnp.arange(half_size, dtype=jnp.float32) / half_size
    )
    phase_angle = positions.astype(jnp.float32)[:, None] * inverse[None, :]
    return (jnp.cos(phase_angle), jnp.sin(phase_angle))


def rotate(vectors, cos_part, sin_part):
    half_size = vectors.shape[-1] // 2
    a = vectors[..., :half_size]
    b = vectors[..., half_size:]
    return jnp.concatenate([a * cos_part - b * sin_part, b * cos_part + a * sin_part], axis=-1)


def local(tokens, doc_start, out_grad, w_qkv):
    row_count = tokens.shape[1]
    score_scale = 1.0 / math.sqrt(HD)
    features = tokens[0]
    begin_rows = doc_start[0]
    grad_rows = out_grad[0].reshape(row_count, HQ, HD)
    fsdp, ctx = lax.axis_index("fsdp"), lax.axis_index("ctx")
    x_me, core = fsdp // NC, fsdp % NC
    y_me = ctx % NY

    column = lax.all_gather(
        w_qkv, "ctx", axis=0, tiled=True,
        axis_index_groups=[[z * NY + y for z in range(NZ)] for y in range(NY)],
    )
    second, first, third = (hop(column, d, 0) for d in (2, 1, 3))

    at = jnp.stack([x_me, y_me, core]).astype(jnp.int32)
    order = order_matrix(y_me)
    plane, theirs = lax.optimization_barrier(
        (stack_plane([column, first, second, third]), pick(at, features))
    )
    two, one, three = (hop(plane, d, 1) for d in (2, 1, 3))
    arranged = arrange(at, order, features, swap_cores(theirs))
    *sums, own_w = early_sums(arranged, [plane, three], (0, 3))
    mine, theirs, own_w = late_sums(arranged, sums, [one, two], own_w, (1, 2))
    projected = mine + swap_cores(theirs)
    pair_pre, query_pre = projected[:, HQ * HD :], projected[:, : HQ * HD]

    first_row = ctx * row_count
    query_index = first_row + jnp.arange(row_count, dtype=jnp.int32)
    cos_part, sin_part = angles_for(query_index - begin_rows, HD)
    pair_rows = jnp.concatenate(
        [rotate(pair_pre[:, :HD], cos_part, sin_part), pair_pre[:, HD:]], axis=1
    ).astype(jnp.bfloat16)
    later_at, pair_rows = lax.optimization_barrier((at, pair_rows))
    back2, pair_w_own = lax.optimization_barrier(
        (shifted(pair_rows, "ctx", 2), pair_weights_of(later_at, own_w))
    )
    back31 = shifted(jnp.concatenate([back2, pair_rows], axis=0), "ctx", 1)
    other_w = swap_cores(own_w)
    window = jnp.concatenate([back31[:row_count], back2, back31[row_count:], pair_rows], axis=0)

    queries = rotate(
        query_pre.reshape(row_count, HQ, HD), cos_part[:, None, :], sin_part[:, None, :]
    ).astype(jnp.bfloat16)
    keys, values = window[:, :HD], window[:, HD:]
    key_index = first_row - (REACH - 1) * row_count + jnp.arange(REACH * row_count, dtype=jnp.int32)
    allowed = (key_index[None, :] <= query_index[:, None]) & (
        key_index[None, :] >= begin_rows[:, None]
    )
    scores = (
        jnp.einsum("qhd,kd->hqk", queries, keys, preferred_element_type=jnp.float32) * score_scale
    )
    scores = jnp.where(allowed[None], scores, MASKED)
    top = jnp.max(scores, axis=-1, keepdims=True)
    unnormed = jnp.where(allowed[None], jnp.exp(scores - top), 0.0)
    probs = unnormed / jnp.sum(unnormed, axis=-1, keepdims=True)
    probs_low = probs.astype(jnp.bfloat16)
    grad_probs = jnp.einsum("qhd,kd->hqk", grad_rows, values, preferred_element_type=jnp.float32)
    attn_out = jnp.einsum(
        "hqk,kd->hqd", probs_low, values, preferred_element_type=jnp.float32
    ).astype(jnp.bfloat16)
    row_delta = jnp.sum(
        jnp.transpose(grad_rows, (1, 0, 2)).astype(jnp.float32) * attn_out.astype(jnp.float32),
        axis=-1, keepdims=True,
    )
    grad_value = jnp.einsum("hqk,qhd->kd", probs_low, grad_rows, preferred_element_type=jnp.float32)
    grad_scores = (probs * (grad_probs - row_delta)).astype(jnp.bfloat16)
    grad_query = (
        jnp.einsum("hqk,kd->qhd", grad_scores, keys, preferred_element_type=jnp.float32)
        * score_scale
    )
    grad_key = (
        jnp.einsum("hqk,qhd->kd", grad_scores, queries, preferred_element_type=jnp.float32)
        * score_scale
    )
    pair_grad = jnp.concatenate([grad_key, grad_value], axis=1)
    query_out = rotate(grad_query, cos_part[:, None, :], -sin_part[:, None, :]).reshape(
        row_count, HQ * HD
    ).astype(jnp.bfloat16)
    back3, back2, back1, own_grad = (
        pair_grad[i * row_count : (i + 1) * row_count] for i in range(REACH)
    )
    came, part_own = lax.optimization_barrier(
        (
            shifted(jnp.concatenate([back3, back1], axis=0).astype(jnp.bfloat16), "ctx", -1),
            query_part_of(at, query_out, own_w, 0),
        )
    )
    came = came.astype(jnp.float32)
    last, part_other, pair_w_other = lax.optimization_barrier(
        (
            shifted((back2 + came[:row_count]).astype(jnp.bfloat16), "ctx", -2),
            query_part_of(at, query_out, other_w, 1),
            swap_cores(pair_w_own),
        )
    )
    pair_total = own_grad + came[row_count:] + last.astype(jnp.float32)
    pair_out = jnp.concatenate(
        [rotate(pair_total[:, :HD], cos_part, -sin_part), pair_total[:, HD:]], axis=1
    ).astype(jnp.bfloat16)
    return finish(at, pair_out, [part_own, part_other], [pair_w_own, pair_w_other])[None]


def solution(mesh):
    placed = (
        P("fsdp", "ctx", None),
        P("fsdp", "ctx"),
        P("fsdp", "ctx", None),
        P(("fsdp", "ctx"), None),
    )
    return jax.shard_map(
        local, mesh=mesh, in_specs=placed, out_specs=P("fsdp", "ctx", None), check_vma=False
    )
```

```python
import functools
import math

import jax
import jax.numpy as jnp
from jax import lax
from jax.experimental import pallas as pl
from jax.experimental.pallas import tpu as pltpu
from jax.sharding import PartitionSpec as P

HQ = 8
HD = 128
REACH = 4
ROPE_BASE = 500000.0
MASKED = -1e30
NX, NC, NZ, NY = 4, 2, 16, 4
ALL = ("fsdp", "ctx")


def place(x, c, z, y):
    return (x * NC + c) * (NZ * NY) + z * NY + y


def route(move):
    return [
        (place(x, c, z, y), place(*move(x, c, z, y)))
        for x in range(NX)
        for c in range(NC)
        for z in range(NZ)
        for y in range(NY)
    ]


def hop(block, distance, x_core):
    def move(x, c, z, y):
        if c == x_core:
            return (x + distance) % NX, c, z, y
        return x, c, z, (y + distance) % NY

    return lax.ppermute(block, ALL, route(move))


def swap_cores(block):
    return lax.ppermute(block, ALL, route(lambda x, c, z, y: (x, 1 - c, z, y)))


BLOCK = NZ * NY * 8
SPAN = NZ * 8
VMEM_LIMIT = 14 * 1024 * 1024


def order_matrix(y_me):
    slot = lax.broadcasted_iota(jnp.int32, (BLOCK, BLOCK), 1)
    source = lax.broadcasted_iota(jnp.int32, (BLOCK, BLOCK), 0)
    step, inner = slot // SPAN, slot % SPAN
    wanted = inner // 8 * (NY * 8) + (y_me - step + NY) % NY * 8 + inner % 8
    return (source == wanted).astype(jnp.bfloat16)


def x_block(x_me, step):
    return pl.multiple_of((x_me - step + NX) % NX * BLOCK, BLOCK)


def arrange_body(at, order, features, theirs, out_ref):
    for s in range(NX):
        x_at = (at[0] - s + NX) % NX
        own = features[:, pl.ds(pl.multiple_of((x_at * NC + at[2]) * BLOCK, BLOCK), BLOCK)]
        other = theirs[:, pl.ds(pl.multiple_of(x_at * BLOCK, BLOCK), BLOCK)]
        both = jnp.concatenate([own, other], axis=0)
        rows = both.shape[0]
        got = jnp.dot(both, order[...], preferred_element_type=jnp.float32).astype(jnp.bfloat16)

        @pl.when(at[2] == 1)
        def _():
            out_ref[s * rows : (s + 1) * rows, :] = got

        @pl.when(at[2] == 0)
        def _():
            for e in range(NY):
                out_ref[e * rows : (e + 1) * rows, s * SPAN : (s + 1) * SPAN] = got[
                    :, e * SPAN : (e + 1) * SPAN
                ]


SCALARS = pl.BlockSpec(memory_space=pltpu.SMEM)
WHOLE = pl.BlockSpec(memory_space=pltpu.VMEM)
LEFT = pl.BlockSpec(memory_space=pltpu.HBM)


def call(body, in_specs, out_shape, flops, mib, **more):
    return pl.pallas_call(
        body,
        in_specs=in_specs,
        out_shape=out_shape,
        compiler_params=pltpu.CompilerParams(vmem_limit_bytes=VMEM_LIMIT),
        cost_estimate=pl.CostEstimate(flops=flops, bytes_accessed=mib << 20, transcendentals=0),
        **more,
    )


def arrange(at, order, features, theirs):
    rows = features.shape[0]
    return call(
        arrange_body,
        [SCALARS] + [WHOLE] * 3,
        pltpu.VMEM((NX * 2 * rows, BLOCK), jnp.bfloat16),
        NX * 4 * rows * BLOCK * BLOCK, 4,
    )(at, order, features, theirs)


def pick_body(at, features, theirs_ref, sems):
    copies = []
    for x in range(NX):
        from_block = pl.ds(pl.multiple_of((x * NC + 1 - at[2]) * BLOCK, BLOCK), BLOCK)
        copies.append(
            pltpu.make_async_copy(
                features.at[:, from_block], theirs_ref.at[:, pl.ds(x * BLOCK, BLOCK)], sems.at[x]
            )
        )
        copies[-1].start()
    for copy in copies:
        copy.wait()


def pick(at, features):
    return call(
        pick_body,
        [SCALARS, LEFT],
        pltpu.HBM((features.shape[0], NX * BLOCK), jnp.bfloat16),
        0, 2,
        out_specs=LEFT,
        scratch_shapes=[pltpu.SemaphoreType.DMA((NX,))],
    )(at, in_hbm(features))


def stack_body(own, first, second, third, plane_ref):
    rows = own.shape[0]
    for i, piece in enumerate((own, first, second, third)):
        plane_ref[i * rows : (i + 1) * rows, :] = piece[...]


def stack_plane(pieces):
    rows, columns = pieces[0].shape
    return call(
        stack_body, [WHOLE] * 4, pltpu.VMEM((4 * rows, columns), jnp.bfloat16), 0, 3
    )(*[in_vmem(p) for p in pieces[:3]], in_hbm(pieces[3]))


def in_hbm(array):
    return pltpu.with_memory_space_constraint(array, pltpu.HBM)


def in_vmem(array):
    return pltpu.with_memory_space_constraint(array, pltpu.VMEM)


def early_body(steps, arranged, *refs):
    pieces, (mine_ref, theirs_ref, rows_ref, sems) = refs[: len(steps)], refs[len(steps) :]
    count, stores, total = mine_ref.shape[0], [], 0.0
    for i, (step, piece) in enumerate(zip(steps, pieces)):
        store = pltpu.make_async_copy(
            piece, rows_ref.at[pl.ds(step * BLOCK, BLOCK)], sems.at[i]
        )
        store.start()
        stores.append(store)
    for step, piece in zip(steps, pieces):
        total += jnp.dot(
            arranged[step * 2 * count : (step + 1) * 2 * count, :], piece[...],
            preferred_element_type=jnp.float32,
        )
    mine_ref[...] = total[:count]
    theirs_ref[...] = total[count:]
    for store in stores:
        store.wait()


def early_sums(arranged, pieces, steps):
    count, columns = arranged.shape[0] // NX // 2, pieces[0].shape[1]
    return call(
        functools.partial(early_body, steps),
        [WHOLE] * (1 + len(pieces)),
        [
            pltpu.VMEM((count, columns), jnp.float32),
            pltpu.VMEM((count, columns), jnp.float32),
            jax.ShapeDtypeStruct((NX * BLOCK, columns), jnp.bfloat16),
        ],
        len(steps) * 4 * count * BLOCK * columns, len(steps) * 2,
        out_specs=[WHOLE, WHOLE, LEFT],
        scratch_shapes=[pltpu.SemaphoreType.DMA((len(pieces),))],
    )(in_vmem(arranged), *[in_vmem(p) for p in pieces])


def late_body(steps, arranged, mine, theirs, *refs):
    pieces, (rows_in, mine_ref, theirs_ref, rows_ref, sems) = refs[: len(steps)], refs[len(steps) :]
    count, stores, more = mine.shape[0], [], 0.0
    for i, (step, piece) in enumerate(zip(steps, pieces)):
        to_rows = rows_ref.at[pl.ds(step * BLOCK, BLOCK)]
        stores.append(pltpu.make_async_copy(piece, to_rows, sems.at[i]))
        stores[-1].start()
    for step, piece in zip(steps, pieces):
        more += jnp.dot(
            arranged[step * 2 * count : (step + 1) * 2 * count, :], piece[...],
            preferred_element_type=jnp.float32,
        )
    mine_ref[...] = mine[...] + more[:count]
    theirs_ref[...] = theirs[...] + more[count:]
    for store in stores:
        store.wait()


def late_sums(arranged, sums, pieces, rows, steps):
    count, columns = sums[0].shape
    operands = [in_vmem(x) for x in (arranged, *sums, *pieces)]
    return call(
        functools.partial(late_body, steps),
        [WHOLE] * len(operands) + [LEFT],
        [
            pltpu.VMEM((count, columns), jnp.float32),
            pltpu.VMEM((count, columns), jnp.float32),
            jax.ShapeDtypeStruct(rows.shape, rows.dtype),
        ],
        len(steps) * 4 * count * BLOCK * columns, 4,
        out_specs=[WHOLE, WHOLE, LEFT],
        scratch_shapes=[pltpu.SemaphoreType.DMA((len(pieces),))],
        input_output_aliases={len(operands): 2},
    )(*operands, rows)


TURN = (((1,), (1,)), ((), ()))


def by_source(pieces, parity, cut, join):
    for s in range(NX):
        turned = join([cut(piece, s) for piece in pieces])
        yield s, jnp.where(parity == 0, turned, pieces[s])


def query_part_body(flip, at, grads, all_rows, out_ref, weights, held, sems):
    parity = at[2] if flip == 0 else 1 - at[2]
    rows = grads.shape[0]
    loads = []
    for e in range(NX):
        source = all_rows.at[pl.ds(e * BLOCK, BLOCK), pl.ds(0, HQ * HD)]
        loads.append(pltpu.make_async_copy(source, weights.at[e], sems.at[e]))
        loads[-1].start()
    order = order_matrix(at[1])
    for e in range(NX):
        loads[e].wait()
        held[e] = lax.dot_general(
            grads[...], weights[e], TURN, preferred_element_type=jnp.float32
        )
    for s, part in by_source(
        [held[e] for e in range(NX)], parity,
        lambda piece, d: piece[:, d * SPAN : (d + 1) * SPAN],
        lambda parts: jnp.concatenate(parts, axis=1),
    ):
        high = part.astype(jnp.bfloat16)
        low = (part - high.astype(jnp.float32)).astype(jnp.bfloat16)
        back = lax.dot_general(
            jnp.concatenate([high, low], axis=0), order, TURN,
            preferred_element_type=jnp.float32,
        )
        out_ref[:, pl.ds(x_block(at[0], s), BLOCK)] = back[:rows] + back[rows:]


def query_part_of(at, grads, all_rows, flip):
    rows = grads.shape[0]
    return call(
        functools.partial(query_part_body, flip),
        [SCALARS, WHOLE, LEFT],
        pltpu.VMEM((rows, NX * BLOCK), jnp.float32),
        NX * 2 * rows * BLOCK * (HQ * HD + 2 * BLOCK), 6,
        scratch_shapes=[
            pltpu.VMEM((NX, BLOCK, HQ * HD), jnp.bfloat16),
            pltpu.VMEM((NX, rows, BLOCK), jnp.float32),
            pltpu.SemaphoreType.DMA((NX,)),
        ],
    )(at, grads, all_rows)


def pair_weights_body(at, all_rows, out_ref, weights, sem):
    load = pltpu.make_async_copy(all_rows.at[:, pl.ds(HQ * HD, 2 * HD)], weights, sem)
    load.start()
    order = order_matrix(at[1])
    load.wait()
    for s, part in by_source(
        [weights[e * BLOCK : (e + 1) * BLOCK, :] for e in range(NX)], at[2],
        lambda piece, d: piece[d * SPAN : (d + 1) * SPAN],
        lambda parts: jnp.concatenate(parts, axis=0),
    ):
        out_ref[pl.ds(x_block(at[0], s), BLOCK), :] = jnp.dot(
            order, part, preferred_element_type=jnp.float32
        ).astype(jnp.bfloat16)


def pair_weights_of(at, all_rows):
    return call(
        pair_weights_body,
        [SCALARS, LEFT],
        pltpu.HBM((NX * BLOCK, 2 * HD), jnp.bfloat16),
        NX * 2 * BLOCK * BLOCK * 2 * HD, 3,
        scratch_shapes=[
            pltpu.VMEM((NX * BLOCK, 2 * HD), jnp.bfloat16),
            pltpu.SemaphoreType.DMA,
        ],
    )(at, all_rows)


def finish_body(at, pair_out, own_part, other_part, own_w, other_w, out_ref):
    for x in range(NX):
        cut = slice(x * BLOCK, (x + 1) * BLOCK)
        for flip, part, w in ((0, own_part, own_w), (1, other_part, other_w)):
            parity = at[2] if flip == 0 else 1 - at[2]
            total = part[:, cut] + lax.dot_general(
                pair_out[...], w[cut, :], TURN, preferred_element_type=jnp.float32
            )
            to_block = pl.ds(pl.multiple_of((x * NC + parity) * BLOCK, BLOCK), BLOCK)
            out_ref[:, to_block] = total.astype(jnp.bfloat16)


def finish(at, pair_out, parts, weights):
    whole = pl.BlockSpec(memory_space=pltpu.VMEM)
    return pl.pallas_call(
        finish_body,
        in_specs=[pl.BlockSpec(memory_space=pltpu.SMEM)] + [whole] * 5,
        out_shape=jax.ShapeDtypeStruct((pair_out.shape[0], NX * NC * BLOCK), jnp.bfloat16),
        compiler_params=pltpu.CompilerParams(vmem_limit_bytes=VMEM_LIMIT),
    )(at, pair_out, *[in_vmem(p) for p in parts], in_vmem(weights[0]), in_hbm(weights[1]))


def shifted(block, axis, distance):
    devices = range(lax.axis_size(axis))
    return lax.ppermute(block, axis, [(i - distance, i) for i in devices if i - distance in devices])


def angles_for(positions, head_size):
    half_size = head_size // 2
    inverse = jnp.power(
        jnp.float32(ROPE_BASE), -jnp.arange(half_size, dtype=jnp.float32) / half_size
    )
    phase_angle = positions.astype(jnp.float32)[:, None] * inverse[None, :]
    return (jnp.cos(phase_angle), jnp.sin(phase_angle))


def rotate(vectors, cos_part, sin_part):
    half_size = vectors.shape[-1] // 2
    a = vectors[..., :half_size]
    b = vectors[..., half_size:]
    return jnp.concatenate([a * cos_part - b * sin_part, b * cos_part + a * sin_part], axis=-1)


def local(tokens, doc_start, out_grad, w_qkv):
    row_count = tokens.shape[1]
    score_scale = 1.0 / math.sqrt(HD)
    features = tokens[0]
    begin_rows = doc_start[0]
    grad_rows = out_grad[0].reshape(row_count, HQ, HD)
    fsdp, ctx = lax.axis_index("fsdp"), lax.axis_index("ctx")
    x_me, core = fsdp // NC, fsdp % NC
    y_me = ctx % NY

    column = lax.all_gather(
        w_qkv, "ctx", axis=0, tiled=True,
        axis_index_groups=[[z * NY + y for z in range(NZ)] for y in range(NY)],
    )
    third, first, second = (hop(column, d, 0) for d in (3, 1, 2))

    at = jnp.stack([x_me, y_me, core]).astype(jnp.int32)
    order = order_matrix(y_me)
    plane, theirs = lax.optimization_barrier(
        (stack_plane([column, first, second, third]), pick(at, features))
    )
    three, one, two = (hop(plane, d, 1) for d in (3, 1, 2))
    arranged = arrange(at, order, features, swap_cores(theirs))
    *sums, own_w = early_sums(arranged, [plane, two], (0, 2))
    mine, theirs, own_w = late_sums(arranged, sums, [one, three], own_w, (1, 3))
    projected = mine + swap_cores(theirs)
    pair_pre, query_pre = projected[:, HQ * HD :], projected[:, : HQ * HD]

    first_row = ctx * row_count
    query_index = first_row + jnp.arange(row_count, dtype=jnp.int32)
    cos_part, sin_part = angles_for(query_index - begin_rows, HD)
    pair_rows = jnp.concatenate(
        [rotate(pair_pre[:, :HD], cos_part, sin_part), pair_pre[:, HD:]], axis=1
    ).astype(jnp.bfloat16)
    later_at, pair_rows = lax.optimization_barrier((at, pair_rows))
    back2, pair_w_own = lax.optimization_barrier(
        (shifted(pair_rows, "ctx", 2), pair_weights_of(later_at, own_w))
    )
    back31 = shifted(jnp.concatenate([back2, pair_rows], axis=0), "ctx", 1)
    other_w = swap_cores(own_w)
    window = jnp.concatenate([back31[:row_count], back2, back31[row_count:], pair_rows], axis=0)

    queries = rotate(
        query_pre.reshape(row_count, HQ, HD), cos_part[:, None, :], sin_part[:, None, :]
    ).astype(jnp.bfloat16)
    keys, values = window[:, :HD], window[:, HD:]
    key_index = first_row - (REACH - 1) * row_count + jnp.arange(REACH * row_count, dtype=jnp.int32)
    allowed = (key_index[None, :] <= query_index[:, None]) & (
        key_index[None, :] >= begin_rows[:, None]
    )
    scores = (
        jnp.einsum("qhd,kd->hqk", queries, keys, preferred_element_type=jnp.float32) * score_scale
    )
    scores = jnp.where(allowed[None], scores, MASKED)
    top = jnp.max(scores, axis=-1, keepdims=True)
    unnormed = jnp.where(allowed[None], jnp.exp(scores - top), 0.0)
    probs = unnormed / jnp.sum(unnormed, axis=-1, keepdims=True)
    probs_low = probs.astype(jnp.bfloat16)
    grad_probs = jnp.einsum("qhd,kd->hqk", grad_rows, values, preferred_element_type=jnp.float32)
    attn_out = jnp.einsum(
        "hqk,kd->hqd", probs_low, values, preferred_element_type=jnp.float32
    ).astype(jnp.bfloat16)
    row_delta = jnp.sum(
        jnp.transpose(grad_rows, (1, 0, 2)).astype(jnp.float32) * attn_out.astype(jnp.float32),
        axis=-1, keepdims=True,
    )
    grad_value = jnp.einsum("hqk,qhd->kd", probs_low, grad_rows, preferred_element_type=jnp.float32)
    grad_scores = (probs * (grad_probs - row_delta)).astype(jnp.bfloat16)
    grad_query = (
        jnp.einsum("hqk,kd->qhd", grad_scores, keys, preferred_element_type=jnp.float32)
        * score_scale
    )
    grad_key = (
        jnp.einsum("hqk,qhd->kd", grad_scores, queries, preferred_element_type=jnp.float32)
        * score_scale
    )
    pair_grad = jnp.concatenate([grad_key, grad_value], axis=1)
    query_out = rotate(grad_query, cos_part[:, None, :], -sin_part[:, None, :]).reshape(
        row_count, HQ * HD
    ).astype(jnp.bfloat16)
    back3, back2, back1, own_grad = (
        pair_grad[i * row_count : (i + 1) * row_count] for i in range(REACH)
    )
    came, part_own = lax.optimization_barrier(
        (
            shifted(jnp.concatenate([back3, back1], axis=0).astype(jnp.bfloat16), "ctx", -1),
            query_part_of(at, query_out, own_w, 0),
        )
    )
    came = came.astype(jnp.float32)
    last, part_other, pair_w_other = lax.optimization_barrier(
        (
            shifted((back2 + came[:row_count]).astype(jnp.bfloat16), "ctx", -2),
            query_part_of(at, query_out, other_w, 1),
            swap_cores(pair_w_own),
        )
    )
    pair_total = own_grad + came[row_count:] + last.astype(jnp.float32)
    pair_out = jnp.concatenate(
        [rotate(pair_total[:, :HD], cos_part, -sin_part), pair_total[:, HD:]], axis=1
    ).astype(jnp.bfloat16)
    return finish(at, pair_out, [part_own, part_other], [pair_w_own, pair_w_other])[None]


def solution(mesh):
    placed = (
        P("fsdp", "ctx", None),
        P("fsdp", "ctx"),
        P("fsdp", "ctx", None),
        P(("fsdp", "ctx"), None),
    )
    return jax.shard_map(
        local, mesh=mesh, in_specs=placed, out_specs=P("fsdp", "ctx", None), check_vma=False
    )
```

```python
import functools
import math

import jax
import jax.numpy as jnp
from jax import lax
from jax.experimental import pallas as pl
from jax.experimental.pallas import tpu as pltpu
from jax.sharding import PartitionSpec as P

HQ = 8
HD = 128
REACH = 4
ROPE_BASE = 500000.0
MASKED = -1e30
NX, NC, NZ, NY = 4, 2, 16, 4
ALL = ("fsdp", "ctx")


def place(x, c, z, y):
    return (x * NC + c) * (NZ * NY) + z * NY + y


def route(move):
    return [
        (place(x, c, z, y), place(*move(x, c, z, y)))
        for x in range(NX)
        for c in range(NC)
        for z in range(NZ)
        for y in range(NY)
    ]


def hop(block, distance, x_core):
    def move(x, c, z, y):
        if c == x_core:
            return (x + distance) % NX, c, z, y
        return x, c, z, (y + distance) % NY

    return lax.ppermute(block, ALL, route(move))


def swap_cores(block):
    return lax.ppermute(block, ALL, route(lambda x, c, z, y: (x, 1 - c, z, y)))


BLOCK = NZ * NY * 8
SPAN = NZ * 8
VMEM_LIMIT = 14 * 1024 * 1024


def order_matrix(y_me):
    slot = lax.broadcasted_iota(jnp.int32, (BLOCK, BLOCK), 1)
    source = lax.broadcasted_iota(jnp.int32, (BLOCK, BLOCK), 0)
    step, inner = slot // SPAN, slot % SPAN
    wanted = inner // 8 * (NY * 8) + (y_me - step + NY) % NY * 8 + inner % 8
    return (source == wanted).astype(jnp.bfloat16)


def x_block(x_me, step):
    return pl.multiple_of((x_me - step + NX) % NX * BLOCK, BLOCK)


def arrange_body(at, order, features, theirs, out_ref):
    for s in range(NX):
        x_at = (at[0] - s + NX) % NX
        own = features[:, pl.ds(pl.multiple_of((x_at * NC + at[2]) * BLOCK, BLOCK), BLOCK)]
        other = theirs[:, pl.ds(pl.multiple_of(x_at * BLOCK, BLOCK), BLOCK)]
        both = jnp.concatenate([own, other], axis=0)
        rows = both.shape[0]
        got = jnp.dot(both, order[...], preferred_element_type=jnp.float32).astype(jnp.bfloat16)

        @pl.when(at[2] == 1)
        def _():
            out_ref[s * rows : (s + 1) * rows, :] = got

        @pl.when(at[2] == 0)
        def _():
            for e in range(NY):
                out_ref[e * rows : (e + 1) * rows, s * SPAN : (s + 1) * SPAN] = got[
                    :, e * SPAN : (e + 1) * SPAN
                ]


SCALARS = pl.BlockSpec(memory_space=pltpu.SMEM)
WHOLE = pl.BlockSpec(memory_space=pltpu.VMEM)
LEFT = pl.BlockSpec(memory_space=pltpu.HBM)


def call(body, in_specs, out_shape, flops, mib, **more):
    return pl.pallas_call(
        body,
        in_specs=in_specs,
        out_shape=out_shape,
        compiler_params=pltpu.CompilerParams(vmem_limit_bytes=VMEM_LIMIT),
        cost_estimate=pl.CostEstimate(flops=flops, bytes_accessed=mib << 20, transcendentals=0),
        **more,
    )


def arrange(at, order, features, theirs):
    rows = features.shape[0]
    return call(
        arrange_body,
        [SCALARS] + [WHOLE] * 3,
        pltpu.VMEM((NX * 2 * rows, BLOCK), jnp.bfloat16),
        NX * 4 * rows * BLOCK * BLOCK, 4,
    )(at, order, features, theirs)


def pick_body(at, features, theirs_ref):
    for x in range(NX):
        from_block = pl.ds(pl.multiple_of((x * NC + 1 - at[2]) * BLOCK, BLOCK), BLOCK)
        theirs_ref[:, x * BLOCK : (x + 1) * BLOCK] = features[:, from_block]


def pick(at, features):
    return call(
        pick_body,
        [SCALARS, WHOLE],
        jax.ShapeDtypeStruct((features.shape[0], NX * BLOCK), jnp.bfloat16),
        0, 2,
    )(at, features)


def stack_body(own, first, second, third, plane_ref):
    rows = own.shape[0]
    for i, piece in enumerate((own, first, second, third)):
        plane_ref[i * rows : (i + 1) * rows, :] = piece[...]


def stack_plane(pieces):
    rows, columns = pieces[0].shape
    return call(
        stack_body, [WHOLE] * 4, pltpu.VMEM((4 * rows, columns), jnp.bfloat16), 0, 3
    )(*[in_vmem(p) for p in pieces[:2]], *[in_hbm(p) for p in pieces[2:]])


def in_hbm(array):
    return pltpu.with_memory_space_constraint(array, pltpu.HBM)


def in_vmem(array):
    return pltpu.with_memory_space_constraint(array, pltpu.VMEM)


def early_body(steps, arranged, *refs):
    pieces, (mine_ref, theirs_ref, rows_ref, sems) = refs[: len(steps)], refs[len(steps) :]
    count, stores, total = mine_ref.shape[0], [], 0.0
    for i, (step, piece) in enumerate(zip(steps, pieces)):
        store = pltpu.make_async_copy(
            piece, rows_ref.at[pl.ds(step * BLOCK, BLOCK)], sems.at[i]
        )
        store.start()
        stores.append(store)
    for step, piece in zip(steps, pieces):
        total += jnp.dot(
            arranged[step * 2 * count : (step + 1) * 2 * count, :], piece[...],
            preferred_element_type=jnp.float32,
        )
    mine_ref[...] = total[:count]
    theirs_ref[...] = total[count:]
    for store in stores:
        store.wait()


def early_sums(arranged, pieces, steps):
    count, columns = arranged.shape[0] // NX // 2, pieces[0].shape[1]
    return call(
        functools.partial(early_body, steps),
        [WHOLE] * (1 + len(pieces)),
        [
            pltpu.VMEM((count, columns), jnp.float32),
            pltpu.VMEM((count, columns), jnp.float32),
            jax.ShapeDtypeStruct((NX * BLOCK, columns), jnp.bfloat16),
        ],
        len(steps) * 4 * count * BLOCK * columns, len(steps) * 2,
        out_specs=[WHOLE, WHOLE, LEFT],
        scratch_shapes=[pltpu.SemaphoreType.DMA((len(pieces),))],
    )(in_vmem(arranged), *[in_vmem(p) for p in pieces])


def late_body(steps, arranged, mine, theirs, *refs):
    pieces, (rows_in, mine_ref, theirs_ref, rows_ref, sems) = refs[: len(steps)], refs[len(steps) :]
    count, stores, more = mine.shape[0], [], 0.0
    for i, (step, piece) in enumerate(zip(steps, pieces)):
        to_rows = rows_ref.at[pl.ds(step * BLOCK, BLOCK)]
        stores.append(pltpu.make_async_copy(piece, to_rows, sems.at[i]))
        stores[-1].start()
    for step, piece in zip(steps, pieces):
        more += jnp.dot(
            arranged[step * 2 * count : (step + 1) * 2 * count, :], piece[...],
            preferred_element_type=jnp.float32,
        )
    mine_ref[...] = mine[...] + more[:count]
    theirs_ref[...] = theirs[...] + more[count:]
    for store in stores:
        store.wait()


def late_sums(arranged, sums, pieces, rows, steps):
    count, columns = sums[0].shape
    operands = [in_vmem(x) for x in (arranged, *sums, *pieces)]
    return call(
        functools.partial(late_body, steps),
        [WHOLE] * len(operands) + [LEFT],
        [
            pltpu.VMEM((count, columns), jnp.float32),
            pltpu.VMEM((count, columns), jnp.float32),
            jax.ShapeDtypeStruct(rows.shape, rows.dtype),
        ],
        len(steps) * 4 * count * BLOCK * columns, 4,
        out_specs=[WHOLE, WHOLE, LEFT],
        scratch_shapes=[pltpu.SemaphoreType.DMA((len(pieces),))],
        input_output_aliases={len(operands): 2},
    )(*operands, rows)


TURN = (((1,), (1,)), ((), ()))


def by_source(pieces, parity, cut, join):
    for s in range(NX):
        turned = join([cut(piece, s) for piece in pieces])
        yield s, jnp.where(parity == 0, turned, pieces[s])


def query_part_body(flip, at, grads, all_rows, out_ref, weights, held, sems):
    parity = at[2] if flip == 0 else 1 - at[2]
    rows = grads.shape[0]
    loads = []
    for e in range(NX):
        source = all_rows.at[pl.ds(e * BLOCK, BLOCK), pl.ds(0, HQ * HD)]
        loads.append(pltpu.make_async_copy(source, weights.at[e], sems.at[e]))
        loads[-1].start()
    order = order_matrix(at[1])
    for e in range(NX):
        loads[e].wait()
        held[e] = lax.dot_general(
            grads[...], weights[e], TURN, preferred_element_type=jnp.float32
        )
    for s, part in by_source(
        [held[e] for e in range(NX)], parity,
        lambda piece, d: piece[:, d * SPAN : (d + 1) * SPAN],
        lambda parts: jnp.concatenate(parts, axis=1),
    ):
        high = part.astype(jnp.bfloat16)
        low = (part - high.astype(jnp.float32)).astype(jnp.bfloat16)
        back = lax.dot_general(
            jnp.concatenate([high, low], axis=0), order, TURN,
            preferred_element_type=jnp.float32,
        )
        out_ref[:, pl.ds(x_block(at[0], s), BLOCK)] = back[:rows] + back[rows:]


def query_part_of(at, grads, all_rows, flip):
    rows = grads.shape[0]
    return call(
        functools.partial(query_part_body, flip),
        [SCALARS, WHOLE, LEFT],
        pltpu.VMEM((rows, NX * BLOCK), jnp.float32),
        NX * 2 * rows * BLOCK * (HQ * HD + 2 * BLOCK), 6,
        scratch_shapes=[
            pltpu.VMEM((NX, BLOCK, HQ * HD), jnp.bfloat16),
            pltpu.VMEM((NX, rows, BLOCK), jnp.float32),
            pltpu.SemaphoreType.DMA((NX,)),
        ],
    )(at, grads, all_rows)


def pair_weights_body(at, all_rows, out_ref, weights, sem):
    load = pltpu.make_async_copy(all_rows.at[:, pl.ds(HQ * HD, 2 * HD)], weights, sem)
    load.start()
    order = order_matrix(at[1])
    load.wait()
    for s, part in by_source(
        [weights[e * BLOCK : (e + 1) * BLOCK, :] for e in range(NX)], at[2],
        lambda piece, d: piece[d * SPAN : (d + 1) * SPAN],
        lambda parts: jnp.concatenate(parts, axis=0),
    ):
        out_ref[pl.ds(x_block(at[0], s), BLOCK), :] = jnp.dot(
            order, part, preferred_element_type=jnp.float32
        ).astype(jnp.bfloat16)


def pair_weights_of(at, all_rows):
    return call(
        pair_weights_body,
        [SCALARS, LEFT],
        pltpu.HBM((NX * BLOCK, 2 * HD), jnp.bfloat16),
        NX * 2 * BLOCK * BLOCK * 2 * HD, 3,
        scratch_shapes=[
            pltpu.VMEM((NX * BLOCK, 2 * HD), jnp.bfloat16),
            pltpu.SemaphoreType.DMA,
        ],
    )(at, all_rows)


def finish_body(at, pair_out, own_part, other_part, own_w, other_w, out_ref):
    for x in range(NX):
        cut = slice(x * BLOCK, (x + 1) * BLOCK)
        for flip, part, w in ((0, own_part, own_w), (1, other_part, other_w)):
            parity = at[2] if flip == 0 else 1 - at[2]
            total = part[:, cut] + lax.dot_general(
                pair_out[...], w[cut, :], TURN, preferred_element_type=jnp.float32
            )
            to_block = pl.ds(pl.multiple_of((x * NC + parity) * BLOCK, BLOCK), BLOCK)
            out_ref[:, to_block] = total.astype(jnp.bfloat16)


def finish(at, pair_out, parts, weights):
    whole = pl.BlockSpec(memory_space=pltpu.VMEM)
    return pl.pallas_call(
        finish_body,
        in_specs=[pl.BlockSpec(memory_space=pltpu.SMEM)] + [whole] * 5,
        out_shape=jax.ShapeDtypeStruct((pair_out.shape[0], NX * NC * BLOCK), jnp.bfloat16),
        compiler_params=pltpu.CompilerParams(vmem_limit_bytes=VMEM_LIMIT),
    )(at, pair_out, *[in_vmem(p) for p in parts], in_vmem(weights[0]), in_hbm(weights[1]))


def shifted(block, axis, distance):
    devices = range(lax.axis_size(axis))
    return lax.ppermute(block, axis, [(i - distance, i) for i in devices if i - distance in devices])


def angles_for(positions, head_size):
    half_size = head_size // 2
    inverse = jnp.power(
        jnp.float32(ROPE_BASE), -jnp.arange(half_size, dtype=jnp.float32) / half_size
    )
    phase_angle = positions.astype(jnp.float32)[:, None] * inverse[None, :]
    return (jnp.cos(phase_angle), jnp.sin(phase_angle))


def rotate(vectors, cos_part, sin_part):
    half_size = vectors.shape[-1] // 2
    a = vectors[..., :half_size]
    b = vectors[..., half_size:]
    return jnp.concatenate([a * cos_part - b * sin_part, b * cos_part + a * sin_part], axis=-1)


def local(tokens, doc_start, out_grad, w_qkv):
    row_count = tokens.shape[1]
    score_scale = 1.0 / math.sqrt(HD)
    features = tokens[0]
    begin_rows = doc_start[0]
    grad_rows = out_grad[0].reshape(row_count, HQ, HD)
    fsdp, ctx = lax.axis_index("fsdp"), lax.axis_index("ctx")
    x_me, core = fsdp // NC, fsdp % NC
    y_me = ctx % NY

    column = lax.all_gather(
        w_qkv, "ctx", axis=0, tiled=True,
        axis_index_groups=[[z * NY + y for z in range(NZ)] for y in range(NY)],
    )
    third, first, second = (hop(column, d, 0) for d in (3, 1, 2))

    at = jnp.stack([x_me, y_me, core]).astype(jnp.int32)
    order = order_matrix(y_me)
    plane, theirs = lax.optimization_barrier(
        (stack_plane([column, first, second, third]), pick(at, features))
    )
    three, one, two = (hop(plane, d, 1) for d in (3, 1, 2))
    arranged = arrange(at, order, features, swap_cores(theirs))
    *sums, own_w = early_sums(arranged, [plane, two], (0, 2))
    mine, theirs, own_w = late_sums(arranged, sums, [one, three], own_w, (1, 3))
    projected = mine + swap_cores(theirs)
    pair_pre, query_pre = projected[:, HQ * HD :], projected[:, : HQ * HD]

    first_row = ctx * row_count
    query_index = first_row + jnp.arange(row_count, dtype=jnp.int32)
    cos_part, sin_part = angles_for(query_index - begin_rows, HD)
    pair_rows = jnp.concatenate(
        [rotate(pair_pre[:, :HD], cos_part, sin_part), pair_pre[:, HD:]], axis=1
    ).astype(jnp.bfloat16)
    later_at, pair_rows = lax.optimization_barrier((at, pair_rows))
    back2, pair_w_own = lax.optimization_barrier(
        (shifted(pair_rows, "ctx", 2), pair_weights_of(later_at, own_w))
    )
    back31 = shifted(jnp.concatenate([back2, pair_rows], axis=0), "ctx", 1)
    other_w = swap_cores(own_w)
    window = jnp.concatenate([back31[:row_count], back2, back31[row_count:], pair_rows], axis=0)

    queries = rotate(
        query_pre.reshape(row_count, HQ, HD), cos_part[:, None, :], sin_part[:, None, :]
    ).astype(jnp.bfloat16)
    keys, values = window[:, :HD], window[:, HD:]
    key_index = first_row - (REACH - 1) * row_count + jnp.arange(REACH * row_count, dtype=jnp.int32)
    allowed = (key_index[None, :] <= query_index[:, None]) & (
        key_index[None, :] >= begin_rows[:, None]
    )
    scores = (
        jnp.einsum("qhd,kd->hqk", queries, keys, preferred_element_type=jnp.float32) * score_scale
    )
    scores = jnp.where(allowed[None], scores, MASKED)
    top = jnp.max(scores, axis=-1, keepdims=True)
    unnormed = jnp.where(allowed[None], jnp.exp(scores - top), 0.0)
    probs = unnormed / jnp.sum(unnormed, axis=-1, keepdims=True)
    probs_low = probs.astype(jnp.bfloat16)
    grad_probs = jnp.einsum("qhd,kd->hqk", grad_rows, values, preferred_element_type=jnp.float32)
    attn_out = jnp.einsum(
        "hqk,kd->hqd", probs_low, values, preferred_element_type=jnp.float32
    ).astype(jnp.bfloat16)
    row_delta = jnp.sum(
        jnp.transpose(grad_rows, (1, 0, 2)).astype(jnp.float32) * attn_out.astype(jnp.float32),
        axis=-1, keepdims=True,
    )
    grad_value = jnp.einsum("hqk,qhd->kd", probs_low, grad_rows, preferred_element_type=jnp.float32)
    grad_scores = (probs * (grad_probs - row_delta)).astype(jnp.bfloat16)
    grad_query = (
        jnp.einsum("hqk,kd->qhd", grad_scores, keys, preferred_element_type=jnp.float32)
        * score_scale
    )
    grad_key = (
        jnp.einsum("hqk,qhd->kd", grad_scores, queries, preferred_element_type=jnp.float32)
        * score_scale
    )
    pair_grad = jnp.concatenate([grad_key, grad_value], axis=1)
    query_out = rotate(grad_query, cos_part[:, None, :], -sin_part[:, None, :]).reshape(
        row_count, HQ * HD
    ).astype(jnp.bfloat16)
    back3, back2, back1, own_grad = (
        pair_grad[i * row_count : (i + 1) * row_count] for i in range(REACH)
    )
    came, part_own = lax.optimization_barrier(
        (
            shifted(jnp.concatenate([back3, back1], axis=0).astype(jnp.bfloat16), "ctx", -1),
            query_part_of(at, query_out, own_w, 0),
        )
    )
    came = came.astype(jnp.float32)
    last, part_other, pair_w_other = lax.optimization_barrier(
        (
            shifted((back2 + came[:row_count]).astype(jnp.bfloat16), "ctx", -2),
            query_part_of(at, query_out, other_w, 1),
            swap_cores(pair_w_own),
        )
    )
    pair_total = own_grad + came[row_count:] + last.astype(jnp.float32)
    pair_out = jnp.concatenate(
        [rotate(pair_total[:, :HD], cos_part, -sin_part), pair_total[:, HD:]], axis=1
    ).astype(jnp.bfloat16)
    return finish(at, pair_out, [part_own, part_other], [pair_w_own, pair_w_other])[None]


def solution(mesh):
    placed = (
        P("fsdp", "ctx", None),
        P("fsdp", "ctx"),
        P("fsdp", "ctx", None),
        P(("fsdp", "ctx"), None),
    )
    return jax.shard_map(
        local, mesh=mesh, in_specs=placed, out_specs=P("fsdp", "ctx", None), check_vma=False
    )
```
